32 devices in a mesh: tile: 4 (over y, core), freq: 8 (over z, x).
Axes of the slice: x: 2, y: 2, z: 4, core: 2. Of those that a mesh axis runs over, the one named last changes fastest.
Arguments:
- sensitivity: float32 [4, 32, 2, 1024, 512], P('tile', 'freq'), may hold values from -0.25 to 0.25
- models: float32 [1024, 256], P(('tile', 'freq')), may hold values from -6 to 6
- observed: float32 [4, 40, 1024], P('tile', None, 'freq'), may hold values from -6 to 6
- waveform: float32 [128], replicated, may hold values from -0.5 to 0.5
- cell_index: int32 [4, 512], P('tile'), may hold values from 0 to 1023, as said below
- gate_index: int32 [40], replicated, may hold values from 10 to 127, as said below
Outputs:
- updated: float32 [1024, 256], P(('tile', 'freq'))
- misfit: float32 [256], replicated
The draws below stay inside these ranges and needn't reach their ends.
Inputs may be any that keep to these rules, and one draw needn't show every extreme that they name: `cell_index`: each tile's indices are distinct. Tile t holds, in some order, the 256 global cells from t * 256 on and the 256 cells of one other tile's block (from u * 256 on, u != t). Every global cell belongs to one or more tiles. `gate_index`: strictly increasing; the last gate is sample 128 - 1.
All inputs are finite; a program needn't handle non-finite values.
Results may differ from the reference program's by a relative error of at most 0.00017.
Values sent between devices are 32-bit elements; how exact they have to be, the bound alone decides.
No kernel may reach another device: no remote copies, remote signals or barrier semaphores. Data moves between devices by JAX's collectives and lax.ppermute only.
A program may use at most 64 MiB of HBM per device.

```python
import math
import jax
import jax.numpy as jnp
from jax import lax

FREQS = 32
GATES = 40
SAMPLES = 128
SOUND = 1024
CELLS = 512
MEMBERS = 256
TILES = 4
NCELL = 1024


def draw_cell_index(key, part):
    half = CELLS // 2
    first_key = jax.random.fold_in(key, 11)
    second_key = jax.random.fold_in(key, 23)
    shifts = jax.random.randint(first_key, (TILES,), 0, TILES - 1)
    others = (jnp.arange(TILES) + 1 + shifts) % TILES
    within = jnp.arange(half)[None, :]
    owned = jnp.arange(TILES)[:, None] * half + within
    borrowed = others[:, None] * half + within
    joined = jnp.concatenate([owned, borrowed], axis=1)
    orders = jax.vmap(lambda k: jax.random.permutation(k, CELLS))(jax.random.split(second_key, TILES))
    return jnp.take_along_axis(joined, orders, axis=1).astype(jnp.int32)


def draw_gate_index(key, part):
    spacing = jax.random.randint(jax.random.fold_in(key, 5), (GATES,), 1, 4)
    after = jnp.cumsum(spacing[::-1])[::-1] - spacing
    return (SAMPLES - 1 - after).astype(jnp.int32)


def levels(key, dims, cuts, low, largest):
    def one(dim, shards_of):
        draws = jax.random.uniform(jax.random.fold_in(jax.random.fold_in(key, 6), dim), (shards_of,), jnp.float32, low / len(cuts), largest / len(cuts))
        return jnp.repeat(jnp.exp(draws), dims[dim] // shards_of).reshape((-1,) + (1,) * (len(dims) - dim - 1))

    gain = one(*cuts[0])
    for cut in cuts[1:]:
        gain = gain * one(*cut)
    return gain


def scatter_about(stream_key, extent, deviation, bound, shards=(), kind=jnp.bfloat16):
    loudness = levels(stream_key, extent, shards, -0.22, 0.18) if shards else 1.0
    values = jax.random.normal(stream_key, extent, jnp.float32) * deviation * loudness
    return jnp.minimum(jnp.maximum(values, -bound), bound).astype(kind)


def setup_inputs(seed: int = 0) -> dict:
    seeds = jax.random.split(jax.random.key(seed), 7)
    return {
        "sensitivity": scatter_about(seeds[0], (TILES, FREQS, 2, SOUND, CELLS), CELLS ** -0.5, 0.25, ((0, 4), (1, 8)), jnp.float32),
        "models": scatter_about(seeds[1], (NCELL, MEMBERS), 1.0, 6.0, ((0, 32),), jnp.float32),
        "observed": scatter_about(seeds[2], (TILES, GATES, SOUND), 1.0, 6.0, ((0, 4), (2, 8)), jnp.float32),
        "waveform": scatter_about(seeds[3], (SAMPLES,), SAMPLES ** -0.5, 0.5, (), jnp.float32),
        "cell_index": draw_cell_index(jax.random.fold_in(seeds[6], 71), 0),
        "gate_index": draw_gate_index(jax.random.fold_in(seeds[6], 71), 0),
    }


HIGH = lax.Precision.HIGHEST
PHASE_RATE = 0.37
STEP_LENGTH = 0.5
EPSILON = 1e-06

def gate_tables(freqs, waveform, gate_index):
    samples = waveform.shape[0]
    freq_col = jnp.arange(freqs, dtype=jnp.float32)[:, None] + 0.5
    time_row = jnp.arange(samples, dtype=jnp.float32)[None, :] + 0.5
    phases = PHASE_RATE * freq_col * time_row
    kernel = jnp.stack([jnp.cos(phases), jnp.sin(phases)], axis=1) / math.sqrt(freqs)
    time_lag = jnp.arange(samples)[:, None] - jnp.arange(samples)[None, :]
    toeplitz = jnp.where(time_lag >= 0, jnp.take(waveform, jnp.clip(time_lag, 0, samples - 1)), 0.0)
    picker = (gate_index[:, None] == jnp.arange(samples)[None, :]).astype(jnp.float32)
    return (kernel, toeplitz, picker)

def reference(sensitivity, models, observed, waveform, cell_index, gate_index):
    freqs = sensitivity.shape[1]
    members = models.shape[1]
    total = sensitivity.shape[0] * sensitivity.shape[3] * gate_index.shape[0]
    kernel, toeplitz, picker = gate_tables(freqs, waveform, gate_index)

    def per_tile(pieces):
        block, cells, seen = pieces
        tile_models = jnp.take(models, cells, axis=0)
        predicted = jnp.einsum('fpsc,cm->fpsm', block, tile_models, precision=HIGH)
        series = jnp.einsum('fpk,fpsm->ksm', kernel, predicted, precision=HIGH)
        series = jnp.einsum('kj,jsm->ksm', toeplitz, series, precision=HIGH)
        response = jnp.einsum('gk,ksm->gsm', picker, series, precision=HIGH)
        misfit_rows = response - seen[:, :, None]
        upward = jnp.einsum('gk,gsm->ksm', picker, misfit_rows, precision=HIGH)
        upward = jnp.einsum('kj,ksm->jsm', toeplitz, upward, precision=HIGH)
        back = jnp.einsum('fpk,ksm->fpsm', kernel, upward, precision=HIGH)
        cell_terms = jnp.einsum('fpsc,fpsm->cm', block, back, precision=HIGH)
        return (cell_terms, lax.optimization_barrier(jnp.sum(misfit_rows * misfit_rows, axis=(0, 1))))
    cell_terms, squares = lax.map(per_tile, (sensitivity, cell_index, observed))
    gradient = jnp.zeros_like(models).at[cell_index.reshape(-1)].add(cell_terms.reshape(-1, members))
    misfit = lax.optimization_barrier(jnp.sum(squares, axis=0)) / (2.0 * total)
    scale = jnp.sqrt(lax.optimization_barrier(jnp.mean(gradient * gradient, axis=0)) + EPSILON)
    updated = models - STEP_LENGTH * (misfit / scale)[None, :] * gradient
    return (updated, misfit)
```

```python
import functools
import math

import jax
import jax.numpy as jnp
from jax import lax
from jax.experimental import pallas as pl
from jax.experimental.pallas import tpu as pltpu
from jax.sharding import PartitionSpec as P

HIGH = lax.Precision.HIGHEST
PHASE_RATE = 0.37
STEP_LENGTH = 0.5
EPSILON = 1e-06
GROUP = 8
LANES = 128
CHUNKS = 4

NN = (((1,), (0,)), ((), ()))
NT = (((1,), (1,)), ((), ()))


def gate_table(freqs, waveform, gate_index):
    samples = waveform.shape[0]
    freq_col = jnp.arange(freqs, dtype=jnp.float32)[:, None] + 0.5
    time_row = jnp.arange(samples, dtype=jnp.float32)[None, :] + 0.5
    phases = PHASE_RATE * freq_col * time_row
    kernel = jnp.stack([jnp.cos(phases), jnp.sin(phases)], axis=1) / math.sqrt(freqs)
    steps = jnp.arange(samples)
    lag = gate_index[:, None] - steps[None, :]
    picked = jnp.sum(
        jnp.where(lag[:, :, None] == steps[None, None, :], waveform[None, None, :], 0.0), axis=-1
    )
    return jnp.einsum("gk,fpk->gfp", picked, kernel, precision=HIGH).reshape(gate_index.shape[0], freqs * 2)


def split(x):
    high = x.astype(jnp.bfloat16)
    return high, (x - high.astype(jnp.float32)).astype(jnp.bfloat16)


def split_outside(x):
    high = lax.reduce_precision(x, 8, 7)
    return high.astype(jnp.bfloat16), (x - high).astype(jnp.bfloat16)


def three_pass(a, b, dims):
    dot = functools.partial(lax.dot_general, dimension_numbers=dims, preferred_element_type=jnp.float32)
    return dot(a[0], b[0]) + (dot(a[0], b[1]) + dot(a[1], b[0]))


def chunk_kernel(sens_ref, model_h, model_l, gate_h, gate_l, obs_ref, terms_in, square_in, terms_ref, square_ref):
    @pl.when(pl.program_id(0) == 0)
    def _():
        terms_ref[...] = terms_in[...]
        square_ref[...] = square_in[...]

    rows = sens_ref.shape[0] * sens_ref.shape[1]
    sens = split(sens_ref[...].reshape(rows, sens_ref.shape[2]))
    gates = (gate_h[...], gate_l[...])
    predicted = three_pass((model_h[...], model_l[...]), sens, NT)
    misfit_rows = three_pass(split(predicted), gates, NN) - obs_ref[0]
    square_ref[...] += jnp.sum(misfit_rows * misfit_rows, axis=1, keepdims=True)
    back = three_pass(split(misfit_rows), gates, NT)
    terms_ref[...] += three_pass(split(back), sens, NN)


def chunk_step(sens, models_t, gates, obs, terms, square):
    spectra, soundings, cells = sens.shape
    groups = soundings // GROUP
    members = terms.shape[0]
    whole = lambda a: pl.BlockSpec(a.shape, lambda i: (0,) * a.ndim)
    return pl.pallas_call(
        chunk_kernel,
        grid=(groups,),
        in_specs=[pl.BlockSpec((spectra, GROUP, cells), lambda i: (0, i, 0))]
        + [whole(a) for a in (*models_t, *gates)]
        + [pl.BlockSpec((1, 1, obs.shape[2]), lambda i: (i, 0, 0)), whole(terms), whole(square)],
        out_specs=[whole(terms), whole(square)],
        out_shape=[
            jax.ShapeDtypeStruct(terms.shape, jnp.float32),
            jax.ShapeDtypeStruct(square.shape, jnp.float32),
        ],
        input_output_aliases={6: 0, 7: 1},
        compiler_params=pltpu.CompilerParams(
            dimension_semantics=("arbitrary",), vmem_limit_bytes=40 * 1024 * 1024
        ),
        cost_estimate=pl.CostEstimate(
            flops=12 * spectra * soundings * cells * members * 2,
            bytes_accessed=4 * spectra * soundings * cells,
            transcendentals=0,
        ),
        name="chunk_step",
    )(sens, *models_t, *gates, obs, terms, square)


def body(sensitivity, models, observed, waveform, cell_index, gate_index):
    both = ("tile", "freq")
    tiles, owners, devices = lax.axis_size("tile"), lax.axis_size("freq"), lax.axis_size(both)
    _, own_freqs, parts, soundings, cells = sensitivity.shape
    freqs = own_freqs * owners
    owned, members = models.shape
    ncells = owned * devices
    gates = gate_index.shape[0]
    total = tiles * soundings * gates
    own_soundings = soundings // owners
    per_chunk = own_soundings // CHUNKS
    block_cells = owned * owners
    me = lax.axis_index("tile")

    block = sensitivity[0].reshape(own_freqs * parts, owners, CHUNKS, per_chunk, cells)
    received = []
    for k in range(CHUNKS):
        piece = jnp.swapaxes(block[:, :, k], 0, 1)
        received.append(lax.all_to_all(piece, "freq", split_axis=0, concat_axis=0, tiled=True))

    tile_cells = cell_index[0]
    home = tile_cells // block_cells
    borrowed_from = jnp.max(jnp.where(home == me, -1, home))
    all_models = lax.all_gather(models, both, axis=0, tiled=True)
    models_t = split_outside(jnp.take(all_models, tile_cells, axis=0).T)
    all_borrowed = lax.all_gather(borrowed_from.reshape(1), "tile", axis=0, tiled=True)

    table = gate_table(freqs, waveform, gate_index).T
    wide = table[:, None, :, None] * jnp.eye(GROUP, dtype=jnp.float32)[None, :, None, :]
    wide = split_outside(wide.reshape(freqs * parts * GROUP, gates * GROUP))
    obs = observed[0].reshape(gates, own_soundings // GROUP, GROUP)
    obs = jnp.swapaxes(obs, 0, 1).reshape(own_soundings // GROUP, 1, gates * GROUP)

    terms = jnp.zeros((members, cells), jnp.float32)
    square = jnp.zeros((members, LANES), jnp.float32)
    groups = per_chunk // GROUP
    for k in range(CHUNKS):
        sens = received[k].reshape(freqs * parts, per_chunk, cells)
        terms, square = chunk_step(sens, models_t, wide, obs[k * groups : (k + 1) * groups], terms, square)

    place = tile_cells % block_cells + jnp.where(home == me, 0, block_cells)
    order = (place[:, None] == jnp.arange(cells)[None, :]).astype(jnp.float32)
    terms = jnp.dot(terms, order, precision=HIGH)
    sent = jnp.concatenate([terms, square], axis=1).reshape(devices, members // devices, cells + LANES)
    got = lax.all_to_all(sent, both, split_axis=0, concat_axis=0, tiled=True)
    got = jnp.sum(got.reshape(tiles, owners, members // devices, cells + LANES), axis=1)
    lent = (all_borrowed[None, :] == jnp.arange(tiles)[:, None]).astype(jnp.float32)
    gradient = got[:, :, :block_cells] + jnp.sum(
        lent[:, :, None, None] * got[None, :, :, block_cells:cells], axis=1
    )
    misfit = jnp.sum(got[:, :, cells], axis=0) / (2.0 * total)
    scale = jnp.sqrt(jnp.sum(gradient * gradient, axis=(0, 2)) / ncells + EPSILON)
    step = STEP_LENGTH * (misfit / scale)[None, :, None] * gradient
    step = step.reshape(tiles, members // devices, owners, owned).transpose(0, 2, 1, 3)
    step = step.reshape(devices, members // devices, owned)
    spread = jnp.broadcast_to(misfit[None, :, None], (devices, members // devices, LANES - owned))
    back = lax.all_to_all(jnp.concatenate([step, spread], axis=2), both, split_axis=0, concat_axis=0, tiled=True)
    back = back.reshape(members, LANES)
    return (models - back[:, :owned].T, back[:, owned])


def solution(mesh):
    in_specs = (
        P("tile", "freq", None, None, None),
        P(("tile", "freq"), None),
        P("tile", None, "freq"),
        P(),
        P("tile", None),
        P(),
    )
    out_specs = (P(("tile", "freq"), None), P())
    return jax.shard_map(body, mesh=mesh, in_specs=in_specs, out_specs=out_specs, check_vma=False)
```

```python
import functools
import math

import jax
import jax.numpy as jnp
from jax import lax
from jax.experimental import pallas as pl
from jax.experimental.pallas import tpu as pltpu
from jax.sharding import PartitionSpec as P

HIGH = lax.Precision.HIGHEST
PHASE_RATE = 0.37
STEP_LENGTH = 0.5
EPSILON = 1e-06
GROUP = 8
LANES = 128
CHUNKS = 5
WINDOW = 2

NN = (((1,), (0,)), ((), ()))
NT = (((1,), (1,)), ((), ()))


def bits_of(size):
    assert size & (size - 1) == 0
    return [1 << b for b in reversed(range(size.bit_length() - 1))]


def swap(x, axis, k):
    size = lax.axis_size(axis)
    return lax.ppermute(x, axis, [(i, i ^ k) for i in range(size)])


def gather_doubling(x, axis):
    for k in bits_of(lax.axis_size(axis)):
        x = jnp.concatenate([x, swap(x, axis, k)], axis=0)
    return x


def place_of(offset, size):
    place = 0
    for b, k in enumerate(bits_of(size)):
        place = place + jnp.where(offset & k != 0, 1 << b, 0)
    return place


def gate_table(owner_order, own_freqs, freqs, waveform, gate_index):
    samples = waveform.shape[0]
    freq_ids = (owner_order[:, None] * own_freqs + jnp.arange(own_freqs)[None, :]).reshape(freqs)
    freq_col = freq_ids.astype(jnp.float32)[:, None] + 0.5
    time_row = jnp.arange(samples, dtype=jnp.float32)[None, :] + 0.5
    phases = PHASE_RATE * freq_col * time_row
    kernel = jnp.stack([jnp.cos(phases), jnp.sin(phases)], axis=1) / math.sqrt(freqs)
    steps = jnp.arange(samples)
    lag = gate_index[:, None] - steps[None, :]
    picked = jnp.sum(
        jnp.where(lag[:, :, None] == steps[None, None, :], waveform[None, None, :], 0.0), axis=-1
    )
    return jnp.einsum("gk,fpk->gfp", picked, kernel, precision=HIGH).reshape(gate_index.shape[0], freqs * 2)


def split(x):
    high = x.astype(jnp.bfloat16)
    return high, (x - high.astype(jnp.float32)).astype(jnp.bfloat16)


def split_outside(x):
    high = lax.reduce_precision(x, 8, 7)
    return high.astype(jnp.bfloat16), (x - high).astype(jnp.bfloat16)


def three_pass(a, b, dims):
    dot = functools.partial(lax.dot_general, dimension_numbers=dims, preferred_element_type=jnp.float32)
    return dot(a[0], b[0]) + (dot(a[0], b[1]) + dot(a[1], b[0]))


def chunk_kernel(pieces, *refs):
    sens_refs = refs[:pieces]
    model_h, model_l, gate_h, gate_l, obs_ref, terms_in, square_in, terms_ref, square_ref = refs[pieces:]

    @pl.when(pl.program_id(0) == 0)
    def _():
        terms_ref[...] = terms_in[...]
        square_ref[...] = square_in[...]

    sens = [split(r[...].reshape(r.shape[0] * r.shape[1], r.shape[2])) for r in sens_refs]
    sens = tuple(jnp.concatenate([s[i] for s in sens], axis=0) for i in range(2))
    gates = (gate_h[...], gate_l[...])
    predicted = three_pass((model_h[...], model_l[...]), sens, NT)
    misfit_rows = three_pass(split(predicted), gates, NN) - obs_ref[0]
    square_ref[...] += jnp.sum(misfit_rows * misfit_rows, axis=1, keepdims=True)
    back = three_pass(split(misfit_rows), gates, NT)
    terms_ref[...] += three_pass(split(back), sens, NN)


def chunk_step(sens, models_t, gates, obs, terms, square):
    spectra, soundings, cells = sens[0].shape
    pieces = len(sens)
    groups = soundings // GROUP
    members = terms.shape[0]
    whole = lambda a: pl.BlockSpec(a.shape, lambda i: (0,) * a.ndim)
    return pl.pallas_call(
        functools.partial(chunk_kernel, pieces),
        grid=(groups,),
        in_specs=[pl.BlockSpec((spectra, GROUP, cells), lambda i: (0, i, 0))] * pieces
        + [whole(a) for a in (*models_t, *gates)]
        + [pl.BlockSpec((1, 1, obs.shape[2]), lambda i: (i, 0, 0)), whole(terms), whole(square)],
        out_specs=[whole(terms), whole(square)],
        out_shape=[
            jax.ShapeDtypeStruct(terms.shape, jnp.float32),
            jax.ShapeDtypeStruct(square.shape, jnp.float32),
        ],
        input_output_aliases={pieces + 5: 0, pieces + 6: 1},
        compiler_params=pltpu.CompilerParams(
            dimension_semantics=("arbitrary",), vmem_limit_bytes=40 * 1024 * 1024
        ),
        cost_estimate=pl.CostEstimate(
            flops=12 * pieces * spectra * soundings * cells * members * 2,
            bytes_accessed=4 * pieces * spectra * soundings * cells,
            transcendentals=0,
        ),
        name="chunk_step",
    )(*sens, *models_t, *gates, obs, terms, square)


def chunk_groups(groups):
    count = min(CHUNKS, groups)
    if count == 1:
        return [groups]
    rest = groups - 1
    base, extra = divmod(rest, count - 1)
    return [base + (i < extra) for i in range(count - 1)] + [1]


def body(sensitivity, models, observed, waveform, cell_index, gate_index):
    both = ("tile", "freq")
    tiles, owners, devices = lax.axis_size("tile"), lax.axis_size("freq"), lax.axis_size(both)
    _, own_freqs, parts, soundings, cells = sensitivity.shape
    freqs = own_freqs * owners
    owned, members = models.shape
    ncells = owned * devices
    gates = gate_index.shape[0]
    total = tiles * soundings * gates
    own_soundings = soundings // owners
    block_cells = owned * owners
    me, my_freq = lax.axis_index("tile"), lax.axis_index("freq")

    block = sensitivity[0].reshape(own_freqs * parts, soundings, cells)
    sizes = chunk_groups(own_soundings // GROUP)
    starts = [sum(sizes[:i]) for i in range(len(sizes))]
    distances = sorted(range(1, owners), reverse=True)
    received = []
    source = block
    for i, (start, size) in enumerate(zip(starts, sizes)):
        if i >= WINDOW:
            source, received[i - WINDOW] = lax.optimization_barrier((block, received[i - WINDOW]))
        piece = lambda k: lax.dynamic_slice_in_dim(
            source, (my_freq ^ k) * own_soundings + start * GROUP, size * GROUP, 1
        )
        received.append([piece(0)] + [swap(piece(k), "freq", k) for k in distances])

    tile_cells = cell_index[0]
    home = tile_cells // block_cells
    borrowed_from = jnp.max(jnp.where(home == me, -1, home))
    all_models = gather_doubling(gather_doubling(models, "freq"), "tile")
    row = tile_cells % owned
    device = (tile_cells // owned) % owners
    spot = place_of(home ^ me, tiles) * block_cells + place_of(device ^ my_freq, owners) * owned + row
    models_t = split_outside(jnp.take(all_models, spot, axis=0).T)
    all_borrowed = gather_doubling(borrowed_from.reshape(1), "tile")
    all_borrowed = jnp.take(all_borrowed, place_of(jnp.arange(tiles) ^ me, tiles))

    order = my_freq ^ jnp.array([0] + distances, jnp.int32)
    table = gate_table(order, own_freqs, freqs, waveform, gate_index).T
    wide = table[:, None, :, None] * jnp.eye(GROUP, dtype=jnp.float32)[None, :, None, :]
    wide = split_outside(wide.reshape(freqs * parts * GROUP, gates * GROUP))
    obs = observed[0].reshape(gates, own_soundings // GROUP, GROUP)
    obs = jnp.swapaxes(obs, 0, 1).reshape(own_soundings // GROUP, 1, gates * GROUP)

    terms = jnp.zeros((members, cells), jnp.float32)
    square = jnp.zeros((members, LANES), jnp.float32)
    for i, (start, size) in enumerate(zip(starts, sizes)):
        terms, square = chunk_step(received[i], models_t, wide, obs[start : start + size], terms, square)

    place = tile_cells % block_cells + jnp.where(home == me, 0, block_cells)
    order = (place[:, None] == jnp.arange(cells)[None, :]).astype(jnp.float32)
    terms = jnp.dot(terms, order, precision=HIGH)
    sent = terms.reshape(devices, members // devices, cells)
    got = lax.all_to_all(sent, both, split_axis=0, concat_axis=0, tiled=True)
    squares = lax.all_gather(square[:, 0], both, axis=0, tiled=False)
    misfit = jnp.sum(squares, axis=0) / (2.0 * total)
    got = jnp.sum(got.reshape(tiles, owners, members // devices, cells), axis=1)
    lent = (all_borrowed[None, :] == jnp.arange(tiles)[:, None]).astype(jnp.float32)
    gradient = got[:, :, :block_cells] + jnp.sum(
        lent[:, :, None, None] * got[None, :, :, block_cells:], axis=1
    )
    scale = jnp.sqrt(jnp.sum(gradient * gradient, axis=(0, 2)) / ncells + EPSILON)
    step = gradient / scale[None, :, None]
    step = step.reshape(tiles, members // devices, owners, owned).transpose(0, 2, 1, 3)
    step = step.reshape(devices, members // devices, owned)
    back = lax.all_to_all(step, both, split_axis=0, concat_axis=0, tiled=True)
    back = back.reshape(members, owned)
    return (models - (STEP_LENGTH * misfit)[None, :] * back.T, misfit)


def solution(mesh):
    in_specs = (
        P("tile", "freq", None, None, None),
        P(("tile", "freq"), None),
        P("tile", None, "freq"),
        P(),
        P("tile", None),
        P(),
    )
    out_specs = (P(("tile", "freq"), None), P())
    return jax.shard_map(body, mesh=mesh, in_specs=in_specs, out_specs=out_specs, check_vma=False)
```

```python
import functools
import math

import jax
import jax.numpy as jnp
from jax import lax
from jax.experimental import pallas as pl
from jax.experimental.pallas import tpu as pltpu
from jax.sharding import PartitionSpec as P

HIGH = lax.Precision.HIGHEST
PHASE_RATE = 0.37
STEP_LENGTH = 0.5
EPSILON = 1e-06
GROUP = 8
LANES = 128

NN = (((1,), (0,)), ((), ()))
NT = (((1,), (1,)), ((), ()))


def swap(x, axis, k):
    return lax.ppermute(x, axis, [(i, i ^ k) for i in range(lax.axis_size(axis))])


def partner_order(size):
    assert size & (size - 1) == 0
    across, near = list(range(size // 2, size))[::-1], list(range(1, size // 2))[::-1]
    order = [k for pair in zip(across, near + [None]) for k in pair if k is not None]
    return order


def gate_table(owner_order, own_freqs, freqs, waveform, gate_index):
    samples = waveform.shape[0]
    freq_ids = (owner_order[:, None] * own_freqs + jnp.arange(own_freqs)[None, :]).reshape(freqs)
    freq_col = freq_ids.astype(jnp.float32)[:, None] + 0.5
    time_row = jnp.arange(samples, dtype=jnp.float32)[None, :] + 0.5
    phases = PHASE_RATE * freq_col * time_row
    kernel = jnp.stack([jnp.cos(phases), jnp.sin(phases)], axis=1) / math.sqrt(freqs)
    steps = jnp.arange(samples)
    lag = gate_index[:, None] - steps[None, :]
    picked = jnp.sum(
        jnp.where(lag[:, :, None] == steps[None, None, :], waveform[None, None, :], 0.0), axis=-1
    )
    return jnp.einsum("gk,fpk->gfp", picked, kernel, precision=HIGH).reshape(gate_index.shape[0], freqs * 2)


def split(x):
    high = x.astype(jnp.bfloat16)
    return high, (x - high.astype(jnp.float32)).astype(jnp.bfloat16)


def split_outside(x):
    high = lax.reduce_precision(x, 8, 7)
    return high.astype(jnp.bfloat16), (x - high).astype(jnp.bfloat16)


def three_pass(a, b, dims):
    dot = functools.partial(lax.dot_general, dimension_numbers=dims, preferred_element_type=jnp.float32)
    return dot(a[0], b[0]) + (dot(a[0], b[1]) + dot(a[1], b[0]))


def chunk_kernel(pieces, *refs):
    sens_refs = refs[:pieces]
    model_h, model_l, gate_h, gate_l, obs_ref, terms_in, square_in, terms_ref, square_ref = refs[pieces:]

    @pl.when(pl.program_id(0) == 0)
    def _():
        terms_ref[...] = terms_in[...]
        square_ref[...] = square_in[...]

    sens = [split(r[...].reshape(r.shape[0] * r.shape[1], r.shape[2])) for r in sens_refs]
    sens = tuple(jnp.concatenate([s[i] for s in sens], axis=0) for i in range(2))
    gates = (gate_h[...], gate_l[...])
    predicted = three_pass((model_h[...], model_l[...]), sens, NT)
    misfit_rows = three_pass(split(predicted), gates, NN) - obs_ref[0]
    square_ref[...] += jnp.sum(misfit_rows * misfit_rows, axis=1, keepdims=True)
    back = three_pass(split(misfit_rows), gates, NT)
    terms_ref[...] += three_pass(split(back), sens, NN)


def chunk_step(sens, spectra, models_t, gates, obs, terms, square):
    _, soundings, cells = sens[0].shape
    pieces = len(sens)
    groups = soundings // GROUP
    members = terms.shape[0]
    whole = lambda a: pl.BlockSpec(a.shape, lambda i: (0,) * a.ndim)
    return pl.pallas_call(
        functools.partial(chunk_kernel, pieces),
        grid=(groups,),
        in_specs=[pl.BlockSpec((spectra, GROUP, cells), lambda i: (0, i, 0))] * pieces
        + [whole(a) for a in (*models_t, *gates)]
        + [pl.BlockSpec((1, 1, obs.shape[2]), lambda i: (i, 0, 0)), whole(terms), whole(square)],
        out_specs=[whole(terms), whole(square)],
        out_shape=[
            jax.ShapeDtypeStruct(terms.shape, jnp.float32),
            jax.ShapeDtypeStruct(square.shape, jnp.float32),
        ],
        input_output_aliases={pieces + 5: 0, pieces + 6: 1},
        compiler_params=pltpu.CompilerParams(
            dimension_semantics=("arbitrary",), vmem_limit_bytes=40 * 1024 * 1024
        ),
        cost_estimate=pl.CostEstimate(
            flops=12 * pieces * spectra * soundings * cells * members * 2,
            bytes_accessed=4 * pieces * spectra * soundings * cells,
            transcendentals=0,
        ),
        name="chunk_step",
    )(*sens, *models_t, *gates, obs, terms, square)


def chunk_groups(groups):
    if groups < 8:
        return [1] * groups
    first, last = groups // 8, [groups // 8, groups // 16 or 1]
    rest = groups - first - sum(last)
    middle = -(-rest // (groups // 4))
    return [first] + [rest // middle + (i < rest % middle) for i in range(middle)] + last


def body(sensitivity, models, observed, waveform, cell_index, gate_index):
    both = ("tile", "freq")
    tiles, owners, devices = lax.axis_size("tile"), lax.axis_size("freq"), lax.axis_size(both)
    _, own_freqs, parts, soundings, cells = sensitivity.shape
    freqs = own_freqs * owners
    spectra = own_freqs * parts
    owned, members = models.shape
    ncells = owned * devices
    gates = gate_index.shape[0]
    total = tiles * soundings * gates
    own_soundings = soundings // owners
    block_cells = owned * owners
    me, my_freq = lax.axis_index("tile"), lax.axis_index("freq")

    block = sensitivity[0].reshape(spectra, soundings, cells)
    sizes = chunk_groups(own_soundings // GROUP)
    starts = [sum(sizes[:i]) for i in range(len(sizes))]
    distances = partner_order(owners)
    received = []
    for i, (start, size) in enumerate(zip(starts, sizes)):
        rows = size * GROUP
        piece = lambda k: lax.dynamic_slice_in_dim(block, (my_freq ^ k) * own_soundings + start * GROUP, rows, 1)
        if i == 0:
            slabs = -(-owned * members // (rows * cells))
            rider = jnp.pad(models.reshape(-1), (0, slabs * rows * cells - owned * members))
            rider = rider.reshape(slabs, rows, cells)
            first = [swap(jnp.concatenate([piece(k), rider]), "freq", k) for k in distances]
            received.append([piece(0)] + first)
            near = [models] + [
                r[spectra:].reshape(-1)[: owned * members].reshape(owned, members) for r in first
            ]
        else:
            received.append([piece(0)] + [swap(piece(k), "freq", k) for k in distances])

    tile_cells = cell_index[0]
    home = tile_cells // block_cells
    borrowed_from = jnp.max(jnp.where(home == me, -1, home))
    near = jnp.concatenate(near + [jnp.full((GROUP, members), borrowed_from, jnp.float32)])
    far = lax.all_gather(near, "tile", axis=0, tiled=False)
    all_borrowed = far[:, block_cells, 0].astype(jnp.int32)
    partners = [0] + distances
    slot = jnp.array([partners.index(k) for k in range(owners)], jnp.int32)
    spot = jnp.take(slot, ((tile_cells // owned) % owners) ^ my_freq) * owned + tile_cells % owned
    spot = home * (block_cells + GROUP) + spot
    models_t = split_outside(jnp.take(far.reshape(-1, members), spot, axis=0).T)

    order = my_freq ^ jnp.array(partners, jnp.int32)
    table = gate_table(order, own_freqs, freqs, waveform, gate_index).T
    wide = table[:, None, :, None] * jnp.eye(GROUP, dtype=jnp.float32)[None, :, None, :]
    wide = split_outside(wide.reshape(freqs * parts * GROUP, gates * GROUP))
    obs = observed[0].reshape(gates, own_soundings // GROUP, GROUP)
    obs = jnp.swapaxes(obs, 0, 1).reshape(own_soundings // GROUP, 1, gates * GROUP)

    terms = jnp.zeros((members, cells), jnp.float32)
    square = jnp.zeros((members, LANES), jnp.float32)
    for i, (start, size) in enumerate(zip(starts, sizes)):
        terms, square = chunk_step(
            received[i], spectra, models_t, wide, obs[start : start + size], terms, square
        )

    place = tile_cells % block_cells + jnp.where(home == me, 0, block_cells)
    order = (place[:, None] == jnp.arange(cells)[None, :]).astype(jnp.float32)
    terms = jnp.dot(terms, order, precision=HIGH)
    slab = members // devices
    sent = terms.reshape(devices, slab, cells)
    got = lax.all_to_all(sent, both, split_axis=0, concat_axis=0, tiled=True)
    got = jnp.sum(got.reshape(tiles, owners, slab, cells), axis=1)
    lent = (all_borrowed[None, :] == jnp.arange(tiles)[:, None]).astype(jnp.float32)
    gradient = got[:, :, :block_cells] + jnp.sum(
        lent[:, :, None, None] * got[None, :, :, block_cells:], axis=1
    )
    scale = jnp.sqrt(jnp.sum(gradient * gradient, axis=(0, 2)) / ncells + EPSILON)
    step = gradient / scale[None, :, None]
    step = step.reshape(tiles, slab, owners, owned).transpose(0, 2, 1, 3)
    step = step.reshape(devices, slab, owned)
    rider = jnp.broadcast_to(square[:, 0].reshape(1, slab, devices), (devices, slab, devices))
    back = lax.all_to_all(
        jnp.concatenate([step, rider], axis=2), both, split_axis=0, concat_axis=0, tiled=True
    )
    misfit = jnp.sum(back[:, :, owned:], axis=0).reshape(members) / (2.0 * total)
    back = back[:, :, :owned].reshape(members, owned)
    return (models - (STEP_LENGTH * misfit)[None, :] * back.T, misfit)


def solution(mesh):
    in_specs = (
        P("tile", "freq", None, None, None),
        P(("tile", "freq"), None),
        P("tile", None, "freq"),
        P(),
        P("tile", None),
        P(),
    )
    out_specs = (P(("tile", "freq"), None), P())
    return jax.shard_map(body, mesh=mesh, in_specs=in_specs, out_specs=out_specs, check_vma=False)
```

```python
import functools
import math

import jax
import jax.numpy as jnp
from jax import lax
from jax.experimental import pallas as pl
from jax.experimental.pallas import tpu as pltpu
from jax.sharding import PartitionSpec as P

HIGH = lax.Precision.HIGHEST
PHASE_RATE = 0.37
STEP_LENGTH = 0.5
EPSILON = 1e-06
GROUP = 8
LANES = 128

NN = (((1,), (0,)), ((), ()))
NT = (((1,), (1,)), ((), ()))


def swap(x, axis, k):
    return lax.ppermute(x, axis, [(i, i ^ k) for i in range(lax.axis_size(axis))])


def partner_order(size):
    assert size & (size - 1) == 0
    across, near = list(range(size // 2, size))[::-1], list(range(1, size // 2))[::-1]
    order = [k for pair in zip(across, near + [None]) for k in pair if k is not None]
    return order


def gate_table(owner_order, own_freqs, freqs, waveform, gate_index):
    samples = waveform.shape[0]
    freq_ids = (owner_order[:, None] * own_freqs + jnp.arange(own_freqs)[None, :]).reshape(freqs)
    freq_col = freq_ids.astype(jnp.float32)[:, None] + 0.5
    time_row = jnp.arange(samples, dtype=jnp.float32)[None, :] + 0.5
    phases = PHASE_RATE * freq_col * time_row
    kernel = jnp.stack([jnp.cos(phases), jnp.sin(phases)], axis=1) / math.sqrt(freqs)
    steps = jnp.arange(samples)
    lag = gate_index[:, None] - steps[None, :]
    picked = jnp.sum(
        jnp.where(lag[:, :, None] == steps[None, None, :], waveform[None, None, :], 0.0), axis=-1
    )
    return jnp.einsum("gk,fpk->gfp", picked, kernel, precision=HIGH).reshape(gate_index.shape[0], freqs * 2)


def split(x):
    high = x.astype(jnp.bfloat16)
    return high, (x - high.astype(jnp.float32)).astype(jnp.bfloat16)


def three_pass(a, b, dims):
    dot = functools.partial(lax.dot_general, dimension_numbers=dims, preferred_element_type=jnp.float32)
    return dot(a[0], b[0]) + (dot(a[0], b[1]) + dot(a[1], b[0]))


def params():
    return pltpu.CompilerParams(vmem_limit_bytes=48 * 1024 * 1024)


def cost(flops, bytes_accessed):
    return pl.CostEstimate(flops=flops, bytes_accessed=bytes_accessed, transcendentals=0)


def whole(a):
    return pl.BlockSpec(a.shape, lambda *_: (0,) * a.ndim)


ANY = pl.BlockSpec(memory_space=pl.ANY)
SCALARS = pl.BlockSpec(memory_space=pltpu.SMEM)


def pack_kernel(distances, own, first, rows, lanes, place_ref, block_ref, models_ref, *refs):
    outs, sems = refs[: len(distances)], refs[len(distances)]
    spectra = block_ref.shape[0]
    copies = []
    for j, k in enumerate(distances):
        row = pl.multiple_of((place_ref[1] ^ k) * own + first, GROUP)
        copies.append((block_ref.at[:, pl.ds(row, rows)], outs[j].at[pl.ds(0, spectra)]))
        owned, members = models_ref.shape
        for lane in range(lanes):
            part = owned // lanes
            target = outs[j].at[spectra, pl.ds(0, part), pl.ds(lane * members, members)]
            copies.append((models_ref.at[pl.ds(lane * part, part)], target))
    copies = [pltpu.make_async_copy(*c, sems.at[n]) for n, c in enumerate(copies)]
    for c in copies:
        c.start()
    for c in copies:
        c.wait()


def pack(place, block, models, distances, own, first, rows, lanes):
    spectra, _, cells = block.shape
    shape = jax.ShapeDtypeStruct((spectra + (lanes > 0), rows, cells), jnp.float32)
    return pl.pallas_call(
        functools.partial(pack_kernel, distances, own, first, rows, lanes),
        in_specs=[SCALARS, ANY, ANY],
        out_specs=[ANY] * len(distances),
        out_shape=[shape] * len(distances),
        scratch_shapes=[pltpu.SemaphoreType.DMA((len(distances) * (1 + lanes),))],
        cost_estimate=cost(0, 8 * len(distances) * spectra * rows * cells),
        name="pack",
    )(place, block, models)


def near_kernel(lanes, place_ref, cells_ref, models_ref, *refs):
    riders, out_ref = refs[:-1], refs[-1]
    owned, members = models_ref.shape
    part = owned // lanes
    out_ref[pl.ds(0, owned), :] = models_ref[...]
    for j, r in enumerate(riders):
        for lane in range(lanes):
            out_ref[pl.ds((j + 1) * owned + lane * part, part), :] = r[
                0, pl.ds(0, part), pl.ds(lane * members, members)
            ]
    block_cells = owned * (len(riders) + 1)
    home = cells_ref[...] // block_cells
    other = jnp.where(home == place_ref[0], -1, home).astype(jnp.float32)
    other = jnp.max(other, axis=1, keepdims=True)
    out_ref[pl.ds(block_cells, GROUP), :] = jnp.broadcast_to(other, (GROUP, members))


def near_models(place, cell_index, models, first, lanes):
    owned, members = models.shape
    slabs, rows, cells = first[0].shape
    rider = pl.BlockSpec((1, rows, cells), lambda i: (slabs - 1, 0, 0))
    return pl.pallas_call(
        functools.partial(near_kernel, lanes),
        grid=(1,),
        in_specs=[SCALARS, whole(cell_index), whole(models)] + [rider] * len(first),
        out_specs=pl.BlockSpec((owned * (len(first) + 1) + GROUP, members), lambda i: (0, 0)),
        out_shape=jax.ShapeDtypeStruct((owned * (len(first) + 1) + GROUP, members), jnp.float32),
        compiler_params=params(),
        cost_estimate=cost(0, 1 << 20),
        name="near_models",
    )(place, cell_index, models, *first)


def tile_models_kernel(owned, partners, place_ref, cells_ref, far_ref, high_ref, low_ref):
    tiles, rows, _ = far_ref.shape
    owners = len(partners)
    block_cells = owned * owners
    cells = cells_ref[...]
    distance = (cells // owned % owners) ^ place_ref[1]
    slot = jnp.zeros_like(cells)
    for n, k in enumerate(partners):
        slot = jnp.where(distance == k, n, slot)
    spot = slot * owned + cells % owned
    home = cells // block_cells
    high, low = None, None
    for t in range(tiles):
        row = lax.broadcasted_iota(jnp.int32, (block_cells, cells.shape[1]), 0)
        pick = jnp.where((row == spot) & (home == t), 1.0, 0.0).astype(jnp.bfloat16)
        h, l = split(far_ref[t, pl.ds(0, block_cells), :].T)
        h = lax.dot_general(h, pick, NN, preferred_element_type=jnp.float32)
        l = lax.dot_general(l, pick, NN, preferred_element_type=jnp.float32)
        high, low = (h, l) if t == 0 else (high + h, low + l)
    high_ref[...] = high.astype(jnp.bfloat16)
    low_ref[...] = low.astype(jnp.bfloat16)


def tile_models(place, cell_index, far, owned, partners):
    shape = jax.ShapeDtypeStruct((far.shape[2], cell_index.shape[1]), jnp.bfloat16)
    return pl.pallas_call(
        functools.partial(tile_models_kernel, owned, partners),
        in_specs=[SCALARS] + [pl.BlockSpec(memory_space=pltpu.VMEM)] * 2,
        out_specs=[pl.BlockSpec(memory_space=pltpu.VMEM)] * 2,
        out_shape=[shape] * 2,
        compiler_params=params(),
        cost_estimate=cost(1 << 30, 2 << 20),
        name="tile_models",
    )(place, cell_index, far)


def wide_kernel(table_ref, high_ref, low_ref):
    fp, gates = table_ref.shape
    rows, columns = high_ref.shape
    iota = lax.broadcasted_iota
    down = (iota(jnp.int32, (rows, fp), 0) // GROUP == iota(jnp.int32, (rows, fp), 1)).astype(jnp.float32)
    across = iota(jnp.int32, (gates, columns), 1) // GROUP == iota(jnp.int32, (gates, columns), 0)
    across = across.astype(jnp.float32).astype(jnp.bfloat16)
    down = down.astype(jnp.bfloat16)
    same = iota(jnp.int32, (rows, columns), 0) % GROUP == iota(jnp.int32, (rows, columns), 1) % GROUP
    for part, ref in zip(split(table_ref[...]), (high_ref, low_ref)):
        tall = lax.dot_general(down, part, NN, preferred_element_type=jnp.float32).astype(jnp.bfloat16)
        full = lax.dot_general(tall, across, NN, preferred_element_type=jnp.float32)
        ref[...] = jnp.where(same, full, 0.0).astype(jnp.bfloat16)


def wide_table(table):
    shape = jax.ShapeDtypeStruct((table.shape[0] * GROUP, table.shape[1] * GROUP), jnp.bfloat16)
    return pl.pallas_call(
        wide_kernel,
        in_specs=[pl.BlockSpec(memory_space=pltpu.VMEM)],
        out_specs=[pl.BlockSpec(memory_space=pltpu.VMEM)] * 2,
        out_shape=[shape] * 2,
        compiler_params=params(),
        cost_estimate=cost(1 << 28, 1 << 20),
        name="wide_table",
    )(table)


def chunk_kernel(pieces, block_cells, last, place_ref, *refs):
    sens_refs = refs[:pieces]
    model_h, model_l, gate_h, gate_l, obs_ref, cells_ref, terms_in, square_in, terms_ref, square_ref = refs[pieces:]

    @pl.when(pl.program_id(0) == 0)
    def _():
        terms_ref[...] = terms_in[...]
        square_ref[...] = square_in[...]

    sens = [split(r[...].reshape(r.shape[0] * r.shape[1], r.shape[2])) for r in sens_refs]
    sens = tuple(jnp.concatenate([s[i] for s in sens], axis=0) for i in range(2))
    gates = (gate_h[...], gate_l[...])
    predicted = three_pass((model_h[...], model_l[...]), sens, NT)
    misfit_rows = three_pass(split(predicted), gates, NN) - obs_ref[0]
    square_ref[...] += jnp.sum(misfit_rows * misfit_rows, axis=1, keepdims=True)
    back = three_pass(split(misfit_rows), gates, NT)
    terms = terms_ref[...] + three_pass(split(back), sens, NN)
    terms_ref[...] = terms

    if last:

        @pl.when(pl.program_id(0) == pl.num_programs(0) - 1)
        def _():
            cells = cells_ref[...]
            spot = cells % block_cells + jnp.where(cells // block_cells == place_ref[0], 0, block_cells)
            size = cells.shape[1]
            row = lax.broadcasted_iota(jnp.int32, (size, size), 0)
            pick = jnp.where(row == spot, 1.0, 0.0).astype(jnp.bfloat16)
            high = terms.astype(jnp.bfloat16)
            middle, low = split(terms - high.astype(jnp.float32))
            dot = functools.partial(lax.dot_general, dimension_numbers=NT, preferred_element_type=jnp.float32)
            terms_ref[...] = dot(high, pick) + (dot(middle, pick) + dot(low, pick))


def chunk_step(place, block, sens, first, models_t, gates, obs, cell_index, terms, square, block_cells, last):
    spectra, soundings, cells = block.shape
    rows = sens[0].shape[1]
    pieces = len(sens) + 1
    members = terms.shape[0]
    own_groups = soundings // (pieces * GROUP)
    return pl.pallas_call(
        functools.partial(chunk_kernel, pieces, block_cells, last),
        grid_spec=pltpu.PrefetchScalarGridSpec(
            num_scalar_prefetch=1,
            grid=(rows // GROUP,),
            in_specs=[
                pl.BlockSpec((spectra, GROUP, cells), lambda i, place: (0, place[1] * own_groups + first + i, 0))
            ]
            + [pl.BlockSpec((spectra, GROUP, cells), lambda i, place: (0, i, 0))] * len(sens)
            + [whole(a) for a in (*models_t, *gates)]
            + [pl.BlockSpec((1, 1, obs.shape[2]), lambda i, place: (first + i, 0, 0)), whole(cell_index)]
            + [whole(terms), whole(square)],
            out_specs=[whole(terms), whole(square)],
        ),
        out_shape=[
            jax.ShapeDtypeStruct(terms.shape, jnp.float32),
            jax.ShapeDtypeStruct(square.shape, jnp.float32),
        ],
        input_output_aliases={pieces + 7: 0, pieces + 8: 1},
        compiler_params=params(),
        cost_estimate=cost(
            12 * pieces * spectra * rows * cells * members * 2, 4 * pieces * spectra * rows * cells
        ),
        name="chunk_step",
    )(place, block, *sens, *models_t, *gates, obs, cell_index, terms, square)


def exact_dot(a, b, dims):
    return lax.dot_general(a, b, dims, precision=HIGH, preferred_element_type=jnp.float32)


def gradient_kernel(tiles, owned, borrowed_ref, got_ref, square_ref, out_ref):
    devices, slab, cells = got_ref.shape
    owners = devices // tiles
    block_cells = owned * owners
    members = square_ref.shape[0]
    sums = []
    for t in range(tiles):
        total = got_ref[t * owners]
        for f in range(1, owners):
            total = total + got_ref[t * owners + f]
        sums.append(total)
    gradient = []
    for b in range(tiles):
        block = sums[b][:, :block_cells]
        for t in range(tiles):
            block = block + jnp.where(borrowed_ref[t] == b, sums[t][:, block_cells:], 0.0)
        gradient.append(block)
    square = sum(jnp.sum(g * g, axis=1, keepdims=True) for g in gradient)
    scale = jnp.sqrt(square / (tiles * block_cells) + EPSILON)
    iota = lax.broadcasted_iota
    per_row = members // slab
    down = (iota(jnp.int32, (slab, members), 1) // per_row == iota(jnp.int32, (slab, members), 0))
    lane = iota(jnp.int32, (members, LANES), 1)
    spread = jnp.where(iota(jnp.int32, (members, LANES), 0) % per_row + owned == lane, square_ref[...], 0.0)
    rider = exact_dot(down.astype(jnp.float32), spread, NN)
    for b in range(tiles):
        step = gradient[b] / scale
        for f in range(owners):
            piece = step[:, f * owned : (f + 1) * owned]
            piece = jnp.concatenate([piece, jnp.zeros((slab, LANES - owned), jnp.float32)], axis=1)
            out_ref[b * owners + f] = piece + rider


def gradient_step(borrowed, got, square, tiles, owned):
    devices, slab, _ = got.shape
    return pl.pallas_call(
        functools.partial(gradient_kernel, tiles, owned),
        in_specs=[SCALARS] + [pl.BlockSpec(memory_space=pltpu.VMEM)] * 2,
        out_specs=pl.BlockSpec(memory_space=pltpu.VMEM),
        out_shape=jax.ShapeDtypeStruct((devices, slab, LANES), jnp.float32),
        compiler_params=params(),
        cost_estimate=cost(1 << 22, 1 << 20),
        name="gradient_step",
    )(borrowed, got, square)


def update_kernel(divisor, models_ref, back_ref, updated_ref, misfit_ref):
    devices, slab, _ = back_ref.shape
    owned, members = models_ref.shape
    per_row = members // slab
    iota = lax.broadcasted_iota
    riders = back_ref[0]
    for d in range(1, devices):
        riders = riders + back_ref[d]
    down = (iota(jnp.int32, (slab, members), 1) // per_row == iota(jnp.int32, (slab, members), 0))
    tall = exact_dot(riders, down.astype(jnp.float32), (((0,), (0,)), ((), ())))
    mine = iota(jnp.int32, (LANES, members), 1) % per_row + owned == iota(jnp.int32, (LANES, members), 0)
    misfit = jnp.sum(jnp.where(mine, tall, 0.0), axis=0, keepdims=True) / divisor
    step = back_ref[...].reshape(members, LANES).T[:owned]
    updated_ref[...] = models_ref[...] - STEP_LENGTH * misfit * step
    misfit_ref[...] = misfit


def update(models, back, divisor):
    return pl.pallas_call(
        functools.partial(update_kernel, divisor),
        in_specs=[pl.BlockSpec(memory_space=pltpu.VMEM)] * 2,
        out_specs=[pl.BlockSpec(memory_space=pltpu.VMEM)] * 2,
        out_shape=[
            jax.ShapeDtypeStruct(models.shape, jnp.float32),
            jax.ShapeDtypeStruct((1, models.shape[1]), jnp.float32),
        ],
        compiler_params=params(),
        cost_estimate=cost(1 << 20, 1 << 18),
        name="update",
    )(models, back)


def chunk_groups(groups, riders):
    if groups < 8:
        return [1] * groups
    first, last = max(groups // 8, riders), [groups // 8, groups // 16 or 1]
    rest = groups - first - sum(last)
    middle = -(-rest // (groups // 4))
    return [first] + [rest // middle + (i < rest % middle) for i in range(middle)] + last


def body(sensitivity, models, observed, waveform, cell_index, gate_index):
    both = ("tile", "freq")
    tiles, owners, devices = lax.axis_size("tile"), lax.axis_size("freq"), lax.axis_size(both)
    _, own_freqs, parts, soundings, cells = sensitivity.shape
    freqs = own_freqs * owners
    spectra = own_freqs * parts
    owned, members = models.shape
    ncells = owned * devices
    gates = gate_index.shape[0]
    divisor = 2.0 * tiles * soundings * gates
    own = soundings // owners
    block_cells = owned * owners
    place = jnp.stack([lax.axis_index("tile"), lax.axis_index("freq")])

    block = sensitivity[0].reshape(spectra, soundings, cells)
    lanes = cells // members if owned % (GROUP * (cells // members)) == 0 else 1
    sizes = chunk_groups(own // GROUP, -(-owned // (lanes * GROUP)))
    starts = [sum(sizes[:i]) for i in range(len(sizes))]
    distances = partner_order(owners)
    partners = [0] + distances
    received = []
    for i, (start, size) in enumerate(zip(starts, sizes)):
        pieces = pack(
            place, block, models, distances, own, start * GROUP, size * GROUP, lanes if i == 0 else 0
        )
        received.append([swap(p, "freq", k) for p, k in zip(pieces, distances)])

    near = near_models(place, cell_index, models, received[0], lanes)
    far = lax.all_gather(near, "tile", axis=0, tiled=False)
    all_borrowed = far[:, block_cells, 0].astype(jnp.int32)
    models_t = tile_models(place, cell_index, far, owned, partners)

    order = place[1] ^ jnp.array(partners, jnp.int32)
    wide = wide_table(gate_table(order, own_freqs, freqs, waveform, gate_index).T)
    obs = observed[0].reshape(gates, own // GROUP, GROUP)
    obs = jnp.swapaxes(obs, 0, 1).reshape(own // GROUP, 1, gates * GROUP)

    terms = jnp.zeros((members, cells), jnp.float32)
    square = jnp.zeros((members, LANES), jnp.float32)
    for i, start in enumerate(starts):
        last = i == len(starts) - 1
        terms, square = chunk_step(
            place, block, received[i], start, models_t, wide, obs, cell_index, terms, square, block_cells, last
        )

    slab = members // devices
    sent = terms.reshape(devices, slab, cells)
    got = lax.all_to_all(sent, both, split_axis=0, concat_axis=0, tiled=True)
    if slab % GROUP == 0 and members // slab + owned <= LANES:
        step = gradient_step(all_borrowed, got, square, tiles, owned)
        back = lax.all_to_all(step, both, split_axis=0, concat_axis=0, tiled=True)
        updated, misfit = update(models, back, divisor)
        return (updated, misfit.reshape(members))

    got = jnp.sum(got.reshape(tiles, owners, slab, cells), axis=1)
    lent = (all_borrowed[None, :] == jnp.arange(tiles)[:, None]).astype(jnp.float32)
    gradient = got[:, :, :block_cells] + jnp.sum(
        lent[:, :, None, None] * got[None, :, :, block_cells:], axis=1
    )
    scale = jnp.sqrt(jnp.sum(gradient * gradient, axis=(0, 2)) / ncells + EPSILON)
    step = gradient / scale[None, :, None]
    step = step.reshape(tiles, slab, owners, owned).transpose(0, 2, 1, 3)
    step = step.reshape(devices, slab, owned)
    rider = jnp.broadcast_to(square[:, 0].reshape(1, slab, devices), (devices, slab, devices))
    back = lax.all_to_all(
        jnp.concatenate([step, rider], axis=2), both, split_axis=0, concat_axis=0, tiled=True
    )
    misfit = jnp.sum(back[:, :, owned:], axis=0).reshape(members) / divisor
    back = back[:, :, :owned].reshape(members, owned)
    return (models - (STEP_LENGTH * misfit)[None, :] * back.T, misfit)


def solution(mesh):
    in_specs = (
        P("tile", "freq", None, None, None),
        P(("tile", "freq"), None),
        P("tile", None, "freq"),
        P(),
        P("tile", None),
        P(),
    )
    out_specs = (P(("tile", "freq"), None), P())
    return jax.shard_map(body, mesh=mesh, in_specs=in_specs, out_specs=out_specs, check_vma=False)
```

```python
import functools
import math

import jax
import jax.numpy as jnp
from jax import lax
from jax.experimental import pallas as pl
from jax.experimental.pallas import tpu as pltpu
from jax.sharding import PartitionSpec as P

HIGH = lax.Precision.HIGHEST
PHASE_RATE = 0.37
STEP_LENGTH = 0.5
EPSILON = 1e-06
GROUP = 8
LANES = 128

NN = (((1,), (0,)), ((), ()))
NT = (((1,), (1,)), ((), ()))


def swap(x, axis, k):
    return lax.ppermute(x, axis, [(i, i ^ k) for i in range(lax.axis_size(axis))])


def partner_order(size):
    assert size & (size - 1) == 0
    across, near = list(range(size // 2, size))[::-1], list(range(1, size // 2))[::-1]
    order = [k for pair in zip(across, near + [None]) for k in pair if k is not None]
    return order


def gate_table(owner_order, own_freqs, freqs, waveform, gate_index):
    samples = waveform.shape[0]
    freq_ids = (owner_order[:, None] * own_freqs + jnp.arange(own_freqs)[None, :]).reshape(freqs)
    freq_col = freq_ids.astype(jnp.float32)[:, None] + 0.5
    time_row = jnp.arange(samples, dtype=jnp.float32)[None, :] + 0.5
    phases = PHASE_RATE * freq_col * time_row
    kernel = jnp.stack([jnp.cos(phases), jnp.sin(phases)], axis=1) / math.sqrt(freqs)
    steps = jnp.arange(samples)
    lag = gate_index[:, None] - steps[None, :]
    picked = jnp.sum(
        jnp.where(lag[:, :, None] == steps[None, None, :], waveform[None, None, :], 0.0), axis=-1
    )
    return jnp.einsum("gk,fpk->gfp", picked, kernel, precision=HIGH).reshape(gate_index.shape[0], freqs * 2)


def split(x):
    high = x.astype(jnp.bfloat16)
    return high, (x - high.astype(jnp.float32)).astype(jnp.bfloat16)


def three_pass(a, b, dims):
    dot = functools.partial(lax.dot_general, dimension_numbers=dims, preferred_element_type=jnp.float32)
    return dot(a[0], b[0]) + (dot(a[0], b[1]) + dot(a[1], b[0]))


def params(mebibytes):
    return pltpu.CompilerParams(vmem_limit_bytes=mebibytes * 1024 * 1024)


def cost(flops, bytes_accessed):
    return pl.CostEstimate(flops=flops, bytes_accessed=bytes_accessed, transcendentals=0)


def whole(a):
    return pl.BlockSpec(a.shape, lambda *_: (0,) * a.ndim)


HBM = pl.BlockSpec(memory_space=pltpu.HBM)
SCALARS = pl.BlockSpec(memory_space=pltpu.SMEM)


def pack_kernel(distances, own, first, lanes, place_ref, block_ref, models_ref, *refs):
    outs, (held, in_sems, out_sems) = refs[: len(distances)], refs[len(distances) :]
    spectra, rows = block_ref.shape[0], held.shape[2]
    owned, members = models_ref.shape
    arrivals, departures = [], []
    for j, k in enumerate(distances):
        row = pl.multiple_of((place_ref[1] ^ k) * own + first, GROUP)
        source, target = block_ref.at[:, pl.ds(row, rows)], held.at[j, pl.ds(0, spectra)]
        arrivals.append(pltpu.make_async_copy(source, target, in_sems.at[j]))
        departures.append(pltpu.make_async_copy(held.at[j], outs[j], out_sems.at[j]))
        arrivals[j].start()
    for j in range(len(distances)):
        for lane in range(lanes):
            part = owned // lanes
            held[j, spectra, pl.ds(0, part), pl.ds(lane * members, members)] = models_ref[pl.ds(lane * part, part), :]
    for arrival, departure in zip(arrivals, departures):
        arrival.wait()
        departure.start()
    for departure in departures:
        departure.wait()


def pack(place, block, models, distances, own, first, rows, lanes):
    spectra, _, cells = block.shape
    count = len(distances)
    shape = (spectra + (lanes > 0), rows, cells)
    return pl.pallas_call(
        functools.partial(pack_kernel, distances, own, first, lanes),
        in_specs=[SCALARS, HBM, pl.BlockSpec(memory_space=pltpu.VMEM)],
        out_specs=[HBM] * count,
        out_shape=[jax.ShapeDtypeStruct(shape, jnp.float32)] * count,
        scratch_shapes=[
            pltpu.VMEM((count, *shape), jnp.float32),
            pltpu.SemaphoreType.DMA((count,)),
            pltpu.SemaphoreType.DMA((count,)),
        ],
        compiler_params=params(48),
        cost_estimate=cost(0, 8 * count * spectra * rows * cells),
        name="pack",
    )(place, block, models)


def near_kernel(lanes, place_ref, cells_ref, models_ref, *refs):
    riders, out_ref = refs[:-1], refs[-1]
    owned, members = models_ref.shape
    part = owned // lanes
    out_ref[pl.ds(0, owned), :] = models_ref[...]
    for j, r in enumerate(riders):
        for lane in range(lanes):
            out_ref[pl.ds((j + 1) * owned + lane * part, part), :] = r[
                0, pl.ds(0, part), pl.ds(lane * members, members)
            ]
    block_cells = owned * (len(riders) + 1)
    home = cells_ref[...] // block_cells
    other = jnp.where(home == place_ref[0], -1, home).astype(jnp.float32)
    other = jnp.max(other, axis=1, keepdims=True)
    out_ref[pl.ds(block_cells, GROUP), :] = jnp.broadcast_to(other, (GROUP, members))


def near_models(place, cell_index, models, first, lanes):
    owned, members = models.shape
    slabs, rows, cells = first[0].shape
    rider = pl.BlockSpec((1, rows, cells), lambda i: (slabs - 1, 0, 0))
    return pl.pallas_call(
        functools.partial(near_kernel, lanes),
        grid=(1,),
        in_specs=[SCALARS, whole(cell_index), whole(models)] + [rider] * len(first),
        out_specs=pl.BlockSpec((owned * (len(first) + 1) + GROUP, members), lambda i: (0, 0)),
        out_shape=jax.ShapeDtypeStruct((owned * (len(first) + 1) + GROUP, members), jnp.float32),
        compiler_params=params(16),
        cost_estimate=cost(0, 1 << 20),
        name="near_models",
    )(place, cell_index, models, *first)


def tile_models_kernel(owned, partners, place_ref, cells_ref, *refs):
    tile_refs, (high_ref, low_ref) = refs[:-2], refs[-2:]
    block_cells = owned * len(partners)
    cells = cells_ref[...]
    distance = (cells // owned % len(partners)) ^ place_ref[1]
    slot = jnp.zeros_like(cells)
    for n, k in enumerate(partners):
        slot = jnp.where(distance == k, n, slot)
    spot = slot * owned + cells % owned
    away = (cells // block_cells) ^ place_ref[0]
    high, low = None, None
    for k, ref in enumerate(tile_refs):
        row = lax.broadcasted_iota(jnp.int32, (block_cells, cells.shape[1]), 0)
        pick = jnp.where((row == spot) & (away == k), 1.0, 0.0).astype(jnp.bfloat16)
        h, l = split(ref[pl.ds(0, block_cells), :].T)
        h = lax.dot_general(h, pick, NN, preferred_element_type=jnp.float32)
        l = lax.dot_general(l, pick, NN, preferred_element_type=jnp.float32)
        high, low = (h, l) if k == 0 else (high + h, low + l)
    high_ref[...] = high.astype(jnp.bfloat16)
    low_ref[...] = low.astype(jnp.bfloat16)


def tile_models(place, cell_index, tiles, owned, partners):
    shape = jax.ShapeDtypeStruct((tiles[0].shape[1], cell_index.shape[1]), jnp.bfloat16)
    return pl.pallas_call(
        functools.partial(tile_models_kernel, owned, partners),
        in_specs=[SCALARS] + [pl.BlockSpec(memory_space=pltpu.VMEM)] * (1 + len(tiles)),
        out_specs=[pl.BlockSpec(memory_space=pltpu.VMEM)] * 2,
        out_shape=[shape] * 2,
        compiler_params=params(16),
        cost_estimate=cost(1 << 30, 2 << 20),
        name="tile_models",
    )(place, cell_index, *tiles)


def wide_kernel(table_ref, high_ref, low_ref):
    fp, gates = table_ref.shape
    rows, columns = high_ref.shape
    iota = lax.broadcasted_iota
    down = (iota(jnp.int32, (rows, fp), 0) // GROUP == iota(jnp.int32, (rows, fp), 1)).astype(jnp.float32)
    across = iota(jnp.int32, (gates, columns), 1) // GROUP == iota(jnp.int32, (gates, columns), 0)
    across = across.astype(jnp.float32).astype(jnp.bfloat16)
    down = down.astype(jnp.bfloat16)
    same = iota(jnp.int32, (rows, columns), 0) % GROUP == iota(jnp.int32, (rows, columns), 1) % GROUP
    for part, ref in zip(split(table_ref[...]), (high_ref, low_ref)):
        tall = lax.dot_general(down, part, NN, preferred_element_type=jnp.float32).astype(jnp.bfloat16)
        full = lax.dot_general(tall, across, NN, preferred_element_type=jnp.float32)
        ref[...] = jnp.where(same, full, 0.0).astype(jnp.bfloat16)


def wide_table(table):
    shape = jax.ShapeDtypeStruct((table.shape[0] * GROUP, table.shape[1] * GROUP), jnp.bfloat16)
    return pl.pallas_call(
        wide_kernel,
        in_specs=[pl.BlockSpec(memory_space=pltpu.VMEM)],
        out_specs=[pl.BlockSpec(memory_space=pltpu.VMEM)] * 2,
        out_shape=[shape] * 2,
        compiler_params=params(16),
        cost_estimate=cost(1 << 28, 1 << 20),
        name="wide_table",
    )(table)


def chunk_kernel(pieces, block_cells, last, place_ref, *refs):
    sens_refs = refs[:pieces]
    model_h, model_l, gate_h, gate_l, obs_ref, cells_ref, terms_in, square_in, terms_ref, square_ref = refs[pieces:]

    @pl.when(pl.program_id(0) == 0)
    def _():
        terms_ref[...] = terms_in[...]
        square_ref[...] = square_in[...]

    sens = [split(r[...].reshape(r.shape[0] * r.shape[1], r.shape[2])) for r in sens_refs]
    sens = tuple(jnp.concatenate([s[i] for s in sens], axis=0) for i in range(2))
    gates = (gate_h[...], gate_l[...])
    predicted = three_pass((model_h[...], model_l[...]), sens, NT)
    misfit_rows = three_pass(split(predicted), gates, NN) - obs_ref[0]
    square_ref[...] += jnp.sum(misfit_rows * misfit_rows, axis=1, keepdims=True)
    back = three_pass(split(misfit_rows), gates, NT)
    terms = terms_ref[...] + three_pass(split(back), sens, NN)
    terms_ref[...] = terms

    if last:

        @pl.when(pl.program_id(0) == pl.num_programs(0) - 1)
        def _():
            cells = cells_ref[...]
            spot = cells % block_cells + jnp.where(cells // block_cells == place_ref[0], 0, block_cells)
            size = cells.shape[1]
            row = lax.broadcasted_iota(jnp.int32, (size, size), 0)
            pick = jnp.where(row == spot, 1.0, 0.0).astype(jnp.bfloat16)
            high = terms.astype(jnp.bfloat16)
            middle, low = split(terms - high.astype(jnp.float32))
            dot = functools.partial(lax.dot_general, dimension_numbers=NT, preferred_element_type=jnp.float32)
            terms_ref[...] = dot(high, pick) + (dot(middle, pick) + dot(low, pick))


def chunk_step(place, block, sens, first, models_t, gates, obs, cell_index, terms, square, block_cells, last):
    spectra, soundings, cells = block.shape
    rows = sens[0].shape[1]
    pieces = len(sens) + 1
    members = terms.shape[0]
    own_groups = soundings // (pieces * GROUP)
    return pl.pallas_call(
        functools.partial(chunk_kernel, pieces, block_cells, last),
        grid_spec=pltpu.PrefetchScalarGridSpec(
            num_scalar_prefetch=1,
            grid=(rows // GROUP,),
            in_specs=[
                pl.BlockSpec((spectra, GROUP, cells), lambda i, place: (0, place[1] * own_groups + first + i, 0))
            ]
            + [pl.BlockSpec((spectra, GROUP, cells), lambda i, place: (0, i, 0))] * len(sens)
            + [whole(a) for a in (*models_t, *gates)]
            + [pl.BlockSpec((1, 1, obs.shape[2]), lambda i, place: (first + i, 0, 0)), whole(cell_index)]
            + [whole(terms), whole(square)],
            out_specs=[whole(terms), whole(square)],
        ),
        out_shape=[
            jax.ShapeDtypeStruct(terms.shape, jnp.float32),
            jax.ShapeDtypeStruct(square.shape, jnp.float32),
        ],
        input_output_aliases={pieces + 7: 0, pieces + 8: 1},
        compiler_params=params(40),
        cost_estimate=cost(
            12 * pieces * spectra * rows * cells * members * 2, 4 * pieces * spectra * rows * cells
        ),
        name="chunk_step",
    )(place, block, *sens, *models_t, *gates, obs, cell_index, terms, square)


def exact_dot(a, b, dims):
    return lax.dot_general(a, b, dims, precision=HIGH, preferred_element_type=jnp.float32)


def gradient_kernel(tiles, owned, place_ref, borrowed_ref, got_ref, square_ref, out_ref):
    devices, slab, cells = got_ref.shape
    owners = devices // tiles
    block_cells = owned * owners
    members = square_ref.shape[0]
    sums = []
    for t in range(tiles):
        total = got_ref[t * owners]
        for f in range(1, owners):
            total = total + got_ref[t * owners + f]
        sums.append(total)
    gradient = []
    for b in range(tiles):
        block = sums[b][:, :block_cells]
        for t in range(tiles):
            block = block + jnp.where(borrowed_ref[place_ref[0] ^ t] == b, sums[t][:, block_cells:], 0.0)
        gradient.append(block)
    square = sum(jnp.sum(g * g, axis=1, keepdims=True) for g in gradient)
    scale = jnp.sqrt(square / (tiles * block_cells) + EPSILON)
    iota = lax.broadcasted_iota
    per_row = members // slab
    down = (iota(jnp.int32, (slab, members), 1) // per_row == iota(jnp.int32, (slab, members), 0))
    lane = iota(jnp.int32, (members, LANES), 1)
    spread = jnp.where(iota(jnp.int32, (members, LANES), 0) % per_row + owned == lane, square_ref[...], 0.0)
    rider = exact_dot(down.astype(jnp.float32), spread, NN)
    for b in range(tiles):
        step = gradient[b] / scale
        for f in range(owners):
            piece = step[:, f * owned : (f + 1) * owned]
            piece = jnp.concatenate([piece, jnp.zeros((slab, LANES - owned), jnp.float32)], axis=1)
            out_ref[b * owners + f] = piece + rider


def gradient_step(place, borrowed, got, square, tiles, owned):
    devices, slab, _ = got.shape
    return pl.pallas_call(
        functools.partial(gradient_kernel, tiles, owned),
        in_specs=[SCALARS] * 2 + [pl.BlockSpec(memory_space=pltpu.VMEM)] * 2,
        out_specs=pl.BlockSpec(memory_space=pltpu.VMEM),
        out_shape=jax.ShapeDtypeStruct((devices, slab, LANES), jnp.float32),
        compiler_params=params(16),
        cost_estimate=cost(1 << 22, 1 << 20),
        name="gradient_step",
    )(place, borrowed, got, square)


def update_kernel(divisor, models_ref, back_ref, updated_ref, misfit_ref):
    devices, slab, _ = back_ref.shape
    owned, members = models_ref.shape
    per_row = members // slab
    iota = lax.broadcasted_iota
    riders = back_ref[0]
    for d in range(1, devices):
        riders = riders + back_ref[d]
    down = (iota(jnp.int32, (slab, members), 1) // per_row == iota(jnp.int32, (slab, members), 0))
    tall = exact_dot(riders, down.astype(jnp.float32), (((0,), (0,)), ((), ())))
    mine = iota(jnp.int32, (LANES, members), 1) % per_row + owned == iota(jnp.int32, (LANES, members), 0)
    misfit = jnp.sum(jnp.where(mine, tall, 0.0), axis=0, keepdims=True) / divisor
    step = back_ref[...].reshape(members, LANES).T[:owned]
    updated_ref[...] = models_ref[...] - STEP_LENGTH * misfit * step
    misfit_ref[...] = misfit


def update(models, back, divisor):
    return pl.pallas_call(
        functools.partial(update_kernel, divisor),
        in_specs=[pl.BlockSpec(memory_space=pltpu.VMEM)] * 2,
        out_specs=[pl.BlockSpec(memory_space=pltpu.VMEM)] * 2,
        out_shape=[
            jax.ShapeDtypeStruct(models.shape, jnp.float32),
            jax.ShapeDtypeStruct((1, models.shape[1]), jnp.float32),
        ],
        compiler_params=params(16),
        cost_estimate=cost(1 << 20, 1 << 18),
        name="update",
    )(models, back)


def chunk_groups(groups, riders):
    if groups < 8:
        return [1] * groups
    first, last = max(groups // 8, riders), [groups // 8, groups // 16 or 1]
    rest = groups - first - sum(last)
    middle = -(-rest // (groups // 4))
    return [first] + [rest // middle + (i < rest % middle) for i in range(middle)] + last


def body(sensitivity, models, observed, waveform, cell_index, gate_index):
    both = ("tile", "freq")
    tiles, owners, devices = lax.axis_size("tile"), lax.axis_size("freq"), lax.axis_size(both)
    _, own_freqs, parts, soundings, cells = sensitivity.shape
    freqs = own_freqs * owners
    spectra = own_freqs * parts
    owned, members = models.shape
    ncells = owned * devices
    gates = gate_index.shape[0]
    divisor = 2.0 * tiles * soundings * gates
    own = soundings // owners
    block_cells = owned * owners
    place = jnp.stack([lax.axis_index("tile"), lax.axis_index("freq")])

    block = sensitivity[0].reshape(spectra, soundings, cells)
    lanes = cells // members if owned % (GROUP * (cells // members)) == 0 else 1
    sizes = chunk_groups(own // GROUP, -(-owned // (lanes * GROUP)))
    starts = [sum(sizes[:i]) for i in range(len(sizes))]
    distances = partner_order(owners)
    partners = [0] + distances
    received = []
    for i, (start, size) in enumerate(zip(starts, sizes)):
        pieces = pack(
            place, block, models, distances, own, start * GROUP, size * GROUP, lanes if i == 0 else 0
        )
        received.append([swap(p, "freq", k) for p, k in zip(pieces, distances)])

    near = near_models(place, cell_index, models, received[0], lanes)
    blocks = [near] + [swap(near, "tile", k) for k in range(1, tiles)]
    borrowed = jnp.stack([b[block_cells, 0] for b in blocks]).astype(jnp.int32)
    models_t = tile_models(place, cell_index, blocks, owned, partners)

    order = place[1] ^ jnp.array(partners, jnp.int32)
    wide = wide_table(gate_table(order, own_freqs, freqs, waveform, gate_index).T)
    obs = observed[0].reshape(gates, own // GROUP, GROUP)
    obs = jnp.swapaxes(obs, 0, 1).reshape(own // GROUP, 1, gates * GROUP)

    terms = jnp.zeros((members, cells), jnp.float32)
    square = jnp.zeros((members, LANES), jnp.float32)
    for i, start in enumerate(starts):
        last = i == len(starts) - 1
        terms, square = chunk_step(
            place, block, received[i], start, models_t, wide, obs, cell_index, terms, square, block_cells, last
        )

    slab = members // devices
    sent = terms.reshape(devices, slab, cells)
    got = lax.all_to_all(sent, both, split_axis=0, concat_axis=0, tiled=True)
    if slab % GROUP == 0 and members // slab + owned <= LANES:
        step = gradient_step(place, borrowed, got, square, tiles, owned)
        back = lax.all_to_all(step, both, split_axis=0, concat_axis=0, tiled=True)
        updated, misfit = update(models, back, divisor)
        return (updated, misfit.reshape(members))

    got = jnp.sum(got.reshape(tiles, owners, slab, cells), axis=1)
    tile_ids = jnp.arange(tiles)
    lent = (jnp.take(borrowed, tile_ids ^ place[0])[None, :] == tile_ids[:, None]).astype(jnp.float32)
    gradient = got[:, :, :block_cells] + jnp.sum(
        lent[:, :, None, None] * got[None, :, :, block_cells:], axis=1
    )
    scale = jnp.sqrt(jnp.sum(gradient * gradient, axis=(0, 2)) / ncells + EPSILON)
    step = gradient / scale[None, :, None]
    step = step.reshape(tiles, slab, owners, owned).transpose(0, 2, 1, 3)
    step = step.reshape(devices, slab, owned)
    rider = jnp.broadcast_to(square[:, 0].reshape(1, slab, devices), (devices, slab, devices))
    back = lax.all_to_all(
        jnp.concatenate([step, rider], axis=2), both, split_axis=0, concat_axis=0, tiled=True
    )
    misfit = jnp.sum(back[:, :, owned:], axis=0).reshape(members) / divisor
    back = back[:, :, :owned].reshape(members, owned)
    return (models - (STEP_LENGTH * misfit)[None, :] * back.T, misfit)


def solution(mesh):
    in_specs = (
        P("tile", "freq", None, None, None),
        P(("tile", "freq"), None),
        P("tile", None, "freq"),
        P(),
        P("tile", None),
        P(),
    )
    out_specs = (P(("tile", "freq"), None), P())
    return jax.shard_map(body, mesh=mesh, in_specs=in_specs, out_specs=out_specs, check_vma=False)
```

```python
import functools
import math

import jax
import jax.numpy as jnp
from jax import lax
from jax.experimental import pallas as pl
from jax.experimental.pallas import tpu as pltpu
from jax.sharding import PartitionSpec as P

HIGH = lax.Precision.HIGHEST
PHASE_RATE = 0.37
STEP_LENGTH = 0.5
EPSILON = 1e-06
GROUP = 8
LANES = 128

NN = (((1,), (0,)), ((), ()))
NT = (((1,), (1,)), ((), ()))


def swap(x, axis, k):
    return lax.ppermute(x, axis, [(i, i ^ k) for i in range(lax.axis_size(axis))])


def partner_order(size):
    assert size & (size - 1) == 0
    return list(range(1, size))[::-1]


def gate_table(owner_order, own_freqs, freqs, waveform, gate_index):
    samples = waveform.shape[0]
    freq_ids = (owner_order[:, None] * own_freqs + jnp.arange(own_freqs)[None, :]).reshape(freqs)
    freq_col = freq_ids.astype(jnp.float32)[:, None] + 0.5
    time_row = jnp.arange(samples, dtype=jnp.float32)[None, :] + 0.5
    phases = PHASE_RATE * freq_col * time_row
    kernel = jnp.stack([jnp.cos(phases), jnp.sin(phases)], axis=1) / math.sqrt(freqs)
    steps = jnp.arange(samples)
    lag = gate_index[:, None] - steps[None, :]
    picked = jnp.sum(
        jnp.where(lag[:, :, None] == steps[None, None, :], waveform[None, None, :], 0.0), axis=-1
    )
    return jnp.einsum("gk,fpk->gfp", picked, kernel, precision=HIGH).reshape(gate_index.shape[0], freqs * 2)


def split(x):
    high = x.astype(jnp.bfloat16)
    return high, (x - high.astype(jnp.float32)).astype(jnp.bfloat16)


def three_pass(a, b, dims):
    dot = functools.partial(lax.dot_general, dimension_numbers=dims, preferred_element_type=jnp.float32)
    return dot(a[0], b[0]) + (dot(a[0], b[1]) + dot(a[1], b[0]))


def params(mebibytes):
    return pltpu.CompilerParams(vmem_limit_bytes=mebibytes * 1024 * 1024)


def cost(flops, bytes_accessed):
    return pl.CostEstimate(flops=flops, bytes_accessed=bytes_accessed, transcendentals=0)


def whole(a):
    return pl.BlockSpec(a.shape, lambda *_: (0,) * a.ndim)


HBM = pl.BlockSpec(memory_space=pltpu.HBM)
SCALARS = pl.BlockSpec(memory_space=pltpu.SMEM)


def pack_kernel(distances, own, first, place_ref, block_ref, *refs):
    outs, (held, in_sems, out_sems) = refs[-len(distances) - 3 : -3], refs[-3:]
    rows = held.shape[2]
    arrivals, departures = [], []
    for j, k in enumerate(distances):
        row = pl.multiple_of((place_ref[1] ^ k) * own + first, GROUP)
        arrivals.append(pltpu.make_async_copy(block_ref.at[:, pl.ds(row, rows)], held.at[j], in_sems.at[j]))
        departures.append(pltpu.make_async_copy(held.at[j], outs[j], out_sems.at[j]))
        arrivals[j].start()
    for arrival, departure in zip(arrivals, departures):
        arrival.wait()
        departure.start()
    for departure in departures:
        departure.wait()


def pack(place, block, after, distances, own, first, rows):
    spectra, _, cells = block.shape
    count = len(distances)
    shape = (spectra, rows, cells)
    return pl.pallas_call(
        functools.partial(pack_kernel, distances, own, first),
        in_specs=[SCALARS, HBM] + [HBM] * len(after),
        out_specs=[HBM] * count,
        out_shape=[jax.ShapeDtypeStruct(shape, jnp.float32)] * count,
        scratch_shapes=[
            pltpu.VMEM((count, *shape), jnp.float32),
            pltpu.SemaphoreType.DMA((count,)),
            pltpu.SemaphoreType.DMA((count,)),
        ],
        compiler_params=params(48),
        cost_estimate=cost(0, 8 * count * spectra * rows * cells),
        name="pack",
    )(place, block, *after)


def near_kernel(block_cells, place_ref, cells_ref, *refs):
    parts, out_ref = refs[:-1], refs[-1]
    row = 0
    for part in parts:
        out_ref[pl.ds(row, part.shape[0]), :] = part[...]
        row += part.shape[0]
    home = cells_ref[...] // block_cells
    other = jnp.where(home == place_ref[0], -1, home).astype(jnp.float32)
    other = jnp.max(other, axis=1, keepdims=True)
    out_ref[pl.ds(block_cells, GROUP), :] = jnp.broadcast_to(other, (GROUP, out_ref.shape[1]))


def near_models(place, cell_index, parts, block_cells):
    return pl.pallas_call(
        functools.partial(near_kernel, block_cells),
        in_specs=[SCALARS] + [pl.BlockSpec(memory_space=pltpu.VMEM)] * (1 + len(parts)),
        out_specs=pl.BlockSpec(memory_space=pltpu.VMEM),
        out_shape=jax.ShapeDtypeStruct((block_cells + GROUP, parts[0].shape[1]), jnp.float32),
        compiler_params=params(16),
        cost_estimate=cost(0, 1 << 20),
        name="near_models",
    )(place, cell_index, *parts)


def tile_models_kernel(owned, partners, place_ref, cells_ref, *refs):
    tile_refs, (high_ref, low_ref) = refs[:-2], refs[-2:]
    block_cells = owned * len(partners)
    cells = cells_ref[...]
    distance = (cells // owned % len(partners)) ^ place_ref[1]
    slot = jnp.zeros_like(cells)
    for n, k in enumerate(partners):
        slot = jnp.where(distance == k, n, slot)
    spot = slot * owned + cells % owned
    away = (cells // block_cells) ^ place_ref[0]
    high, low = None, None
    for k, ref in enumerate(tile_refs):
        row = lax.broadcasted_iota(jnp.int32, (block_cells, cells.shape[1]), 0)
        pick = jnp.where((row == spot) & (away == k), 1.0, 0.0).astype(jnp.bfloat16)
        h, l = split(ref[pl.ds(0, block_cells), :].T)
        h = lax.dot_general(h, pick, NN, preferred_element_type=jnp.float32)
        l = lax.dot_general(l, pick, NN, preferred_element_type=jnp.float32)
        high, low = (h, l) if k == 0 else (high + h, low + l)
    high_ref[...] = high.astype(jnp.bfloat16)
    low_ref[...] = low.astype(jnp.bfloat16)


def tile_models(place, cell_index, tiles, owned, partners):
    shape = jax.ShapeDtypeStruct((tiles[0].shape[1], cell_index.shape[1]), jnp.bfloat16)
    return pl.pallas_call(
        functools.partial(tile_models_kernel, owned, partners),
        in_specs=[SCALARS] + [pl.BlockSpec(memory_space=pltpu.VMEM)] * (1 + len(tiles)),
        out_specs=[pl.BlockSpec(memory_space=pltpu.VMEM)] * 2,
        out_shape=[shape] * 2,
        compiler_params=params(16),
        cost_estimate=cost(1 << 30, 2 << 20),
        name="tile_models",
    )(place, cell_index, *tiles)


def wide_kernel(table_ref, high_ref, low_ref):
    fp, gates = table_ref.shape
    rows, columns = high_ref.shape
    iota = lax.broadcasted_iota
    down = (iota(jnp.int32, (rows, fp), 0) // GROUP == iota(jnp.int32, (rows, fp), 1)).astype(jnp.float32)
    across = iota(jnp.int32, (gates, columns), 1) // GROUP == iota(jnp.int32, (gates, columns), 0)
    across = across.astype(jnp.float32).astype(jnp.bfloat16)
    down = down.astype(jnp.bfloat16)
    same = iota(jnp.int32, (rows, columns), 0) % GROUP == iota(jnp.int32, (rows, columns), 1) % GROUP
    for part, ref in zip(split(table_ref[...]), (high_ref, low_ref)):
        tall = lax.dot_general(down, part, NN, preferred_element_type=jnp.float32).astype(jnp.bfloat16)
        full = lax.dot_general(tall, across, NN, preferred_element_type=jnp.float32)
        ref[...] = jnp.where(same, full, 0.0).astype(jnp.bfloat16)


def wide_table(table):
    shape = jax.ShapeDtypeStruct((table.shape[0] * GROUP, table.shape[1] * GROUP), jnp.bfloat16)
    return pl.pallas_call(
        wide_kernel,
        in_specs=[pl.BlockSpec(memory_space=pltpu.VMEM)],
        out_specs=[pl.BlockSpec(memory_space=pltpu.VMEM)] * 2,
        out_shape=[shape] * 2,
        compiler_params=params(16),
        cost_estimate=cost(1 << 28, 1 << 20),
        name="wide_table",
    )(table)


def chunk_kernel(pieces, block_cells, last, place_ref, *refs):
    sens_refs = refs[:pieces]
    model_h, model_l, gate_h, gate_l, obs_ref, cells_ref, terms_in, square_in, terms_ref, square_ref = refs[pieces:]

    @pl.when(pl.program_id(0) == 0)
    def _():
        terms_ref[...] = terms_in[...]
        square_ref[...] = square_in[...]

    sens = [split(r[...].reshape(r.shape[0] * r.shape[1], r.shape[2])) for r in sens_refs]
    sens = tuple(jnp.concatenate([s[i] for s in sens], axis=0) for i in range(2))
    gates = (gate_h[...], gate_l[...])
    predicted = three_pass((model_h[...], model_l[...]), sens, NT)
    misfit_rows = three_pass(split(predicted), gates, NN) - obs_ref[0]
    square_ref[...] += jnp.sum(misfit_rows * misfit_rows, axis=1, keepdims=True)
    back = three_pass(split(misfit_rows), gates, NT)
    terms = terms_ref[...] + three_pass(split(back), sens, NN)
    terms_ref[...] = terms

    if last:

        @pl.when(pl.program_id(0) == pl.num_programs(0) - 1)
        def _():
            cells = cells_ref[...]
            spot = cells % block_cells + jnp.where(cells // block_cells == place_ref[0], 0, block_cells)
            size = cells.shape[1]
            row = lax.broadcasted_iota(jnp.int32, (size, size), 0)
            pick = jnp.where(row == spot, 1.0, 0.0).astype(jnp.bfloat16)
            high = terms.astype(jnp.bfloat16)
            middle, low = split(terms - high.astype(jnp.float32))
            dot = functools.partial(lax.dot_general, dimension_numbers=NT, preferred_element_type=jnp.float32)
            terms_ref[...] = dot(high, pick) + (dot(middle, pick) + dot(low, pick))


def chunk_step(place, block, sens, first, models_t, gates, obs, cell_index, terms, square, block_cells, last):
    spectra, soundings, cells = block.shape
    rows = sens[0].shape[1]
    pieces = len(sens) + 1
    members = terms.shape[0]
    own_groups = soundings // (pieces * GROUP)
    return pl.pallas_call(
        functools.partial(chunk_kernel, pieces, block_cells, last),
        grid_spec=pltpu.PrefetchScalarGridSpec(
            num_scalar_prefetch=1,
            grid=(rows // GROUP,),
            in_specs=[
                pl.BlockSpec((spectra, GROUP, cells), lambda i, place: (0, place[1] * own_groups + first + i, 0))
            ]
            + [pl.BlockSpec((spectra, GROUP, cells), lambda i, place: (0, i, 0))] * len(sens)
            + [whole(a) for a in (*models_t, *gates)]
            + [pl.BlockSpec((1, 1, obs.shape[2]), lambda i, place: (first + i, 0, 0)), whole(cell_index)]
            + [whole(terms), whole(square)],
            out_specs=[whole(terms), whole(square)],
        ),
        out_shape=[
            jax.ShapeDtypeStruct(terms.shape, jnp.float32),
            jax.ShapeDtypeStruct(square.shape, jnp.float32),
        ],
        input_output_aliases={pieces + 7: 0, pieces + 8: 1},
        compiler_params=params(40),
        cost_estimate=cost(
            12 * pieces * spectra * rows * cells * members * 2, 4 * pieces * spectra * rows * cells
        ),
        name="chunk_step",
    )(place, block, *sens, *models_t, *gates, obs, cell_index, terms, square)


def exact_dot(a, b, dims):
    return lax.dot_general(a, b, dims, precision=HIGH, preferred_element_type=jnp.float32)


def gradient_kernel(tiles, owned, place_ref, borrowed_ref, got_ref, square_ref, out_ref):
    devices, slab, cells = got_ref.shape
    owners = devices // tiles
    block_cells = owned * owners
    members = square_ref.shape[0]
    sums = []
    for t in range(tiles):
        total = got_ref[t * owners]
        for f in range(1, owners):
            total = total + got_ref[t * owners + f]
        sums.append(total)
    gradient = []
    for b in range(tiles):
        block = sums[b][:, :block_cells]
        for t in range(tiles):
            block = block + jnp.where(borrowed_ref[place_ref[0] ^ t] == b, sums[t][:, block_cells:], 0.0)
        gradient.append(block)
    square = sum(jnp.sum(g * g, axis=1, keepdims=True) for g in gradient)
    scale = jnp.sqrt(square / (tiles * block_cells) + EPSILON)
    iota = lax.broadcasted_iota
    per_row = members // slab
    down = (iota(jnp.int32, (slab, members), 1) // per_row == iota(jnp.int32, (slab, members), 0))
    lane = iota(jnp.int32, (members, LANES), 1)
    spread = jnp.where(iota(jnp.int32, (members, LANES), 0) % per_row + owned == lane, square_ref[...], 0.0)
    rider = exact_dot(down.astype(jnp.float32), spread, NN)
    for b in range(tiles):
        step = gradient[b] / scale
        for f in range(owners):
            piece = step[:, f * owned : (f + 1) * owned]
            piece = jnp.concatenate([piece, jnp.zeros((slab, LANES - owned), jnp.float32)], axis=1)
            out_ref[b * owners + f] = piece + rider


def gradient_step(place, borrowed, got, square, tiles, owned):
    devices, slab, _ = got.shape
    return pl.pallas_call(
        functools.partial(gradient_kernel, tiles, owned),
        in_specs=[SCALARS] * 2 + [pl.BlockSpec(memory_space=pltpu.VMEM)] * 2,
        out_specs=pl.BlockSpec(memory_space=pltpu.VMEM),
        out_shape=jax.ShapeDtypeStruct((devices, slab, LANES), jnp.float32),
        compiler_params=params(16),
        cost_estimate=cost(1 << 22, 1 << 20),
        name="gradient_step",
    )(place, borrowed, got, square)


def update_kernel(divisor, models_ref, back_ref, updated_ref, misfit_ref):
    devices, slab, _ = back_ref.shape
    owned, members = models_ref.shape
    per_row = members // slab
    iota = lax.broadcasted_iota
    riders = back_ref[0]
    for d in range(1, devices):
        riders = riders + back_ref[d]
    down = (iota(jnp.int32, (slab, members), 1) // per_row == iota(jnp.int32, (slab, members), 0))
    tall = exact_dot(riders, down.astype(jnp.float32), (((0,), (0,)), ((), ())))
    mine = iota(jnp.int32, (LANES, members), 1) % per_row + owned == iota(jnp.int32, (LANES, members), 0)
    misfit = jnp.sum(jnp.where(mine, tall, 0.0), axis=0, keepdims=True) / divisor
    step = back_ref[...].reshape(members, LANES).T[:owned]
    updated_ref[...] = models_ref[...] - STEP_LENGTH * misfit * step
    misfit_ref[...] = misfit


def update(models, back, divisor):
    return pl.pallas_call(
        functools.partial(update_kernel, divisor),
        in_specs=[pl.BlockSpec(memory_space=pltpu.VMEM)] * 2,
        out_specs=[pl.BlockSpec(memory_space=pltpu.VMEM)] * 2,
        out_shape=[
            jax.ShapeDtypeStruct(models.shape, jnp.float32),
            jax.ShapeDtypeStruct((1, models.shape[1]), jnp.float32),
        ],
        compiler_params=params(16),
        cost_estimate=cost(1 << 20, 1 << 18),
        name="update",
    )(models, back)


def chunk_groups(groups):
    if groups < 16:
        return [1] * groups
    first, last = groups // 8, [groups * 3 // 16, groups // 16]
    rest = groups - first - sum(last)
    return [first, rest - rest // 2, rest // 2] + last


def body(sensitivity, models, observed, waveform, cell_index, gate_index):
    both = ("tile", "freq")
    tiles, owners, devices = lax.axis_size("tile"), lax.axis_size("freq"), lax.axis_size(both)
    _, own_freqs, parts, soundings, cells = sensitivity.shape
    freqs = own_freqs * owners
    spectra = own_freqs * parts
    owned, members = models.shape
    ncells = owned * devices
    gates = gate_index.shape[0]
    divisor = 2.0 * tiles * soundings * gates
    own = soundings // owners
    block_cells = owned * owners
    place = jnp.stack([lax.axis_index("tile"), lax.axis_index("freq")])

    block = sensitivity[0].reshape(spectra, soundings, cells)
    sizes = chunk_groups(own // GROUP)
    starts = [sum(sizes[:i]) for i in range(len(sizes))]
    distances = partner_order(owners)
    partners = [0] + distances
    half = owners // 2
    pair = jnp.concatenate([models, swap(models, "freq", half)])
    parts_near = [pair] + [swap(pair, "freq", k) for k in range(1, half)]
    slots = [k ^ j for k in range(half) for j in (0, half)]
    received = []
    for i, (start, size) in enumerate(zip(starts, sizes)):
        after = received[i - 1][:1] if i else []
        pieces = pack(place, block, after, distances, own, start * GROUP, size * GROUP)
        received.append([swap(p, "freq", k) for p, k in zip(pieces, distances)])

    near = near_models(place, cell_index, parts_near, block_cells)
    blocks = [near] + [swap(near, "tile", k) for k in range(1, tiles)]
    borrowed = jnp.stack([b[block_cells, 0] for b in blocks]).astype(jnp.int32)
    models_t = tile_models(place, cell_index, blocks, owned, slots)

    order = place[1] ^ jnp.array(partners, jnp.int32)
    wide = wide_table(gate_table(order, own_freqs, freqs, waveform, gate_index).T)
    obs = observed[0].reshape(gates, own // GROUP, GROUP)
    obs = jnp.swapaxes(obs, 0, 1).reshape(own // GROUP, 1, gates * GROUP)

    terms = jnp.zeros((members, cells), jnp.float32)
    square = jnp.zeros((members, LANES), jnp.float32)
    for i, start in enumerate(starts):
        last = i == len(starts) - 1
        terms, square = chunk_step(
            place, block, received[i], start, models_t, wide, obs, cell_index, terms, square, block_cells, last
        )

    slab = members // devices
    sent = terms.reshape(devices, slab, cells)
    got = lax.all_to_all(sent, both, split_axis=0, concat_axis=0, tiled=True)
    if slab % GROUP == 0 and members // slab + owned <= LANES:
        step = gradient_step(place, borrowed, got, square, tiles, owned)
        back = lax.all_to_all(step, both, split_axis=0, concat_axis=0, tiled=True)
        updated, misfit = update(models, back, divisor)
        return (updated, misfit.reshape(members))

    got = jnp.sum(got.reshape(tiles, owners, slab, cells), axis=1)
    tile_ids = jnp.arange(tiles)
    lent = (jnp.take(borrowed, tile_ids ^ place[0])[None, :] == tile_ids[:, None]).astype(jnp.float32)
    gradient = got[:, :, :block_cells] + jnp.sum(
        lent[:, :, None, None] * got[None, :, :, block_cells:], axis=1
    )
    scale = jnp.sqrt(jnp.sum(gradient * gradient, axis=(0, 2)) / ncells + EPSILON)
    step = gradient / scale[None, :, None]
    step = step.reshape(tiles, slab, owners, owned).transpose(0, 2, 1, 3)
    step = step.reshape(devices, slab, owned)
    rider = jnp.broadcast_to(square[:, 0].reshape(1, slab, devices), (devices, slab, devices))
    back = lax.all_to_all(
        jnp.concatenate([step, rider], axis=2), both, split_axis=0, concat_axis=0, tiled=True
    )
    misfit = jnp.sum(back[:, :, owned:], axis=0).reshape(members) / divisor
    back = back[:, :, :owned].reshape(members, owned)
    return (models - (STEP_LENGTH * misfit)[None, :] * back.T, misfit)


def solution(mesh):
    in_specs = (
        P("tile", "freq", None, None, None),
        P(("tile", "freq"), None),
        P("tile", None, "freq"),
        P(),
        P("tile", None),
        P(),
    )
    out_specs = (P(("tile", "freq"), None), P())
    return jax.shard_map(body, mesh=mesh, in_specs=in_specs, out_specs=out_specs, check_vma=False)
```

```python
import functools
import math

import jax
import jax.numpy as jnp
from jax import lax
from jax.experimental import pallas as pl
from jax.experimental.pallas import tpu as pltpu
from jax.sharding import PartitionSpec as P

HIGH = lax.Precision.HIGHEST
PHASE_RATE = 0.37
STEP_LENGTH = 0.5
EPSILON = 1e-06
GROUP = 8
LANES = 128

NN = (((1,), (0,)), ((), ()))
NT = (((1,), (1,)), ((), ()))


def gate_table(owner_order, own_freqs, freqs, waveform, gate_index):
    samples = waveform.shape[0]
    freq_ids = (owner_order[:, None] * own_freqs + jnp.arange(own_freqs)[None, :]).reshape(freqs)
    freq_col = freq_ids.astype(jnp.float32)[:, None] + 0.5
    time_row = jnp.arange(samples, dtype=jnp.float32)[None, :] + 0.5
    phases = PHASE_RATE * freq_col * time_row
    kernel = jnp.stack([jnp.cos(phases), jnp.sin(phases)], axis=1) / math.sqrt(freqs)
    steps = jnp.arange(samples)
    lag = gate_index[:, None] - steps[None, :]
    picked = jnp.sum(
        jnp.where(lag[:, :, None] == steps[None, None, :], waveform[None, None, :], 0.0), axis=-1
    )
    return jnp.einsum("gk,fpk->gfp", picked, kernel, precision=HIGH).reshape(gate_index.shape[0], freqs * 2)


def split(x):
    high = x.astype(jnp.bfloat16)
    return high, (x - high.astype(jnp.float32)).astype(jnp.bfloat16)


def three_pass(a, b, dims):
    dot = functools.partial(lax.dot_general, dimension_numbers=dims, preferred_element_type=jnp.float32)
    return dot(a[0], b[0]) + (dot(a[0], b[1]) + dot(a[1], b[0]))


def params(mebibytes):
    return pltpu.CompilerParams(vmem_limit_bytes=mebibytes * 1024 * 1024)


def cost(flops, bytes_accessed):
    return pl.CostEstimate(flops=flops, bytes_accessed=bytes_accessed, transcendentals=0)


def whole(a):
    return pl.BlockSpec(a.shape, lambda *_: (0,) * a.ndim)


HBM = pl.BlockSpec(memory_space=pltpu.HBM)
SCALARS = pl.BlockSpec(memory_space=pltpu.SMEM)


def pack_kernel(owners_of, own, first, rows, lanes, joined, place_ref, block_ref, models_ref, *refs):
    held, in_sems, out_sems = refs[-3:]
    count = held.shape[0]
    outs = [refs[-4].at[j] for j in range(count)] if joined else refs[-3 - count : -3]
    spectra = block_ref.shape[0]
    owned, members = models_ref.shape
    arrivals, departures = [], []
    for j in range(count):
        row = pl.multiple_of(owners_of(place_ref[1], j) * own + first, GROUP)
        source, target = block_ref.at[:, pl.ds(row, rows)], held.at[j, pl.ds(0, spectra)]
        arrivals.append(pltpu.make_async_copy(source, target, in_sems.at[j]))
        departures.append(pltpu.make_async_copy(held.at[j], outs[j], out_sems.at[j]))
        arrivals[j].start()
    for j in range(count):
        for lane in range(lanes):
            part = owned // lanes
            held[j, spectra, pl.ds(0, part), pl.ds(lane * members, members)] = models_ref[pl.ds(lane * part, part), :]
    for arrival, departure in zip(arrivals, departures):
        arrival.wait()
        departure.start()
    for departure in departures:
        departure.wait()


def pack(place, block, models, after, count, owners_of, own, first, rows, lanes, joined):
    spectra, _, cells = block.shape
    shape = (spectra + (lanes > 0), rows, cells)
    if joined:
        out_shape = [jax.ShapeDtypeStruct((count, *shape), jnp.float32)]
    else:
        out_shape = [jax.ShapeDtypeStruct(shape, jnp.float32)] * count
    return pl.pallas_call(
        functools.partial(pack_kernel, owners_of, own, first, rows, lanes, joined),
        in_specs=[SCALARS, HBM, pl.BlockSpec(memory_space=pltpu.VMEM)] + [HBM] * len(after),
        out_specs=[HBM] * len(out_shape),
        out_shape=out_shape,
        scratch_shapes=[
            pltpu.VMEM((count, *shape), jnp.float32),
            pltpu.SemaphoreType.DMA((count,)),
            pltpu.SemaphoreType.DMA((count,)),
        ],
        compiler_params=params(48),
        cost_estimate=cost(0, 8 * count * spectra * rows * cells),
        name="pack_near" if joined else "pack_across",
    )(place, block, models, *after)


def block_kernel(block_cells, owned, lanes, place_ref, cells_ref, near_ref, *refs):
    riders, out_ref = refs[:-1], refs[-1]
    members = out_ref.shape[1]
    part = owned // lanes
    sources = [near_ref.at[r, 0] for r in range(near_ref.shape[0])] + [r.at[0] for r in riders]
    for n, source in enumerate(sources):
        for lane in range(lanes):
            out_ref[pl.ds(n * owned + lane * part, part), :] = source[pl.ds(0, part), pl.ds(lane * members, members)]
    home = cells_ref[...] // block_cells
    other = jnp.where(home == place_ref[0], -1, home).astype(jnp.float32)
    other = jnp.max(other, axis=1, keepdims=True)
    out_ref[pl.ds(block_cells, GROUP), :] = jnp.broadcast_to(other, (GROUP, members))


def block_models(place, cell_index, near, across, block_cells, owned, members, lanes):
    count, slabs, near_rows, cells = near.shape
    rows = across[0].shape[1]
    out = jax.ShapeDtypeStruct((block_cells + GROUP, members), jnp.float32)
    return pl.pallas_call(
        functools.partial(block_kernel, block_cells, owned, lanes),
        grid=(1,),
        in_specs=[SCALARS, whole(cell_index), pl.BlockSpec((count, 1, rows, cells), lambda i: (0, slabs - 1, 0, 0))]
        + [pl.BlockSpec((1, rows, cells), lambda i: (slabs - 1, 0, 0))] * len(across),
        out_specs=whole(out),
        out_shape=out,
        compiler_params=params(16),
        cost_estimate=cost(0, 1 << 20),
        name="block_models",
    )(place, cell_index, near, *across)


def tile_models_kernel(owned, across, place_ref, cells_ref, *refs):
    tile_refs, (high_ref, low_ref) = refs[:-2], refs[-2:]
    half = len(across)
    block_cells = owned * 2 * half
    cells = cells_ref[...]
    owner = cells // owned % (2 * half)
    slot = owner % half
    for n, k in enumerate(across):
        slot = jnp.where(owner ^ place_ref[1] == k, half + n, slot)
    spot = slot * owned + cells % owned
    away = (cells // block_cells) ^ place_ref[0]
    high, low = None, None
    for k, ref in enumerate(tile_refs):
        row = lax.broadcasted_iota(jnp.int32, (block_cells, cells.shape[1]), 0)
        pick = jnp.where((row == spot) & (away == k), 1.0, 0.0).astype(jnp.bfloat16)
        h, l = split(ref[pl.ds(0, block_cells), :].T)
        h = lax.dot_general(h, pick, NN, preferred_element_type=jnp.float32)
        l = lax.dot_general(l, pick, NN, preferred_element_type=jnp.float32)
        high, low = (h, l) if k == 0 else (high + h, low + l)
    high_ref[...] = high.astype(jnp.bfloat16)
    low_ref[...] = low.astype(jnp.bfloat16)


def tile_models(place, cell_index, tiles, owned, across):
    shape = jax.ShapeDtypeStruct((tiles[0].shape[1], cell_index.shape[1]), jnp.bfloat16)
    return pl.pallas_call(
        functools.partial(tile_models_kernel, owned, across),
        in_specs=[SCALARS] + [pl.BlockSpec(memory_space=pltpu.VMEM)] * (1 + len(tiles)),
        out_specs=[pl.BlockSpec(memory_space=pltpu.VMEM)] * 2,
        out_shape=[shape] * 2,
        compiler_params=params(16),
        cost_estimate=cost(1 << 30, 2 << 20),
        name="tile_models",
    )(place, cell_index, *tiles)


def wide_kernel(table_ref, high_ref, low_ref):
    fp, gates = table_ref.shape
    rows, columns = high_ref.shape
    iota = lax.broadcasted_iota
    down = (iota(jnp.int32, (rows, fp), 0) // GROUP == iota(jnp.int32, (rows, fp), 1)).astype(jnp.float32)
    across = iota(jnp.int32, (gates, columns), 1) // GROUP == iota(jnp.int32, (gates, columns), 0)
    across = across.astype(jnp.float32).astype(jnp.bfloat16)
    down = down.astype(jnp.bfloat16)
    same = iota(jnp.int32, (rows, columns), 0) % GROUP == iota(jnp.int32, (rows, columns), 1) % GROUP
    for part, ref in zip(split(table_ref[...]), (high_ref, low_ref)):
        tall = lax.dot_general(down, part, NN, preferred_element_type=jnp.float32).astype(jnp.bfloat16)
        full = lax.dot_general(tall, across, NN, preferred_element_type=jnp.float32)
        ref[...] = jnp.where(same, full, 0.0).astype(jnp.bfloat16)


def wide_table(table):
    shape = jax.ShapeDtypeStruct((table.shape[0] * GROUP, table.shape[1] * GROUP), jnp.bfloat16)
    return pl.pallas_call(
        wide_kernel,
        in_specs=[pl.BlockSpec(memory_space=pltpu.VMEM)],
        out_specs=[pl.BlockSpec(memory_space=pltpu.VMEM)] * 2,
        out_shape=[shape] * 2,
        compiler_params=params(16),
        cost_estimate=cost(1 << 28, 1 << 20),
        name="wide_table",
    )(table)


def chunk_kernel(pieces, block_cells, last, place_ref, *refs):
    sens_refs = refs[:pieces]
    model_h, model_l, gate_h, gate_l, obs_ref, cells_ref, terms_in, square_in, terms_ref, square_ref = refs[pieces:]

    @pl.when(pl.program_id(0) == 0)
    def _():
        terms_ref[...] = terms_in[...]
        square_ref[...] = square_in[...]

    sens = [split(r[...].reshape(-1, r.shape[-1])) for r in sens_refs]
    sens = tuple(jnp.concatenate([s[i] for s in sens], axis=0) for i in range(2))
    gates = (gate_h[...], gate_l[...])
    predicted = three_pass((model_h[...], model_l[...]), sens, NT)
    misfit_rows = three_pass(split(predicted), gates, NN) - obs_ref[0]
    square_ref[...] += jnp.sum(misfit_rows * misfit_rows, axis=1, keepdims=True)
    back = three_pass(split(misfit_rows), gates, NT)
    terms = terms_ref[...] + three_pass(split(back), sens, NN)
    terms_ref[...] = terms

    if last:

        @pl.when(pl.program_id(0) == pl.num_programs(0) - 1)
        def _():
            cells = cells_ref[...]
            spot = cells % block_cells + jnp.where(cells // block_cells == place_ref[0], 0, block_cells)
            size = cells.shape[1]
            row = lax.broadcasted_iota(jnp.int32, (size, size), 0)
            pick = jnp.where(row == spot, 1.0, 0.0).astype(jnp.bfloat16)
            high = terms.astype(jnp.bfloat16)
            middle, low = split(terms - high.astype(jnp.float32))
            dot = functools.partial(lax.dot_general, dimension_numbers=NT, preferred_element_type=jnp.float32)
            terms_ref[...] = dot(high, pick) + (dot(middle, pick) + dot(low, pick))


def chunk_step(place, near, near_first, across, first, models_t, gates, obs, cell_index, terms, square, block_cells, last):
    half, rows, cells = near.shape[0], across[0].shape[1], across[0].shape[2]
    members = terms.shape[0]
    spectra = gates[0].shape[0] // (2 * half * GROUP)
    pieces = 1 + len(across)
    work = 2 * half * spectra * rows * cells
    return pl.pallas_call(
        functools.partial(chunk_kernel, pieces, block_cells, last),
        grid=(rows // GROUP,),
        in_specs=[SCALARS]
        + [pl.BlockSpec((half, spectra, GROUP, cells), lambda i: (0, 0, near_first + i, 0))]
        + [pl.BlockSpec((spectra, GROUP, cells), lambda i: (0, i, 0))] * len(across)
        + [whole(a) for a in (*models_t, *gates)]
        + [pl.BlockSpec((1, 1, obs.shape[2]), lambda i: (first + i, 0, 0)), whole(cell_index)]
        + [whole(terms), whole(square)],
        out_specs=[whole(terms), whole(square)],
        out_shape=[
            jax.ShapeDtypeStruct(terms.shape, jnp.float32),
            jax.ShapeDtypeStruct(square.shape, jnp.float32),
        ],
        input_output_aliases={pieces + 7: 0, pieces + 8: 1},
        compiler_params=params(40),
        cost_estimate=cost(12 * work * members * 2, 4 * work),
        name="chunk_step",
    )(place, near, *across, *models_t, *gates, obs, cell_index, terms, square)


def exact_dot(a, b, dims):
    return lax.dot_general(a, b, dims, precision=HIGH, preferred_element_type=jnp.float32)


def gradient_kernel(tiles, owned, place_ref, borrowed_ref, got_ref, square_ref, out_ref):
    devices, slab, cells = got_ref.shape
    owners = devices // tiles
    block_cells = owned * owners
    members = square_ref.shape[0]
    sums = []
    for t in range(tiles):
        total = got_ref[t * owners]
        for f in range(1, owners):
            total = total + got_ref[t * owners + f]
        sums.append(total)
    gradient = []
    for b in range(tiles):
        block = sums[b][:, :block_cells]
        for t in range(tiles):
            block = block + jnp.where(borrowed_ref[place_ref[0] ^ t] == b, sums[t][:, block_cells:], 0.0)
        gradient.append(block)
    square = sum(jnp.sum(g * g, axis=1, keepdims=True) for g in gradient)
    scale = jnp.sqrt(square / (tiles * block_cells) + EPSILON)
    iota = lax.broadcasted_iota
    per_row = members // slab
    down = (iota(jnp.int32, (slab, members), 1) // per_row == iota(jnp.int32, (slab, members), 0))
    lane = iota(jnp.int32, (members, LANES), 1)
    spread = jnp.where(iota(jnp.int32, (members, LANES), 0) % per_row + owned == lane, square_ref[...], 0.0)
    rider = exact_dot(down.astype(jnp.float32), spread, NN)
    for b in range(tiles):
        step = gradient[b] / scale
        for f in range(owners):
            piece = step[:, f * owned : (f + 1) * owned]
            piece = jnp.concatenate([piece, jnp.zeros((slab, LANES - owned), jnp.float32)], axis=1)
            out_ref[b * owners + f] = piece + rider


def gradient_step(place, borrowed, got, square, tiles, owned):
    devices, slab, _ = got.shape
    return pl.pallas_call(
        functools.partial(gradient_kernel, tiles, owned),
        in_specs=[SCALARS] * 2 + [pl.BlockSpec(memory_space=pltpu.VMEM)] * 2,
        out_specs=pl.BlockSpec(memory_space=pltpu.VMEM),
        out_shape=jax.ShapeDtypeStruct((devices, slab, LANES), jnp.float32),
        compiler_params=params(16),
        cost_estimate=cost(1 << 22, 1 << 20),
        name="gradient_step",
    )(place, borrowed, got, square)


def update_kernel(divisor, models_ref, back_ref, updated_ref, misfit_ref):
    devices, slab, _ = back_ref.shape
    owned, members = models_ref.shape
    per_row = members // slab
    iota = lax.broadcasted_iota
    riders = back_ref[0]
    for d in range(1, devices):
        riders = riders + back_ref[d]
    down = (iota(jnp.int32, (slab, members), 1) // per_row == iota(jnp.int32, (slab, members), 0))
    tall = exact_dot(riders, down.astype(jnp.float32), (((0,), (0,)), ((), ())))
    mine = iota(jnp.int32, (LANES, members), 1) % per_row + owned == iota(jnp.int32, (LANES, members), 0)
    misfit = jnp.sum(jnp.where(mine, tall, 0.0), axis=0, keepdims=True) / divisor
    step = back_ref[...].reshape(members, LANES).T[:owned]
    updated_ref[...] = models_ref[...] - STEP_LENGTH * misfit * step
    misfit_ref[...] = misfit


def update(models, back, divisor):
    return pl.pallas_call(
        functools.partial(update_kernel, divisor),
        in_specs=[pl.BlockSpec(memory_space=pltpu.VMEM)] * 2,
        out_specs=[pl.BlockSpec(memory_space=pltpu.VMEM)] * 2,
        out_shape=[
            jax.ShapeDtypeStruct(models.shape, jnp.float32),
            jax.ShapeDtypeStruct((1, models.shape[1]), jnp.float32),
        ],
        compiler_params=params(16),
        cost_estimate=cost(1 << 20, 1 << 18),
        name="update",
    )(models, back)


def chunk_groups(groups):
    if groups < 16:
        return [1] * groups
    ends = [groups // 8, groups * 3 // 16, groups // 8, groups // 16]
    rest = groups - sum(ends)
    return [ends[0], rest - rest // 2, rest // 2] + ends[1:]


def body(sensitivity, models, observed, waveform, cell_index, gate_index):
    both = ("tile", "freq")
    tiles, owners, devices = lax.axis_size("tile"), lax.axis_size("freq"), lax.axis_size(both)
    _, own_freqs, parts, soundings, cells = sensitivity.shape
    freqs = own_freqs * owners
    spectra = own_freqs * parts
    owned, members = models.shape
    ncells = owned * devices
    gates = gate_index.shape[0]
    divisor = 2.0 * tiles * soundings * gates
    own = soundings // owners
    block_cells = owned * owners
    place = jnp.stack([lax.axis_index("tile"), lax.axis_index("freq")])

    block = sensitivity[0].reshape(spectra, soundings, cells)
    half = owners // 2
    lanes = cells // members if owned % (GROUP * (cells // members)) == 0 else 1
    sizes = chunk_groups(own // GROUP)
    starts = [sum(sizes[:i]) for i in range(len(sizes))]
    across_by = list(range(half, owners))[::-1]
    in_halves = [[h * half + r for r in range(half)] for h in range(2)]

    def send_across(i, after):
        pieces = pack(
            place, block, models, after, half, lambda f, j: f ^ across_by[j],
            own, starts[i] * GROUP, sizes[i] * GROUP, lanes if i == 0 else 0, False,
        )
        return [
            lax.ppermute(p, "freq", [(f, f ^ k) for f in range(owners)]) for p, k in zip(pieces, across_by)
        ]

    def send_near(first, groups, after, lanes):
        [pieces] = pack(
            place, block, models, after, half, lambda f, j: f // half * half + j,
            own, first * GROUP, groups * GROUP, lanes, True,
        )
        return lax.all_to_all(
            pieces, "freq", split_axis=0, concat_axis=0, axis_index_groups=in_halves, tiled=True
        )

    split_at = starts[2]
    across = [send_across(0, [])]
    near = [send_near(0, split_at, [], lanes)]
    across.append(send_across(1, across[0][:1]))
    near.append(send_near(split_at, own // GROUP - split_at, across[0][-1:], 0))

    mine = block_models(place, cell_index, near[0], across[0], block_cells, owned, members, lanes)
    blocks = [mine] + [
        lax.ppermute(mine, "tile", [(t, t ^ k) for t in range(tiles)]) for k in range(1, tiles)
    ]
    borrowed = jnp.stack([b[block_cells, 0] for b in blocks]).astype(jnp.int32)
    models_t = tile_models(place, cell_index, blocks, owned, across_by)

    order = jnp.concatenate([place[1] // half * half + jnp.arange(half), place[1] ^ jnp.array(across_by)])
    wide = wide_table(gate_table(order, own_freqs, freqs, waveform, gate_index).T)
    obs = observed[0].reshape(gates, own // GROUP, GROUP)
    obs = jnp.swapaxes(obs, 0, 1).reshape(own // GROUP, 1, gates * GROUP)

    terms = jnp.zeros((members, cells), jnp.float32)
    square = jnp.zeros((members, LANES), jnp.float32)
    done = []
    for i, start in enumerate(starts):
        if i >= 2:
            across.append(send_across(i, across[i - 1][:1] + done[: i - 2][-1:]))
        part, offset = (near[0], start) if start < split_at else (near[1], start - split_at)
        terms, square = chunk_step(
            place, part, offset, across[i], start, models_t, wide, obs, cell_index, terms, square, block_cells,
            i == len(starts) - 1,
        )
        done.append(square)

    slab = members // devices
    sent = terms.reshape(devices, slab, cells)
    got = lax.all_to_all(sent, both, split_axis=0, concat_axis=0, tiled=True)
    if slab % GROUP == 0 and members // slab + owned <= LANES:
        step = gradient_step(place, borrowed, got, square, tiles, owned)
        back = lax.all_to_all(step, both, split_axis=0, concat_axis=0, tiled=True)
        updated, misfit = update(models, back, divisor)
        return (updated, misfit.reshape(members))

    got = jnp.sum(got.reshape(tiles, owners, slab, cells), axis=1)
    tile_ids = jnp.arange(tiles)
    lent = (jnp.take(borrowed, tile_ids ^ place[0])[None, :] == tile_ids[:, None]).astype(jnp.float32)
    gradient = got[:, :, :block_cells] + jnp.sum(
        lent[:, :, None, None] * got[None, :, :, block_cells:], axis=1
    )
    scale = jnp.sqrt(jnp.sum(gradient * gradient, axis=(0, 2)) / ncells + EPSILON)
    step = gradient / scale[None, :, None]
    step = step.reshape(tiles, slab, owners, owned).transpose(0, 2, 1, 3)
    step = step.reshape(devices, slab, owned)
    rider = jnp.broadcast_to(square[:, 0].reshape(1, slab, devices), (devices, slab, devices))
    back = lax.all_to_all(
        jnp.concatenate([step, rider], axis=2), both, split_axis=0, concat_axis=0, tiled=True
    )
    misfit = jnp.sum(back[:, :, owned:], axis=0).reshape(members) / divisor
    back = back[:, :, :owned].reshape(members, owned)
    return (models - (STEP_LENGTH * misfit)[None, :] * back.T, misfit)


def solution(mesh):
    in_specs = (
        P("tile", "freq", None, None, None),
        P(("tile", "freq"), None),
        P("tile", None, "freq"),
        P(),
        P("tile", None),
        P(),
    )
    out_specs = (P(("tile", "freq"), None), P())
    return jax.shard_map(body, mesh=mesh, in_specs=in_specs, out_specs=out_specs, check_vma=False)
```

```python
import functools
import math

import jax
import jax.numpy as jnp
from jax import lax
from jax.experimental import pallas as pl
from jax.experimental.pallas import tpu as pltpu
from jax.sharding import PartitionSpec as P

HIGH = lax.Precision.HIGHEST
PHASE_RATE = 0.37
STEP_LENGTH = 0.5
EPSILON = 1e-06
GROUP = 8
LANES = 128

NN = (((1,), (0,)), ((), ()))
NT = (((1,), (1,)), ((), ()))


def swap(x, axis, k):
    return lax.ppermute(x, axis, [(i, i ^ k) for i in range(lax.axis_size(axis))])


def partner_order(size):
    assert size & (size - 1) == 0
    return list(range(1, size))[::-1]


def gate_table(owner_order, own_freqs, freqs, waveform, gate_index):
    samples = waveform.shape[0]
    freq_ids = (owner_order[:, None] * own_freqs + jnp.arange(own_freqs)[None, :]).reshape(freqs)
    freq_col = freq_ids.astype(jnp.float32)[:, None] + 0.5
    time_row = jnp.arange(samples, dtype=jnp.float32)[None, :] + 0.5
    phases = PHASE_RATE * freq_col * time_row
    kernel = jnp.stack([jnp.cos(phases), jnp.sin(phases)], axis=1) / math.sqrt(freqs)
    steps = jnp.arange(samples)
    lag = gate_index[:, None] - steps[None, :]
    picked = jnp.sum(
        jnp.where(lag[:, :, None] == steps[None, None, :], waveform[None, None, :], 0.0), axis=-1
    )
    return jnp.einsum("gk,fpk->gfp", picked, kernel, precision=HIGH).reshape(gate_index.shape[0], freqs * 2)


def split(x):
    high = x.astype(jnp.bfloat16)
    return high, (x - high.astype(jnp.float32)).astype(jnp.bfloat16)


def three_pass(a, b, dims):
    dot = functools.partial(lax.dot_general, dimension_numbers=dims, preferred_element_type=jnp.float32)
    return dot(a[0], b[0]) + (dot(a[0], b[1]) + dot(a[1], b[0]))


def params(mebibytes):
    return pltpu.CompilerParams(vmem_limit_bytes=mebibytes * 1024 * 1024)


def cost(flops, bytes_accessed):
    return pl.CostEstimate(flops=flops, bytes_accessed=bytes_accessed, transcendentals=0)


def whole(a):
    return pl.BlockSpec(a.shape, lambda *_: (0,) * a.ndim)


HBM = pl.BlockSpec(memory_space=pltpu.HBM)
SCALARS = pl.BlockSpec(memory_space=pltpu.SMEM)


def pack_kernel(distances, own, first, rows, lanes, place_ref, block_ref, models_ref, *refs):
    outs, (held, in_sems, out_sems) = refs[-len(distances) - 3 : -3], refs[-3:]
    spectra = block_ref.shape[0]
    owned, members = models_ref.shape
    arrivals, departures = [], []
    for j, k in enumerate(distances):
        row = pl.multiple_of((place_ref[1] ^ k) * own + first, GROUP)
        source, target = block_ref.at[:, pl.ds(row, rows)], held.at[j, pl.ds(0, spectra)]
        arrivals.append(pltpu.make_async_copy(source, target, in_sems.at[j]))
        departures.append(pltpu.make_async_copy(held.at[j], outs[j], out_sems.at[j]))
        arrivals[j].start()
    for j in range(len(distances)):
        for lane in range(lanes):
            part = owned // lanes
            held[j, spectra, pl.ds(0, part), pl.ds(lane * members, members)] = models_ref[pl.ds(lane * part, part), :]
    for arrival, departure in zip(arrivals, departures):
        arrival.wait()
        departure.start()
    for departure in departures:
        departure.wait()


def pack(place, block, models, after, distances, own, first, rows, lanes):
    spectra, _, cells = block.shape
    count = len(distances)
    shape = (spectra + (lanes > 0), rows, cells)
    return pl.pallas_call(
        functools.partial(pack_kernel, distances, own, first, rows, lanes),
        in_specs=[SCALARS, HBM, pl.BlockSpec(memory_space=pltpu.VMEM)] + [HBM] * len(after),
        out_specs=[HBM] * count,
        out_shape=[jax.ShapeDtypeStruct(shape, jnp.float32)] * count,
        scratch_shapes=[
            pltpu.VMEM((count, *shape), jnp.float32),
            pltpu.SemaphoreType.DMA((count,)),
            pltpu.SemaphoreType.DMA((count,)),
        ],
        compiler_params=params(48),
        cost_estimate=cost(0, 8 * count * spectra * rows * cells),
        name="pack",
    )(place, block, models, *after)


def near_kernel(lanes, place_ref, cells_ref, models_ref, *refs):
    riders, out_ref = refs[:-1], refs[-1]
    owned, members = models_ref.shape
    part = owned // lanes
    out_ref[pl.ds(0, owned), :] = models_ref[...]
    for j, r in enumerate(riders):
        for lane in range(lanes):
            out_ref[pl.ds((j + 1) * owned + lane * part, part), :] = r[
                0, pl.ds(0, part), pl.ds(lane * members, members)
            ]
    block_cells = owned * (len(riders) + 1)
    home = cells_ref[...] // block_cells
    other = jnp.where(home == place_ref[0], -1, home).astype(jnp.float32)
    other = jnp.max(other, axis=1, keepdims=True)
    out_ref[pl.ds(block_cells, GROUP), :] = jnp.broadcast_to(other, (GROUP, members))


def near_models(place, cell_index, models, first, lanes):
    owned, members = models.shape
    slabs, rows, cells = first[0].shape
    rider = pl.BlockSpec((1, rows, cells), lambda i: (slabs - 1, 0, 0))
    return pl.pallas_call(
        functools.partial(near_kernel, lanes),
        grid=(1,),
        in_specs=[SCALARS, whole(cell_index), whole(models)] + [rider] * len(first),
        out_specs=pl.BlockSpec((owned * (len(first) + 1) + GROUP, members), lambda i: (0, 0)),
        out_shape=jax.ShapeDtypeStruct((owned * (len(first) + 1) + GROUP, members), jnp.float32),
        compiler_params=params(16),
        cost_estimate=cost(0, 1 << 20),
        name="near_models",
    )(place, cell_index, models, *first)


def tile_models_kernel(owned, partners, place_ref, cells_ref, *refs):
    tile_refs, (high_ref, low_ref) = refs[:-2], refs[-2:]
    block_cells = owned * len(partners)
    cells = cells_ref[...]
    distance = (cells // owned % len(partners)) ^ place_ref[1]
    slot = jnp.zeros_like(cells)
    for n, k in enumerate(partners):
        slot = jnp.where(distance == k, n, slot)
    spot = slot * owned + cells % owned
    away = (cells // block_cells) ^ place_ref[0]
    high, low = None, None
    for k, ref in enumerate(tile_refs):
        row = lax.broadcasted_iota(jnp.int32, (block_cells, cells.shape[1]), 0)
        pick = jnp.where((row == spot) & (away == k), 1.0, 0.0).astype(jnp.bfloat16)
        h, l = split(ref[pl.ds(0, block_cells), :].T)
        h = lax.dot_general(h, pick, NN, preferred_element_type=jnp.float32)
        l = lax.dot_general(l, pick, NN, preferred_element_type=jnp.float32)
        high, low = (h, l) if k == 0 else (high + h, low + l)
    high_ref[...] = high.astype(jnp.bfloat16)
    low_ref[...] = low.astype(jnp.bfloat16)


def tile_models(place, cell_index, tiles, owned, partners):
    shape = jax.ShapeDtypeStruct((tiles[0].shape[1], cell_index.shape[1]), jnp.bfloat16)
    return pl.pallas_call(
        functools.partial(tile_models_kernel, owned, partners),
        in_specs=[SCALARS] + [pl.BlockSpec(memory_space=pltpu.VMEM)] * (1 + len(tiles)),
        out_specs=[pl.BlockSpec(memory_space=pltpu.VMEM)] * 2,
        out_shape=[shape] * 2,
        compiler_params=params(16),
        cost_estimate=cost(1 << 30, 2 << 20),
        name="tile_models",
    )(place, cell_index, *tiles)


def wide_kernel(table_ref, high_ref, low_ref):
    fp, gates = table_ref.shape
    rows, columns = high_ref.shape
    iota = lax.broadcasted_iota
    down = (iota(jnp.int32, (rows, fp), 0) // GROUP == iota(jnp.int32, (rows, fp), 1)).astype(jnp.float32)
    across = iota(jnp.int32, (gates, columns), 1) // GROUP == iota(jnp.int32, (gates, columns), 0)
    across = across.astype(jnp.float32).astype(jnp.bfloat16)
    down = down.astype(jnp.bfloat16)
    same = iota(jnp.int32, (rows, columns), 0) % GROUP == iota(jnp.int32, (rows, columns), 1) % GROUP
    for part, ref in zip(split(table_ref[...]), (high_ref, low_ref)):
        tall = lax.dot_general(down, part, NN, preferred_element_type=jnp.float32).astype(jnp.bfloat16)
        full = lax.dot_general(tall, across, NN, preferred_element_type=jnp.float32)
        ref[...] = jnp.where(same, full, 0.0).astype(jnp.bfloat16)


def wide_table(table):
    shape = jax.ShapeDtypeStruct((table.shape[0] * GROUP, table.shape[1] * GROUP), jnp.bfloat16)
    return pl.pallas_call(
        wide_kernel,
        in_specs=[pl.BlockSpec(memory_space=pltpu.VMEM)],
        out_specs=[pl.BlockSpec(memory_space=pltpu.VMEM)] * 2,
        out_shape=[shape] * 2,
        compiler_params=params(16),
        cost_estimate=cost(1 << 28, 1 << 20),
        name="wide_table",
    )(table)


def chunk_kernel(pieces, block_cells, last, place_ref, *refs):
    sens_refs = refs[:pieces]
    model_h, model_l, gate_h, gate_l, obs_ref, cells_ref, terms_in, square_in, terms_ref, square_ref = refs[pieces:]

    @pl.when(pl.program_id(0) == 0)
    def _():
        terms_ref[...] = terms_in[...]
        square_ref[...] = square_in[...]

    sens = [split(r[...].reshape(r.shape[0] * r.shape[1], r.shape[2])) for r in sens_refs]
    sens = tuple(jnp.concatenate([s[i] for s in sens], axis=0) for i in range(2))
    gates = (gate_h[...], gate_l[...])
    predicted = three_pass((model_h[...], model_l[...]), sens, NT)
    misfit_rows = three_pass(split(predicted), gates, NN) - obs_ref[0]
    square_ref[...] += jnp.sum(misfit_rows * misfit_rows, axis=1, keepdims=True)
    back = three_pass(split(misfit_rows), gates, NT)
    terms = terms_ref[...] + three_pass(split(back), sens, NN)
    terms_ref[...] = terms

    if last:

        @pl.when(pl.program_id(0) == pl.num_programs(0) - 1)
        def _():
            cells = cells_ref[...]
            spot = cells % block_cells + jnp.where(cells // block_cells == place_ref[0], 0, block_cells)
            size = cells.shape[1]
            row = lax.broadcasted_iota(jnp.int32, (size, size), 0)
            pick = jnp.where(row == spot, 1.0, 0.0).astype(jnp.bfloat16)
            high = terms.astype(jnp.bfloat16)
            middle, low = split(terms - high.astype(jnp.float32))
            dot = functools.partial(lax.dot_general, dimension_numbers=NT, preferred_element_type=jnp.float32)
            terms_ref[...] = dot(high, pick) + (dot(middle, pick) + dot(low, pick))


def chunk_step(place, block, sens, first, models_t, gates, obs, cell_index, terms, square, block_cells, last):
    spectra, soundings, cells = block.shape
    rows = sens[0].shape[1]
    pieces = len(sens) + 1
    members = terms.shape[0]
    own_groups = soundings // (pieces * GROUP)
    return pl.pallas_call(
        functools.partial(chunk_kernel, pieces, block_cells, last),
        grid_spec=pltpu.PrefetchScalarGridSpec(
            num_scalar_prefetch=1,
            grid=(rows // GROUP,),
            in_specs=[
                pl.BlockSpec((spectra, GROUP, cells), lambda i, place: (0, place[1] * own_groups + first + i, 0))
            ]
            + [pl.BlockSpec((spectra, GROUP, cells), lambda i, place: (0, i, 0))] * len(sens)
            + [whole(a) for a in (*models_t, *gates)]
            + [pl.BlockSpec((1, 1, obs.shape[2]), lambda i, place: (first + i, 0, 0)), whole(cell_index)]
            + [whole(terms), whole(square)],
            out_specs=[whole(terms), whole(square)],
        ),
        out_shape=[
            jax.ShapeDtypeStruct(terms.shape, jnp.float32),
            jax.ShapeDtypeStruct(square.shape, jnp.float32),
        ],
        input_output_aliases={pieces + 7: 0, pieces + 8: 1},
        compiler_params=params(40),
        cost_estimate=cost(
            12 * pieces * spectra * rows * cells * members * 2, 4 * pieces * spectra * rows * cells
        ),
        name="chunk_step",
    )(place, block, *sens, *models_t, *gates, obs, cell_index, terms, square)


def exact_dot(a, b, dims):
    return lax.dot_general(a, b, dims, precision=HIGH, preferred_element_type=jnp.float32)


def gradient_kernel(tiles, owned, place_ref, borrowed_ref, got_ref, square_ref, out_ref):
    devices, slab, cells = got_ref.shape
    owners = devices // tiles
    block_cells = owned * owners
    members = square_ref.shape[0]
    sums = []
    for t in range(tiles):
        total = got_ref[t * owners]
        for f in range(1, owners):
            total = total + got_ref[t * owners + f]
        sums.append(total)
    gradient = []
    for b in range(tiles):
        block = sums[b][:, :block_cells]
        for t in range(tiles):
            block = block + jnp.where(borrowed_ref[place_ref[0] ^ t] == b, sums[t][:, block_cells:], 0.0)
        gradient.append(block)
    square = sum(jnp.sum(g * g, axis=1, keepdims=True) for g in gradient)
    scale = jnp.sqrt(square / (tiles * block_cells) + EPSILON)
    iota = lax.broadcasted_iota
    per_row = members // slab
    down = (iota(jnp.int32, (slab, members), 1) // per_row == iota(jnp.int32, (slab, members), 0))
    lane = iota(jnp.int32, (members, LANES), 1)
    spread = jnp.where(iota(jnp.int32, (members, LANES), 0) % per_row + owned == lane, square_ref[...], 0.0)
    rider = exact_dot(down.astype(jnp.float32), spread, NN)
    for b in range(tiles):
        step = gradient[b] / scale
        for f in range(owners):
            piece = step[:, f * owned : (f + 1) * owned]
            piece = jnp.concatenate([piece, jnp.zeros((slab, LANES - owned), jnp.float32)], axis=1)
            out_ref[b * owners + f] = piece + rider


def gradient_step(place, borrowed, got, square, tiles, owned):
    devices, slab, _ = got.shape
    return pl.pallas_call(
        functools.partial(gradient_kernel, tiles, owned),
        in_specs=[SCALARS] * 2 + [pl.BlockSpec(memory_space=pltpu.VMEM)] * 2,
        out_specs=pl.BlockSpec(memory_space=pltpu.VMEM),
        out_shape=jax.ShapeDtypeStruct((devices, slab, LANES), jnp.float32),
        compiler_params=params(16),
        cost_estimate=cost(1 << 22, 1 << 20),
        name="gradient_step",
    )(place, borrowed, got, square)


def update_kernel(divisor, models_ref, back_ref, updated_ref, misfit_ref):
    devices, slab, _ = back_ref.shape
    owned, members = models_ref.shape
    per_row = members // slab
    iota = lax.broadcasted_iota
    riders = back_ref[0]
    for d in range(1, devices):
        riders = riders + back_ref[d]
    down = (iota(jnp.int32, (slab, members), 1) // per_row == iota(jnp.int32, (slab, members), 0))
    tall = exact_dot(riders, down.astype(jnp.float32), (((0,), (0,)), ((), ())))
    mine = iota(jnp.int32, (LANES, members), 1) % per_row + owned == iota(jnp.int32, (LANES, members), 0)
    misfit = jnp.sum(jnp.where(mine, tall, 0.0), axis=0, keepdims=True) / divisor
    step = back_ref[...].reshape(members, LANES).T[:owned]
    updated_ref[...] = models_ref[...] - STEP_LENGTH * misfit * step
    misfit_ref[...] = misfit


def update(models, back, divisor):
    return pl.pallas_call(
        functools.partial(update_kernel, divisor),
        in_specs=[pl.BlockSpec(memory_space=pltpu.VMEM)] * 2,
        out_specs=[pl.BlockSpec(memory_space=pltpu.VMEM)] * 2,
        out_shape=[
            jax.ShapeDtypeStruct(models.shape, jnp.float32),
            jax.ShapeDtypeStruct((1, models.shape[1]), jnp.float32),
        ],
        compiler_params=params(16),
        cost_estimate=cost(1 << 20, 1 << 18),
        name="update",
    )(models, back)


def chunk_groups(groups):
    if groups < 16:
        return [1] * groups
    ends = [groups // 8, groups * 3 // 16, groups // 8, groups // 16]
    rest = groups - sum(ends)
    return [ends[0], rest - rest // 2, rest // 2] + ends[1:]


def body(sensitivity, models, observed, waveform, cell_index, gate_index):
    both = ("tile", "freq")
    tiles, owners, devices = lax.axis_size("tile"), lax.axis_size("freq"), lax.axis_size(both)
    _, own_freqs, parts, soundings, cells = sensitivity.shape
    freqs = own_freqs * owners
    spectra = own_freqs * parts
    owned, members = models.shape
    ncells = owned * devices
    gates = gate_index.shape[0]
    divisor = 2.0 * tiles * soundings * gates
    own = soundings // owners
    block_cells = owned * owners
    place = jnp.stack([lax.axis_index("tile"), lax.axis_index("freq")])

    block = sensitivity[0].reshape(spectra, soundings, cells)
    lanes = cells // members if owned % (GROUP * (cells // members)) == 0 else 1
    sizes = chunk_groups(own // GROUP)
    starts = [sum(sizes[:i]) for i in range(len(sizes))]
    distances = partner_order(owners)
    partners = [0] + distances
    received, done = [], []

    def send(i):
        after = received[i - 1][:1] if i else []
        if i > 2:
            after = after + done[i - 3 : i - 2]
        pieces = pack(
            place, block, models, after, distances, own, starts[i] * GROUP, sizes[i] * GROUP, 0 if i else lanes
        )
        received.append([swap(p, "freq", k) for p, k in zip(pieces, distances)])

    send(0)
    send(1)
    near = near_models(place, cell_index, models, received[0], lanes)
    blocks = [near] + [swap(near, "tile", k) for k in range(1, tiles)]
    borrowed = jnp.stack([b[block_cells, 0] for b in blocks]).astype(jnp.int32)
    models_t = tile_models(place, cell_index, blocks, owned, partners)

    order = place[1] ^ jnp.array(partners, jnp.int32)
    wide = wide_table(gate_table(order, own_freqs, freqs, waveform, gate_index).T)
    obs = observed[0].reshape(gates, own // GROUP, GROUP)
    obs = jnp.swapaxes(obs, 0, 1).reshape(own // GROUP, 1, gates * GROUP)

    terms = jnp.zeros((members, cells), jnp.float32)
    square = jnp.zeros((members, LANES), jnp.float32)
    for i, start in enumerate(starts):
        if i > 1:
            send(i)
        last = i == len(starts) - 1
        terms, square = chunk_step(
            place, block, received[i], start, models_t, wide, obs, cell_index, terms, square, block_cells, last
        )
        done.append(square)

    slab = members // devices
    sent = terms.reshape(devices, slab, cells)
    got = lax.all_to_all(sent, both, split_axis=0, concat_axis=0, tiled=True)
    if slab % GROUP == 0 and members // slab + owned <= LANES:
        step = gradient_step(place, borrowed, got, square, tiles, owned)
        back = lax.all_to_all(step, both, split_axis=0, concat_axis=0, tiled=True)
        updated, misfit = update(models, back, divisor)
        return (updated, misfit.reshape(members))

    got = jnp.sum(got.reshape(tiles, owners, slab, cells), axis=1)
    tile_ids = jnp.arange(tiles)
    lent = (jnp.take(borrowed, tile_ids ^ place[0])[None, :] == tile_ids[:, None]).astype(jnp.float32)
    gradient = got[:, :, :block_cells] + jnp.sum(
        lent[:, :, None, None] * got[None, :, :, block_cells:], axis=1
    )
    scale = jnp.sqrt(jnp.sum(gradient * gradient, axis=(0, 2)) / ncells + EPSILON)
    step = gradient / scale[None, :, None]
    step = step.reshape(tiles, slab, owners, owned).transpose(0, 2, 1, 3)
    step = step.reshape(devices, slab, owned)
    rider = jnp.broadcast_to(square[:, 0].reshape(1, slab, devices), (devices, slab, devices))
    back = lax.all_to_all(
        jnp.concatenate([step, rider], axis=2), both, split_axis=0, concat_axis=0, tiled=True
    )
    misfit = jnp.sum(back[:, :, owned:], axis=0).reshape(members) / divisor
    back = back[:, :, :owned].reshape(members, owned)
    return (models - (STEP_LENGTH * misfit)[None, :] * back.T, misfit)


def solution(mesh):
    in_specs = (
        P("tile", "freq", None, None, None),
        P(("tile", "freq"), None),
        P("tile", None, "freq"),
        P(),
        P("tile", None),
        P(),
    )
    out_specs = (P(("tile", "freq"), None), P())
    return jax.shard_map(body, mesh=mesh, in_specs=in_specs, out_specs=out_specs, check_vma=False)
```

```python
import functools
import math

import jax
import jax.numpy as jnp
from jax import lax
from jax.experimental import pallas as pl
from jax.experimental.pallas import tpu as pltpu
from jax.sharding import PartitionSpec as P

HIGH = lax.Precision.HIGHEST
PHASE_RATE = 0.37
STEP_LENGTH = 0.5
EPSILON = 1e-06
GROUP = 8
LANES = 128

NN = (((1,), (0,)), ((), ()))
NT = (((1,), (1,)), ((), ()))


def swap(x, axis, k):
    return lax.ppermute(x, axis, [(i, i ^ k) for i in range(lax.axis_size(axis))])


def partner_order(size):
    assert size & (size - 1) == 0
    across, near = list(range(size // 2, size)), list(range(1, size // 2))[::-1]
    across = across[:1] + across[1:][::-1]
    return [k for pair in zip(across, near + [None]) for k in pair if k is not None]


def gate_table(owner_order, own_freqs, freqs, waveform, gate_index):
    samples = waveform.shape[0]
    freq_ids = (owner_order[:, None] * own_freqs + jnp.arange(own_freqs)[None, :]).reshape(freqs)
    freq_col = freq_ids.astype(jnp.float32)[:, None] + 0.5
    time_row = jnp.arange(samples, dtype=jnp.float32)[None, :] + 0.5
    phases = PHASE_RATE * freq_col * time_row
    kernel = jnp.stack([jnp.cos(phases), jnp.sin(phases)], axis=1) / math.sqrt(freqs)
    steps = jnp.arange(samples)
    lag = gate_index[:, None] - steps[None, :]
    picked = jnp.sum(
        jnp.where(lag[:, :, None] == steps[None, None, :], waveform[None, None, :], 0.0), axis=-1
    )
    return jnp.einsum("gk,fpk->gfp", picked, kernel, precision=HIGH).reshape(gate_index.shape[0], freqs * 2)


def split(x):
    high = x.astype(jnp.bfloat16)
    return high, (x - high.astype(jnp.float32)).astype(jnp.bfloat16)


def three_pass(a, b, dims):
    dot = functools.partial(lax.dot_general, dimension_numbers=dims, preferred_element_type=jnp.float32)
    return dot(a[0], b[0]) + (dot(a[0], b[1]) + dot(a[1], b[0]))


def params(mebibytes):
    return pltpu.CompilerParams(vmem_limit_bytes=mebibytes * 1024 * 1024)


def cost(flops, bytes_accessed):
    return pl.CostEstimate(flops=flops, bytes_accessed=bytes_accessed, transcendentals=0)


def whole(a):
    return pl.BlockSpec(a.shape, lambda *_: (0,) * a.ndim)


HBM = pl.BlockSpec(memory_space=pltpu.HBM)
SCALARS = pl.BlockSpec(memory_space=pltpu.SMEM)


def pack_kernel(distances, own, first, rows, lanes, place_ref, block_ref, models_ref, *refs):
    outs, (held, in_sems, out_sems) = refs[-len(distances) - 3 : -3], refs[-3:]
    spectra = block_ref.shape[0]
    owned, members = models_ref.shape
    arrivals, departures = [], []
    for j, k in enumerate(distances):
        row = pl.multiple_of((place_ref[1] ^ k) * own + first, GROUP)
        source, target = block_ref.at[:, pl.ds(row, rows)], held.at[j, pl.ds(0, spectra)]
        arrivals.append(pltpu.make_async_copy(source, target, in_sems.at[j]))
        departures.append(pltpu.make_async_copy(held.at[j], outs[j], out_sems.at[j]))
        arrivals[j].start()
    for j in range(len(distances)):
        for lane in range(lanes):
            part = owned // lanes
            held[j, spectra, pl.ds(0, part), pl.ds(lane * members, members)] = models_ref[pl.ds(lane * part, part), :]
    for arrival, departure in zip(arrivals, departures):
        arrival.wait()
        departure.start()
    for departure in departures:
        departure.wait()


def pack(place, block, models, after, distances, own, first, rows, lanes):
    spectra, _, cells = block.shape
    count = len(distances)
    shape = (spectra + (lanes > 0), rows, cells)
    return pl.pallas_call(
        functools.partial(pack_kernel, distances, own, first, rows, lanes),
        in_specs=[SCALARS, HBM, pl.BlockSpec(memory_space=pltpu.VMEM)] + [HBM] * len(after),
        out_specs=[HBM] * count,
        out_shape=[jax.ShapeDtypeStruct(shape, jnp.float32)] * count,
        scratch_shapes=[
            pltpu.VMEM((count, *shape), jnp.float32),
            pltpu.SemaphoreType.DMA((count,)),
            pltpu.SemaphoreType.DMA((count,)),
        ],
        compiler_params=params(48),
        cost_estimate=cost(0, 8 * count * spectra * rows * cells),
        name="pack",
    )(place, block, models, *after)


def near_kernel(lanes, place_ref, cells_ref, models_ref, *refs):
    riders, out_ref = refs[:-1], refs[-1]
    owned, members = models_ref.shape
    part = owned // lanes
    out_ref[pl.ds(0, owned), :] = models_ref[...]
    for j, r in enumerate(riders):
        for lane in range(lanes):
            out_ref[pl.ds((j + 1) * owned + lane * part, part), :] = r[
                0, pl.ds(0, part), pl.ds(lane * members, members)
            ]
    block_cells = owned * (len(riders) + 1)
    home = cells_ref[...] // block_cells
    other = jnp.where(home == place_ref[0], -1, home).astype(jnp.float32)
    other = jnp.max(other, axis=1, keepdims=True)
    out_ref[pl.ds(block_cells, GROUP), :] = jnp.broadcast_to(other, (GROUP, members))


def near_models(place, cell_index, models, first, lanes):
    owned, members = models.shape
    slabs, rows, cells = first[0].shape
    rider = pl.BlockSpec((1, rows, cells), lambda i: (slabs - 1, 0, 0))
    return pl.pallas_call(
        functools.partial(near_kernel, lanes),
        grid=(1,),
        in_specs=[SCALARS, whole(cell_index), whole(models)] + [rider] * len(first),
        out_specs=pl.BlockSpec((owned * (len(first) + 1) + GROUP, members), lambda i: (0, 0)),
        out_shape=jax.ShapeDtypeStruct((owned * (len(first) + 1) + GROUP, members), jnp.float32),
        compiler_params=params(16),
        cost_estimate=cost(0, 1 << 20),
        name="near_models",
    )(place, cell_index, models, *first)


def tile_models_kernel(owned, partners, place_ref, cells_ref, *refs):
    tile_refs, (high_ref, low_ref) = refs[:-2], refs[-2:]
    block_cells = owned * len(partners)
    cells = cells_ref[...]
    distance = (cells // owned % len(partners)) ^ place_ref[1]
    slot = jnp.zeros_like(cells)
    for n, k in enumerate(partners):
        slot = jnp.where(distance == k, n, slot)
    spot = slot * owned + cells % owned
    away = (cells // block_cells) ^ place_ref[0]
    high, low = None, None
    for k, ref in enumerate(tile_refs):
        row = lax.broadcasted_iota(jnp.int32, (block_cells, cells.shape[1]), 0)
        pick = jnp.where((row == spot) & (away == k), 1.0, 0.0).astype(jnp.bfloat16)
        h, l = split(ref[pl.ds(0, block_cells), :].T)
        h = lax.dot_general(h, pick, NN, preferred_element_type=jnp.float32)
        l = lax.dot_general(l, pick, NN, preferred_element_type=jnp.float32)
        high, low = (h, l) if k == 0 else (high + h, low + l)
    high_ref[...] = high.astype(jnp.bfloat16)
    low_ref[...] = low.astype(jnp.bfloat16)


def tile_models(place, cell_index, tiles, owned, partners):
    shape = jax.ShapeDtypeStruct((tiles[0].shape[1], cell_index.shape[1]), jnp.bfloat16)
    return pl.pallas_call(
        functools.partial(tile_models_kernel, owned, partners),
        in_specs=[SCALARS] + [pl.BlockSpec(memory_space=pltpu.VMEM)] * (1 + len(tiles)),
        out_specs=[pl.BlockSpec(memory_space=pltpu.VMEM)] * 2,
        out_shape=[shape] * 2,
        compiler_params=params(16),
        cost_estimate=cost(1 << 30, 2 << 20),
        name="tile_models",
    )(place, cell_index, *tiles)


def wide_kernel(table_ref, high_ref, low_ref):
    fp, gates = table_ref.shape
    rows, columns = high_ref.shape
    iota = lax.broadcasted_iota
    down = (iota(jnp.int32, (rows, fp), 0) // GROUP == iota(jnp.int32, (rows, fp), 1)).astype(jnp.float32)
    across = iota(jnp.int32, (gates, columns), 1) // GROUP == iota(jnp.int32, (gates, columns), 0)
    across = across.astype(jnp.float32).astype(jnp.bfloat16)
    down = down.astype(jnp.bfloat16)
    same = iota(jnp.int32, (rows, columns), 0) % GROUP == iota(jnp.int32, (rows, columns), 1) % GROUP
    for part, ref in zip(split(table_ref[...]), (high_ref, low_ref)):
        tall = lax.dot_general(down, part, NN, preferred_element_type=jnp.float32).astype(jnp.bfloat16)
        full = lax.dot_general(tall, across, NN, preferred_element_type=jnp.float32)
        ref[...] = jnp.where(same, full, 0.0).astype(jnp.bfloat16)


def wide_table(table):
    shape = jax.ShapeDtypeStruct((table.shape[0] * GROUP, table.shape[1] * GROUP), jnp.bfloat16)
    return pl.pallas_call(
        wide_kernel,
        in_specs=[pl.BlockSpec(memory_space=pltpu.VMEM)],
        out_specs=[pl.BlockSpec(memory_space=pltpu.VMEM)] * 2,
        out_shape=[shape] * 2,
        compiler_params=params(16),
        cost_estimate=cost(1 << 28, 1 << 20),
        name="wide_table",
    )(table)


def chunk_kernel(pieces, block_cells, last, place_ref, *refs):
    sens_refs = refs[:pieces]
    model_h, model_l, gate_h, gate_l, obs_ref, cells_ref, terms_in, square_in, terms_ref, square_ref = refs[pieces:]

    @pl.when(pl.program_id(0) == 0)
    def _():
        terms_ref[...] = terms_in[...]
        square_ref[...] = square_in[...]

    sens = [split(r[...].reshape(r.shape[0] * r.shape[1], r.shape[2])) for r in sens_refs]
    sens = tuple(jnp.concatenate([s[i] for s in sens], axis=0) for i in range(2))
    gates = (gate_h[...], gate_l[...])
    predicted = three_pass((model_h[...], model_l[...]), sens, NT)
    misfit_rows = three_pass(split(predicted), gates, NN) - obs_ref[0]
    square_ref[...] += jnp.sum(misfit_rows * misfit_rows, axis=1, keepdims=True)
    back = three_pass(split(misfit_rows), gates, NT)
    terms = terms_ref[...] + three_pass(split(back), sens, NN)
    terms_ref[...] = terms

    if last:

        @pl.when(pl.program_id(0) == pl.num_programs(0) - 1)
        def _():
            cells = cells_ref[...]
            spot = cells % block_cells + jnp.where(cells // block_cells == place_ref[0], 0, block_cells)
            size = cells.shape[1]
            row = lax.broadcasted_iota(jnp.int32, (size, size), 0)
            pick = jnp.where(row == spot, 1.0, 0.0).astype(jnp.bfloat16)
            high = terms.astype(jnp.bfloat16)
            middle, low = split(terms - high.astype(jnp.float32))
            dot = functools.partial(lax.dot_general, dimension_numbers=NT, preferred_element_type=jnp.float32)
            terms_ref[...] = dot(high, pick) + (dot(middle, pick) + dot(low, pick))


def chunk_step(place, block, sens, first, models_t, gates, obs, cell_index, terms, square, block_cells, last):
    spectra, soundings, cells = block.shape
    rows = sens[0].shape[1]
    pieces = len(sens) + 1
    members = terms.shape[0]
    own_groups = soundings // (pieces * GROUP)
    return pl.pallas_call(
        functools.partial(chunk_kernel, pieces, block_cells, last),
        grid_spec=pltpu.PrefetchScalarGridSpec(
            num_scalar_prefetch=1,
            grid=(rows // GROUP,),
            in_specs=[
                pl.BlockSpec((spectra, GROUP, cells), lambda i, place: (0, place[1] * own_groups + first + i, 0))
            ]
            + [pl.BlockSpec((spectra, GROUP, cells), lambda i, place: (0, i, 0))] * len(sens)
            + [whole(a) for a in (*models_t, *gates)]
            + [pl.BlockSpec((1, 1, obs.shape[2]), lambda i, place: (first + i, 0, 0)), whole(cell_index)]
            + [whole(terms), whole(square)],
            out_specs=[whole(terms), whole(square)],
        ),
        out_shape=[
            jax.ShapeDtypeStruct(terms.shape, jnp.float32),
            jax.ShapeDtypeStruct(square.shape, jnp.float32),
        ],
        input_output_aliases={pieces + 7: 0, pieces + 8: 1},
        compiler_params=params(40),
        cost_estimate=cost(
            12 * pieces * spectra * rows * cells * members * 2, 4 * pieces * spectra * rows * cells
        ),
        name="chunk_step",
    )(place, block, *sens, *models_t, *gates, obs, cell_index, terms, square)


def exact_dot(a, b, dims):
    return lax.dot_general(a, b, dims, precision=HIGH, preferred_element_type=jnp.float32)


def gradient_kernel(tiles, owned, place_ref, borrowed_ref, got_ref, square_ref, out_ref):
    devices, slab, cells = got_ref.shape
    owners = devices // tiles
    block_cells = owned * owners
    members = square_ref.shape[0]
    sums = []
    for t in range(tiles):
        total = got_ref[t * owners]
        for f in range(1, owners):
            total = total + got_ref[t * owners + f]
        sums.append(total)
    gradient = []
    for b in range(tiles):
        block = sums[b][:, :block_cells]
        for t in range(tiles):
            block = block + jnp.where(borrowed_ref[place_ref[0] ^ t] == b, sums[t][:, block_cells:], 0.0)
        gradient.append(block)
    square = sum(jnp.sum(g * g, axis=1, keepdims=True) for g in gradient)
    scale = jnp.sqrt(square / (tiles * block_cells) + EPSILON)
    iota = lax.broadcasted_iota
    per_row = members // slab
    down = (iota(jnp.int32, (slab, members), 1) // per_row == iota(jnp.int32, (slab, members), 0))
    lane = iota(jnp.int32, (members, LANES), 1)
    spread = jnp.where(iota(jnp.int32, (members, LANES), 0) % per_row + owned == lane, square_ref[...], 0.0)
    rider = exact_dot(down.astype(jnp.float32), spread, NN)
    for b in range(tiles):
        step = gradient[b] / scale
        for f in range(owners):
            piece = step[:, f * owned : (f + 1) * owned]
            piece = jnp.concatenate([piece, jnp.zeros((slab, LANES - owned), jnp.float32)], axis=1)
            out_ref[b * owners + f] = piece + rider


def gradient_step(place, borrowed, got, square, tiles, owned):
    devices, slab, _ = got.shape
    return pl.pallas_call(
        functools.partial(gradient_kernel, tiles, owned),
        in_specs=[SCALARS] * 2 + [pl.BlockSpec(memory_space=pltpu.VMEM)] * 2,
        out_specs=pl.BlockSpec(memory_space=pltpu.VMEM),
        out_shape=jax.ShapeDtypeStruct((devices, slab, LANES), jnp.float32),
        compiler_params=params(16),
        cost_estimate=cost(1 << 22, 1 << 20),
        name="gradient_step",
    )(place, borrowed, got, square)


def update_kernel(divisor, models_ref, back_ref, updated_ref, misfit_ref):
    devices, slab, _ = back_ref.shape
    owned, members = models_ref.shape
    per_row = members // slab
    iota = lax.broadcasted_iota
    riders = back_ref[0]
    for d in range(1, devices):
        riders = riders + back_ref[d]
    down = (iota(jnp.int32, (slab, members), 1) // per_row == iota(jnp.int32, (slab, members), 0))
    tall = exact_dot(riders, down.astype(jnp.float32), (((0,), (0,)), ((), ())))
    mine = iota(jnp.int32, (LANES, members), 1) % per_row + owned == iota(jnp.int32, (LANES, members), 0)
    misfit = jnp.sum(jnp.where(mine, tall, 0.0), axis=0, keepdims=True) / divisor
    step = back_ref[...].reshape(members, LANES).T[:owned]
    updated_ref[...] = models_ref[...] - STEP_LENGTH * misfit * step
    misfit_ref[...] = misfit


def update(models, back, divisor):
    return pl.pallas_call(
        functools.partial(update_kernel, divisor),
        in_specs=[pl.BlockSpec(memory_space=pltpu.VMEM)] * 2,
        out_specs=[pl.BlockSpec(memory_space=pltpu.VMEM)] * 2,
        out_shape=[
            jax.ShapeDtypeStruct(models.shape, jnp.float32),
            jax.ShapeDtypeStruct((1, models.shape[1]), jnp.float32),
        ],
        compiler_params=params(16),
        cost_estimate=cost(1 << 20, 1 << 18),
        name="update",
    )(models, back)


def chunk_groups(groups):
    if groups < 16:
        return [1] * groups
    ends = [groups // 8, groups * 3 // 16, groups // 8, groups // 16]
    rest = groups - sum(ends)
    return [ends[0], rest - rest // 2, rest // 2] + ends[1:]


def body(sensitivity, models, observed, waveform, cell_index, gate_index):
    both = ("tile", "freq")
    tiles, owners, devices = lax.axis_size("tile"), lax.axis_size("freq"), lax.axis_size(both)
    _, own_freqs, parts, soundings, cells = sensitivity.shape
    freqs = own_freqs * owners
    spectra = own_freqs * parts
    owned, members = models.shape
    ncells = owned * devices
    gates = gate_index.shape[0]
    divisor = 2.0 * tiles * soundings * gates
    own = soundings // owners
    block_cells = owned * owners
    place = jnp.stack([lax.axis_index("tile"), lax.axis_index("freq")])

    block = sensitivity[0].reshape(spectra, soundings, cells)
    lanes = cells // members if owned % (GROUP * (cells // members)) == 0 else 1
    sizes = chunk_groups(own // GROUP)
    starts = [sum(sizes[:i]) for i in range(len(sizes))]
    distances = partner_order(owners)
    partners = [0] + distances
    received, done = [], []

    def send(i):
        after = received[i - 1][:1] if i else []
        if i > 2:
            after = after + done[i - 3 : i - 2]
        pieces = pack(
            place, block, models, after, distances, own, starts[i] * GROUP, sizes[i] * GROUP, 0 if i else lanes
        )
        received.append([swap(p, "freq", k) for p, k in zip(pieces, distances)])

    send(0)
    send(1)
    near = near_models(place, cell_index, models, received[0], lanes)
    blocks = [near] + [swap(near, "tile", k) for k in range(1, tiles)]
    borrowed = jnp.stack([b[block_cells, 0] for b in blocks]).astype(jnp.int32)
    models_t = tile_models(place, cell_index, blocks, owned, partners)

    order = place[1] ^ jnp.array(partners, jnp.int32)
    wide = wide_table(gate_table(order, own_freqs, freqs, waveform, gate_index).T)
    obs = observed[0].reshape(gates, own // GROUP, GROUP)
    obs = jnp.swapaxes(obs, 0, 1).reshape(own // GROUP, 1, gates * GROUP)

    terms = jnp.zeros((members, cells), jnp.float32)
    square = jnp.zeros((members, LANES), jnp.float32)
    for i, start in enumerate(starts):
        if i > 1:
            send(i)
        last = i == len(starts) - 1
        terms, square = chunk_step(
            place, block, received[i], start, models_t, wide, obs, cell_index, terms, square, block_cells, last
        )
        done.append(square)

    slab = members // devices
    sent = terms.reshape(devices, slab, cells)
    got = lax.all_to_all(sent, both, split_axis=0, concat_axis=0, tiled=True)
    if slab % GROUP == 0 and members // slab + owned <= LANES:
        step = gradient_step(place, borrowed, got, square, tiles, owned)
        back = lax.all_to_all(step, both, split_axis=0, concat_axis=0, tiled=True)
        updated, misfit = update(models, back, divisor)
        return (updated, misfit.reshape(members))

    got = jnp.sum(got.reshape(tiles, owners, slab, cells), axis=1)
    tile_ids = jnp.arange(tiles)
    lent = (jnp.take(borrowed, tile_ids ^ place[0])[None, :] == tile_ids[:, None]).astype(jnp.float32)
    gradient = got[:, :, :block_cells] + jnp.sum(
        lent[:, :, None, None] * got[None, :, :, block_cells:], axis=1
    )
    scale = jnp.sqrt(jnp.sum(gradient * gradient, axis=(0, 2)) / ncells + EPSILON)
    step = gradient / scale[None, :, None]
    step = step.reshape(tiles, slab, owners, owned).transpose(0, 2, 1, 3)
    step = step.reshape(devices, slab, owned)
    rider = jnp.broadcast_to(square[:, 0].reshape(1, slab, devices), (devices, slab, devices))
    back = lax.all_to_all(
        jnp.concatenate([step, rider], axis=2), both, split_axis=0, concat_axis=0, tiled=True
    )
    misfit = jnp.sum(back[:, :, owned:], axis=0).reshape(members) / divisor
    back = back[:, :, :owned].reshape(members, owned)
    return (models - (STEP_LENGTH * misfit)[None, :] * back.T, misfit)


def solution(mesh):
    in_specs = (
        P("tile", "freq", None, None, None),
        P(("tile", "freq"), None),
        P("tile", None, "freq"),
        P(),
        P("tile", None),
        P(),
    )
    out_specs = (P(("tile", "freq"), None), P())
    return jax.shard_map(body, mesh=mesh, in_specs=in_specs, out_specs=out_specs, check_vma=False)
```

```python
import functools
import math

import jax
import jax.numpy as jnp
from jax import lax
from jax.experimental import pallas as pl
from jax.experimental.pallas import tpu as pltpu
from jax.sharding import PartitionSpec as P

HIGH = lax.Precision.HIGHEST
PHASE_RATE = 0.37
STEP_LENGTH = 0.5
EPSILON = 1e-06
GROUP = 8
LANES = 128

NN = (((1,), (0,)), ((), ()))
NT = (((1,), (1,)), ((), ()))


def swap(x, axis, k):
    return lax.ppermute(x, axis, [(i, i ^ k) for i in range(lax.axis_size(axis))])


def partner_order(size):
    assert size & (size - 1) == 0
    across, near = list(range(size // 2, size)), list(range(1, size // 2))[::-1]
    across = across[:1] + across[1:][::-1]
    return [k for pair in zip(across, near + [None]) for k in pair if k is not None]


def gate_table(owner_order, own_freqs, freqs, waveform, gate_index):
    samples = waveform.shape[0]
    freq_ids = (owner_order[:, None] * own_freqs + jnp.arange(own_freqs)[None, :]).reshape(freqs)
    freq_col = freq_ids.astype(jnp.float32)[:, None] + 0.5
    time_row = jnp.arange(samples, dtype=jnp.float32)[None, :] + 0.5
    phases = PHASE_RATE * freq_col * time_row
    kernel = jnp.stack([jnp.cos(phases), jnp.sin(phases)], axis=1) / math.sqrt(freqs)
    steps = jnp.arange(samples)
    lag = gate_index[:, None] - steps[None, :]
    picked = jnp.sum(
        jnp.where(lag[:, :, None] == steps[None, None, :], waveform[None, None, :], 0.0), axis=-1
    )
    return jnp.einsum("gk,fpk->gfp", picked, kernel, precision=HIGH).reshape(gate_index.shape[0], freqs * 2)


def split(x):
    high = x.astype(jnp.bfloat16)
    return high, (x - high.astype(jnp.float32)).astype(jnp.bfloat16)


def three_pass(a, b, dims):
    dot = functools.partial(lax.dot_general, dimension_numbers=dims, preferred_element_type=jnp.float32)
    return dot(a[0], b[0]) + (dot(a[0], b[1]) + dot(a[1], b[0]))


def params(mebibytes):
    return pltpu.CompilerParams(vmem_limit_bytes=mebibytes * 1024 * 1024)


def cost(flops, bytes_accessed):
    return pl.CostEstimate(flops=flops, bytes_accessed=bytes_accessed, transcendentals=0)


def whole(a):
    return pl.BlockSpec(a.shape, lambda *_: (0,) * a.ndim)


HBM = pl.BlockSpec(memory_space=pltpu.HBM)
SCALARS = pl.BlockSpec(memory_space=pltpu.SMEM)


def pack_kernel(parts, own, lanes, place_ref, block_ref, models_ref, *refs):
    outs, held = refs[-2 * len(parts) - 2 : -len(parts) - 2], refs[-len(parts) - 2 : -2]
    in_sems, out_sems = refs[-2:]
    spectra = block_ref.shape[0]
    owned, members = models_ref.shape
    arrivals, departures = [], []
    for j, (k, first, rows) in enumerate(parts):
        row = pl.multiple_of((place_ref[1] ^ k) * own + first, GROUP)
        source, target = block_ref.at[:, pl.ds(row, rows)], held[j].at[pl.ds(0, spectra)]
        arrivals.append(pltpu.make_async_copy(source, target, in_sems.at[j]))
        departures.append(pltpu.make_async_copy(held[j], outs[j], out_sems.at[j]))
        arrivals[j].start()
    for j in range(len(parts)):
        for lane in range(lanes):
            part = owned // lanes
            held[j][spectra, pl.ds(0, part), pl.ds(lane * members, members)] = models_ref[pl.ds(lane * part, part), :]
    for arrival, departure in zip(arrivals, departures):
        arrival.wait()
        departure.start()
    for departure in departures:
        departure.wait()


def pack(place, block, models, after, parts, own, lanes):
    spectra, _, cells = block.shape
    shapes = [(spectra + (lanes > 0), rows, cells) for _, _, rows in parts]
    return pl.pallas_call(
        functools.partial(pack_kernel, parts, own, lanes),
        in_specs=[SCALARS, HBM, pl.BlockSpec(memory_space=pltpu.VMEM)] + [HBM] * len(after),
        out_specs=[HBM] * len(parts),
        out_shape=[jax.ShapeDtypeStruct(shape, jnp.float32) for shape in shapes],
        scratch_shapes=[pltpu.VMEM(shape, jnp.float32) for shape in shapes]
        + [pltpu.SemaphoreType.DMA((len(parts),)), pltpu.SemaphoreType.DMA((len(parts),))],
        compiler_params=params(48),
        cost_estimate=cost(0, 8 * spectra * cells * sum(rows for _, _, rows in parts)),
        name="pack",
    )(place, block, models, *after)


def near_kernel(lanes, place_ref, cells_ref, models_ref, *refs):
    riders, out_ref = refs[:-2], refs[-1]
    owned, members = models_ref.shape
    part = owned // lanes
    out_ref[pl.ds(0, owned), :] = models_ref[...]
    for j, r in enumerate(riders):
        for lane in range(lanes):
            out_ref[pl.ds((j + 1) * owned + lane * part, part), :] = r[
                0, pl.ds(0, part), pl.ds(lane * members, members)
            ]
    block_cells = owned * (len(riders) + 1)
    home = cells_ref[...] // block_cells
    other = jnp.where(home == place_ref[0], -1, home).astype(jnp.float32)
    other = jnp.max(other, axis=1, keepdims=True)
    out_ref[pl.ds(block_cells, GROUP), :] = jnp.broadcast_to(other, (GROUP, members))


def near_models(place, cell_index, models, first, after, rows, lanes):
    owned, members = models.shape
    slabs, _, cells = first[0].shape
    rider = pl.BlockSpec((1, rows, cells), lambda i: (slabs - 1, 0, 0))
    return pl.pallas_call(
        functools.partial(near_kernel, lanes),
        grid=(1,),
        in_specs=[SCALARS, whole(cell_index), whole(models)] + [rider] * len(first) + [HBM],
        out_specs=pl.BlockSpec((owned * (len(first) + 1) + GROUP, members), lambda i: (0, 0)),
        out_shape=jax.ShapeDtypeStruct((owned * (len(first) + 1) + GROUP, members), jnp.float32),
        compiler_params=params(16),
        cost_estimate=cost(0, 1 << 20),
        name="near_models",
    )(place, cell_index, models, *first, after)


def tile_models_kernel(owned, partners, place_ref, cells_ref, *refs):
    tile_refs, (high_ref, low_ref) = refs[:-2], refs[-2:]
    block_cells = owned * len(partners)
    cells = cells_ref[...]
    distance = (cells // owned % len(partners)) ^ place_ref[1]
    slot = jnp.zeros_like(cells)
    for n, k in enumerate(partners):
        slot = jnp.where(distance == k, n, slot)
    spot = slot * owned + cells % owned
    away = (cells // block_cells) ^ place_ref[0]
    high, low = None, None
    for k, ref in enumerate(tile_refs):
        row = lax.broadcasted_iota(jnp.int32, (block_cells, cells.shape[1]), 0)
        pick = jnp.where((row == spot) & (away == k), 1.0, 0.0).astype(jnp.bfloat16)
        h, l = split(ref[pl.ds(0, block_cells), :].T)
        h = lax.dot_general(h, pick, NN, preferred_element_type=jnp.float32)
        l = lax.dot_general(l, pick, NN, preferred_element_type=jnp.float32)
        high, low = (h, l) if k == 0 else (high + h, low + l)
    high_ref[...] = high.astype(jnp.bfloat16)
    low_ref[...] = low.astype(jnp.bfloat16)


def tile_models(place, cell_index, tiles, owned, partners):
    shape = jax.ShapeDtypeStruct((tiles[0].shape[1], cell_index.shape[1]), jnp.bfloat16)
    return pl.pallas_call(
        functools.partial(tile_models_kernel, owned, partners),
        in_specs=[SCALARS] + [pl.BlockSpec(memory_space=pltpu.VMEM)] * (1 + len(tiles)),
        out_specs=[pl.BlockSpec(memory_space=pltpu.VMEM)] * 2,
        out_shape=[shape] * 2,
        compiler_params=params(16),
        cost_estimate=cost(1 << 30, 2 << 20),
        name="tile_models",
    )(place, cell_index, *tiles)


def wide_kernel(table_ref, high_ref, low_ref):
    fp, gates = table_ref.shape
    rows, columns = high_ref.shape
    iota = lax.broadcasted_iota
    down = (iota(jnp.int32, (rows, fp), 0) // GROUP == iota(jnp.int32, (rows, fp), 1)).astype(jnp.float32)
    across = iota(jnp.int32, (gates, columns), 1) // GROUP == iota(jnp.int32, (gates, columns), 0)
    across = across.astype(jnp.float32).astype(jnp.bfloat16)
    down = down.astype(jnp.bfloat16)
    same = iota(jnp.int32, (rows, columns), 0) % GROUP == iota(jnp.int32, (rows, columns), 1) % GROUP
    for part, ref in zip(split(table_ref[...]), (high_ref, low_ref)):
        tall = lax.dot_general(down, part, NN, preferred_element_type=jnp.float32).astype(jnp.bfloat16)
        full = lax.dot_general(tall, across, NN, preferred_element_type=jnp.float32)
        ref[...] = jnp.where(same, full, 0.0).astype(jnp.bfloat16)


def wide_table(table):
    shape = jax.ShapeDtypeStruct((table.shape[0] * GROUP, table.shape[1] * GROUP), jnp.bfloat16)
    return pl.pallas_call(
        wide_kernel,
        in_specs=[pl.BlockSpec(memory_space=pltpu.VMEM)],
        out_specs=[pl.BlockSpec(memory_space=pltpu.VMEM)] * 2,
        out_shape=[shape] * 2,
        compiler_params=params(16),
        cost_estimate=cost(1 << 28, 1 << 20),
        name="wide_table",
    )(table)


def chunk_kernel(pieces, block_cells, last, place_ref, *refs):
    sens_refs = refs[:pieces]
    model_h, model_l, gate_h, gate_l, obs_ref, cells_ref, terms_in, square_in, terms_ref, square_ref = refs[pieces:]

    @pl.when(pl.program_id(0) == 0)
    def _():
        terms_ref[...] = terms_in[...]
        square_ref[...] = square_in[...]

    sens = [split(r[...].reshape(r.shape[0] * r.shape[1], r.shape[2])) for r in sens_refs]
    sens = tuple(jnp.concatenate([s[i] for s in sens], axis=0) for i in range(2))
    gates = (gate_h[...], gate_l[...])
    predicted = three_pass((model_h[...], model_l[...]), sens, NT)
    misfit_rows = three_pass(split(predicted), gates, NN) - obs_ref[0]
    square_ref[...] += jnp.sum(misfit_rows * misfit_rows, axis=1, keepdims=True)
    back = three_pass(split(misfit_rows), gates, NT)
    terms = terms_ref[...] + three_pass(split(back), sens, NN)
    terms_ref[...] = terms

    if last:

        @pl.when(pl.program_id(0) == pl.num_programs(0) - 1)
        def _():
            cells = cells_ref[...]
            spot = cells % block_cells + jnp.where(cells // block_cells == place_ref[0], 0, block_cells)
            size = cells.shape[1]
            row = lax.broadcasted_iota(jnp.int32, (size, size), 0)
            pick = jnp.where(row == spot, 1.0, 0.0).astype(jnp.bfloat16)
            high = terms.astype(jnp.bfloat16)
            middle, low = split(terms - high.astype(jnp.float32))
            dot = functools.partial(lax.dot_general, dimension_numbers=NT, preferred_element_type=jnp.float32)
            terms_ref[...] = dot(high, pick) + (dot(middle, pick) + dot(low, pick))


def chunk_step(place, block, sens, offsets, first, rows, models_t, gates, obs, cell_index, terms, square, block_cells, last):
    spectra, soundings, cells = block.shape
    pieces = len(sens) + 1
    members = terms.shape[0]
    own_groups = soundings // (pieces * GROUP)
    return pl.pallas_call(
        functools.partial(chunk_kernel, pieces, block_cells, last),
        grid_spec=pltpu.PrefetchScalarGridSpec(
            num_scalar_prefetch=1,
            grid=(rows // GROUP,),
            in_specs=[
                pl.BlockSpec((spectra, GROUP, cells), lambda i, place: (0, place[1] * own_groups + first + i, 0))
            ]
            + [
                pl.BlockSpec((spectra, GROUP, cells), lambda i, place, offset=offset: (0, offset + i, 0))
                for offset in offsets
            ]
            + [whole(a) for a in (*models_t, *gates)]
            + [pl.BlockSpec((1, 1, obs.shape[2]), lambda i, place: (first + i, 0, 0)), whole(cell_index)]
            + [whole(terms), whole(square)],
            out_specs=[whole(terms), whole(square)],
        ),
        out_shape=[
            jax.ShapeDtypeStruct(terms.shape, jnp.float32),
            jax.ShapeDtypeStruct(square.shape, jnp.float32),
        ],
        input_output_aliases={pieces + 7: 0, pieces + 8: 1},
        compiler_params=params(40),
        cost_estimate=cost(
            12 * pieces * spectra * rows * cells * members * 2, 4 * pieces * spectra * rows * cells
        ),
        name="chunk_step",
    )(place, block, *sens, *models_t, *gates, obs, cell_index, terms, square)


def exact_dot(a, b, dims):
    return lax.dot_general(a, b, dims, precision=HIGH, preferred_element_type=jnp.float32)


def gradient_kernel(tiles, owned, place_ref, borrowed_ref, got_ref, square_ref, out_ref):
    devices, slab, cells = got_ref.shape
    owners = devices // tiles
    block_cells = owned * owners
    members = square_ref.shape[0]
    sums = []
    for t in range(tiles):
        total = got_ref[t * owners]
        for f in range(1, owners):
            total = total + got_ref[t * owners + f]
        sums.append(total)
    gradient = []
    for b in range(tiles):
        block = sums[b][:, :block_cells]
        for t in range(tiles):
            block = block + jnp.where(borrowed_ref[place_ref[0] ^ t] == b, sums[t][:, block_cells:], 0.0)
        gradient.append(block)
    square = sum(jnp.sum(g * g, axis=1, keepdims=True) for g in gradient)
    scale = jnp.sqrt(square / (tiles * block_cells) + EPSILON)
    iota = lax.broadcasted_iota
    per_row = members // slab
    down = (iota(jnp.int32, (slab, members), 1) // per_row == iota(jnp.int32, (slab, members), 0))
    lane = iota(jnp.int32, (members, LANES), 1)
    spread = jnp.where(iota(jnp.int32, (members, LANES), 0) % per_row + owned == lane, square_ref[...], 0.0)
    rider = exact_dot(down.astype(jnp.float32), spread, NN)
    for b in range(tiles):
        step = gradient[b] / scale
        for f in range(owners):
            piece = step[:, f * owned : (f + 1) * owned]
            piece = jnp.concatenate([piece, jnp.zeros((slab, LANES - owned), jnp.float32)], axis=1)
            out_ref[b * owners + f] = piece + rider


def gradient_step(place, borrowed, got, square, tiles, owned):
    devices, slab, _ = got.shape
    return pl.pallas_call(
        functools.partial(gradient_kernel, tiles, owned),
        in_specs=[SCALARS] * 2 + [pl.BlockSpec(memory_space=pltpu.VMEM)] * 2,
        out_specs=pl.BlockSpec(memory_space=pltpu.VMEM),
        out_shape=jax.ShapeDtypeStruct((devices, slab, LANES), jnp.float32),
        compiler_params=params(16),
        cost_estimate=cost(1 << 22, 1 << 20),
        name="gradient_step",
    )(place, borrowed, got, square)


def update_kernel(divisor, models_ref, back_ref, updated_ref, misfit_ref):
    devices, slab, _ = back_ref.shape
    owned, members = models_ref.shape
    per_row = members // slab
    iota = lax.broadcasted_iota
    riders = back_ref[0]
    for d in range(1, devices):
        riders = riders + back_ref[d]
    down = (iota(jnp.int32, (slab, members), 1) // per_row == iota(jnp.int32, (slab, members), 0))
    tall = exact_dot(riders, down.astype(jnp.float32), (((0,), (0,)), ((), ())))
    mine = iota(jnp.int32, (LANES, members), 1) % per_row + owned == iota(jnp.int32, (LANES, members), 0)
    misfit = jnp.sum(jnp.where(mine, tall, 0.0), axis=0, keepdims=True) / divisor
    step = back_ref[...].reshape(members, LANES).T[:owned]
    updated_ref[...] = models_ref[...] - STEP_LENGTH * misfit * step
    misfit_ref[...] = misfit


def update(models, back, divisor):
    return pl.pallas_call(
        functools.partial(update_kernel, divisor),
        in_specs=[pl.BlockSpec(memory_space=pltpu.VMEM)] * 2,
        out_specs=[pl.BlockSpec(memory_space=pltpu.VMEM)] * 2,
        out_shape=[
            jax.ShapeDtypeStruct(models.shape, jnp.float32),
            jax.ShapeDtypeStruct((1, models.shape[1]), jnp.float32),
        ],
        compiler_params=params(16),
        cost_estimate=cost(1 << 20, 1 << 18),
        name="update",
    )(models, back)


def chunk_groups(groups):
    if groups < 16:
        return [1] * groups
    ends = [groups // 8, groups * 3 // 16, groups // 8, groups // 16]
    rest = groups - sum(ends)
    return [ends[0], rest - rest // 2, rest // 2] + ends[1:]


def body(sensitivity, models, observed, waveform, cell_index, gate_index):
    both = ("tile", "freq")
    tiles, owners, devices = lax.axis_size("tile"), lax.axis_size("freq"), lax.axis_size(both)
    _, own_freqs, parts, soundings, cells = sensitivity.shape
    freqs = own_freqs * owners
    spectra = own_freqs * parts
    owned, members = models.shape
    ncells = owned * devices
    gates = gate_index.shape[0]
    divisor = 2.0 * tiles * soundings * gates
    own = soundings // owners
    block_cells = owned * owners
    place = jnp.stack([lax.axis_index("tile"), lax.axis_index("freq")])

    block = sensitivity[0].reshape(spectra, soundings, cells)
    lanes = cells // members if owned % (GROUP * (cells // members)) == 0 else 1
    sizes = chunk_groups(own // GROUP)
    starts = [sum(sizes[:i]) for i in range(len(sizes))]
    distances = partner_order(owners)
    partners = [0] + distances
    received, offsets, done = [], [], []
    batches = [i for i in (0, 1, 3) if i < len(sizes)]
    near_by = {}

    def send(i):
        after = [received[i - 1][distances[0]]] if i else []
        if i > 2:
            after = after + done[i - 3 : i - 2]
        batch = max(b for b in batches if b <= i)
        end = starts[min([b for b in batches if b > i] + [len(starts)])] if batch != batches[-1] else own // GROUP
        parts = []
        for k in distances:
            if k >= owners // 2:
                parts.append((k, starts[i] * GROUP, sizes[i] * GROUP))
            elif batch == i:
                parts.append((k, starts[i] * GROUP, (end - starts[i]) * GROUP))
        pieces = pack(place, block, models, after, parts, own, 0 if i else lanes)
        got = {k: swap(p, "freq", k) for p, (k, _, _) in zip(pieces, parts)}
        near_by.update({k: p for k, p in got.items() if k < owners // 2})
        received.append({k: got.get(k, near_by.get(k)) for k in distances})
        offsets.append([0 if k >= owners // 2 else starts[i] - starts[batch] for k in distances])

    send(0)
    send(1)
    near = near_models(
        place, cell_index, models, [received[0][k] for k in distances], received[1][distances[2]], sizes[0] * GROUP, lanes
    )
    blocks = [near] + [swap(near, "tile", k) for k in range(1, tiles)]
    borrowed = jnp.stack([b[block_cells, 0] for b in blocks]).astype(jnp.int32)
    models_t = tile_models(place, cell_index, blocks, owned, partners)

    order = place[1] ^ jnp.array(partners, jnp.int32)
    wide = wide_table(gate_table(order, own_freqs, freqs, waveform, gate_index).T)
    obs = observed[0].reshape(gates, own // GROUP, GROUP)
    obs = jnp.swapaxes(obs, 0, 1).reshape(own // GROUP, 1, gates * GROUP)

    terms = jnp.zeros((members, cells), jnp.float32)
    square = jnp.zeros((members, LANES), jnp.float32)
    for i, start in enumerate(starts):
        if i > 1:
            send(i)
        last = i == len(starts) - 1
        terms, square = chunk_step(
            place, block, [received[i][k] for k in distances], offsets[i], start, sizes[i] * GROUP,
            models_t, wide, obs, cell_index, terms, square, block_cells, last,
        )
        done.append(square)

    slab = members // devices
    sent = terms.reshape(devices, slab, cells)
    got = lax.all_to_all(sent, both, split_axis=0, concat_axis=0, tiled=True)
    if slab % GROUP == 0 and members // slab + owned <= LANES:
        step = gradient_step(place, borrowed, got, square, tiles, owned)
        back = lax.all_to_all(step, both, split_axis=0, concat_axis=0, tiled=True)
        updated, misfit = update(models, back, divisor)
        return (updated, misfit.reshape(members))

    got = jnp.sum(got.reshape(tiles, owners, slab, cells), axis=1)
    tile_ids = jnp.arange(tiles)
    lent = (jnp.take(borrowed, tile_ids ^ place[0])[None, :] == tile_ids[:, None]).astype(jnp.float32)
    gradient = got[:, :, :block_cells] + jnp.sum(
        lent[:, :, None, None] * got[None, :, :, block_cells:], axis=1
    )
    scale = jnp.sqrt(jnp.sum(gradient * gradient, axis=(0, 2)) / ncells + EPSILON)
    step = gradient / scale[None, :, None]
    step = step.reshape(tiles, slab, owners, owned).transpose(0, 2, 1, 3)
    step = step.reshape(devices, slab, owned)
    rider = jnp.broadcast_to(square[:, 0].reshape(1, slab, devices), (devices, slab, devices))
    back = lax.all_to_all(
        jnp.concatenate([step, rider], axis=2), both, split_axis=0, concat_axis=0, tiled=True
    )
    misfit = jnp.sum(back[:, :, owned:], axis=0).reshape(members) / divisor
    back = back[:, :, :owned].reshape(members, owned)
    return (models - (STEP_LENGTH * misfit)[None, :] * back.T, misfit)


def solution(mesh):
    in_specs = (
        P("tile", "freq", None, None, None),
        P(("tile", "freq"), None),
        P("tile", None, "freq"),
        P(),
        P("tile", None),
        P(),
    )
    out_specs = (P(("tile", "freq"), None), P())
    return jax.shard_map(body, mesh=mesh, in_specs=in_specs, out_specs=out_specs, check_vma=False)
```

```python
import functools
import math

import jax
import jax.numpy as jnp
from jax import lax
from jax.experimental import pallas as pl
from jax.experimental.pallas import tpu as pltpu
from jax.sharding import PartitionSpec as P

HIGH = lax.Precision.HIGHEST
PHASE_RATE = 0.37
STEP_LENGTH = 0.5
EPSILON = 1e-06
GROUP = 8
LANES = 128

NN = (((1,), (0,)), ((), ()))
NT = (((1,), (1,)), ((), ()))


def swap(x, axis, k):
    return lax.ppermute(x, axis, [(i, i ^ k) for i in range(lax.axis_size(axis))])


def partner_order(size):
    assert size & (size - 1) == 0
    across, near = list(range(size // 2, size)), list(range(1, size // 2))[::-1]
    across = across[:1] + across[1:][::-1]
    return [k for pair in zip(across, near + [None]) for k in pair if k is not None]


def gate_table(owner_order, own_freqs, freqs, waveform, gate_index):
    samples = waveform.shape[0]
    freq_ids = (owner_order[:, None] * own_freqs + jnp.arange(own_freqs)[None, :]).reshape(freqs)
    freq_col = freq_ids.astype(jnp.float32)[:, None] + 0.5
    time_row = jnp.arange(samples, dtype=jnp.float32)[None, :] + 0.5
    phases = PHASE_RATE * freq_col * time_row
    kernel = jnp.stack([jnp.cos(phases), jnp.sin(phases)], axis=1) / math.sqrt(freqs)
    steps = jnp.arange(samples)
    lag = gate_index[:, None] - steps[None, :]
    picked = jnp.sum(
        jnp.where(lag[:, :, None] == steps[None, None, :], waveform[None, None, :], 0.0), axis=-1
    )
    return jnp.einsum("gk,fpk->gfp", picked, kernel, precision=HIGH).reshape(gate_index.shape[0], freqs * 2)


def split(x):
    high = x.astype(jnp.bfloat16)
    return high, (x - high.astype(jnp.float32)).astype(jnp.bfloat16)


def three_pass(a, b, dims):
    dot = functools.partial(lax.dot_general, dimension_numbers=dims, preferred_element_type=jnp.float32)
    return dot(a[0], b[0]) + (dot(a[0], b[1]) + dot(a[1], b[0]))


def params(mebibytes):
    return pltpu.CompilerParams(vmem_limit_bytes=mebibytes * 1024 * 1024)


def cost(flops, bytes_accessed):
    return pl.CostEstimate(flops=flops, bytes_accessed=bytes_accessed, transcendentals=0)


def whole(a):
    return pl.BlockSpec(a.shape, lambda *_: (0,) * a.ndim)


HBM = pl.BlockSpec(memory_space=pltpu.HBM)
SCALARS = pl.BlockSpec(memory_space=pltpu.SMEM)


def pack_kernel(parts, own, lanes, place_ref, block_ref, models_ref, *refs):
    outs, held = refs[-2 * len(parts) - 2 : -len(parts) - 2], refs[-len(parts) - 2 : -2]
    in_sems, out_sems = refs[-2:]
    spectra = block_ref.shape[0]
    owned, members = models_ref.shape
    arrivals, departures = [], []
    for j, (k, first, rows) in enumerate(parts):
        row = pl.multiple_of((place_ref[1] ^ k) * own + first, GROUP)
        source, target = block_ref.at[:, pl.ds(row, rows)], held[j].at[pl.ds(0, spectra)]
        arrivals.append(pltpu.make_async_copy(source, target, in_sems.at[j]))
        departures.append(pltpu.make_async_copy(held[j], outs[j], out_sems.at[j]))
        arrivals[j].start()
    for j in range(len(parts)):
        for lane in range(lanes):
            part = owned // lanes
            held[j][spectra, pl.ds(0, part), pl.ds(lane * members, members)] = models_ref[pl.ds(lane * part, part), :]
    for arrival, departure in zip(arrivals, departures):
        arrival.wait()
        departure.start()
    for departure in departures:
        departure.wait()


def pack(place, block, models, after, parts, own, lanes):
    spectra, _, cells = block.shape
    shapes = [(spectra + (lanes > 0), rows, cells) for _, _, rows in parts]
    return pl.pallas_call(
        functools.partial(pack_kernel, parts, own, lanes),
        in_specs=[SCALARS, HBM, pl.BlockSpec(memory_space=pltpu.VMEM)] + [HBM] * len(after),
        out_specs=[HBM] * len(parts),
        out_shape=[jax.ShapeDtypeStruct(shape, jnp.float32) for shape in shapes],
        scratch_shapes=[pltpu.VMEM(shape, jnp.float32) for shape in shapes]
        + [pltpu.SemaphoreType.DMA((len(parts),)), pltpu.SemaphoreType.DMA((len(parts),))],
        compiler_params=params(48),
        cost_estimate=cost(0, 8 * spectra * cells * sum(rows for _, _, rows in parts)),
        name="pack",
    )(place, block, models, *after)


def near_kernel(lanes, place_ref, cells_ref, models_ref, *refs):
    riders, out_ref = refs[:-2], refs[-1]
    owned, members = models_ref.shape
    part = owned // lanes
    out_ref[pl.ds(0, owned), :] = models_ref[...]
    for j, r in enumerate(riders):
        for lane in range(lanes):
            out_ref[pl.ds((j + 1) * owned + lane * part, part), :] = r[
                0, pl.ds(0, part), pl.ds(lane * members, members)
            ]
    block_cells = owned * (len(riders) + 1)
    home = cells_ref[...] // block_cells
    other = jnp.where(home == place_ref[0], -1, home).astype(jnp.float32)
    other = jnp.max(other, axis=1, keepdims=True)
    out_ref[pl.ds(block_cells, GROUP), :] = jnp.broadcast_to(other, (GROUP, members))


def near_models(place, cell_index, models, first, after, rows, lanes):
    owned, members = models.shape
    slabs, _, cells = first[0].shape
    rider = pl.BlockSpec((1, rows, cells), lambda i: (slabs - 1, 0, 0))
    return pl.pallas_call(
        functools.partial(near_kernel, lanes),
        grid=(1,),
        in_specs=[SCALARS, whole(cell_index), whole(models)] + [rider] * len(first) + [HBM],
        out_specs=pl.BlockSpec((owned * (len(first) + 1) + GROUP, members), lambda i: (0, 0)),
        out_shape=jax.ShapeDtypeStruct((owned * (len(first) + 1) + GROUP, members), jnp.float32),
        compiler_params=params(16),
        cost_estimate=cost(0, 1 << 20),
        name="near_models",
    )(place, cell_index, models, *first, after)


def tile_models_kernel(owned, partners, place_ref, cells_ref, *refs):
    tile_refs, (high_ref, low_ref) = refs[:-2], refs[-2:]
    block_cells = owned * len(partners)
    cells = cells_ref[...]
    distance = (cells // owned % len(partners)) ^ place_ref[1]
    slot = jnp.zeros_like(cells)
    for n, k in enumerate(partners):
        slot = jnp.where(distance == k, n, slot)
    spot = slot * owned + cells % owned
    away = (cells // block_cells) ^ place_ref[0]
    high, low = None, None
    for k, ref in enumerate(tile_refs):
        row = lax.broadcasted_iota(jnp.int32, (block_cells, cells.shape[1]), 0)
        pick = jnp.where((row == spot) & (away == k), 1.0, 0.0).astype(jnp.bfloat16)
        h, l = split(ref[pl.ds(0, block_cells), :].T)
        h = lax.dot_general(h, pick, NN, preferred_element_type=jnp.float32)
        l = lax.dot_general(l, pick, NN, preferred_element_type=jnp.float32)
        high, low = (h, l) if k == 0 else (high + h, low + l)
    high_ref[...] = high.astype(jnp.bfloat16)
    low_ref[...] = low.astype(jnp.bfloat16)


def tile_models(place, cell_index, tiles, owned, partners):
    shape = jax.ShapeDtypeStruct((tiles[0].shape[1], cell_index.shape[1]), jnp.bfloat16)
    return pl.pallas_call(
        functools.partial(tile_models_kernel, owned, partners),
        in_specs=[SCALARS] + [pl.BlockSpec(memory_space=pltpu.VMEM)] * (1 + len(tiles)),
        out_specs=[pl.BlockSpec(memory_space=pltpu.VMEM)] * 2,
        out_shape=[shape] * 2,
        compiler_params=params(16),
        cost_estimate=cost(1 << 30, 2 << 20),
        name="tile_models",
    )(place, cell_index, *tiles)


def wide_kernel(table_ref, high_ref, low_ref):
    fp, gates = table_ref.shape
    rows, columns = high_ref.shape
    iota = lax.broadcasted_iota
    down = (iota(jnp.int32, (rows, fp), 0) // GROUP == iota(jnp.int32, (rows, fp), 1)).astype(jnp.float32)
    across = iota(jnp.int32, (gates, columns), 1) // GROUP == iota(jnp.int32, (gates, columns), 0)
    across = across.astype(jnp.float32).astype(jnp.bfloat16)
    down = down.astype(jnp.bfloat16)
    same = iota(jnp.int32, (rows, columns), 0) % GROUP == iota(jnp.int32, (rows, columns), 1) % GROUP
    for part, ref in zip(split(table_ref[...]), (high_ref, low_ref)):
        tall = lax.dot_general(down, part, NN, preferred_element_type=jnp.float32).astype(jnp.bfloat16)
        full = lax.dot_general(tall, across, NN, preferred_element_type=jnp.float32)
        ref[...] = jnp.where(same, full, 0.0).astype(jnp.bfloat16)


def wide_table(table):
    shape = jax.ShapeDtypeStruct((table.shape[0] * GROUP, table.shape[1] * GROUP), jnp.bfloat16)
    return pl.pallas_call(
        wide_kernel,
        in_specs=[pl.BlockSpec(memory_space=pltpu.VMEM)],
        out_specs=[pl.BlockSpec(memory_space=pltpu.VMEM)] * 2,
        out_shape=[shape] * 2,
        compiler_params=params(16),
        cost_estimate=cost(1 << 28, 1 << 20),
        name="wide_table",
    )(table)


def chunk_kernel(pieces, block_cells, last, place_ref, *refs):
    sens_refs = refs[:pieces]
    model_h, model_l, gate_h, gate_l, obs_ref, cells_ref, terms_in, square_in, terms_ref, square_ref = refs[pieces:]

    @pl.when(pl.program_id(0) == 0)
    def _():
        terms_ref[...] = terms_in[...]
        square_ref[...] = square_in[...]

    sens = [split(r[...].reshape(r.shape[0] * r.shape[1], r.shape[2])) for r in sens_refs]
    sens = tuple(jnp.concatenate([s[i] for s in sens], axis=0) for i in range(2))
    gates = (gate_h[...], gate_l[...])
    predicted = three_pass((model_h[...], model_l[...]), sens, NT)
    misfit_rows = three_pass(split(predicted), gates, NN) - obs_ref[0]
    square_ref[...] += jnp.sum(misfit_rows * misfit_rows, axis=1, keepdims=True)
    back = three_pass(split(misfit_rows), gates, NT)
    terms = terms_ref[...] + three_pass(split(back), sens, NN)
    terms_ref[...] = terms

    if last:

        @pl.when(pl.program_id(0) == pl.num_programs(0) - 1)
        def _():
            cells = cells_ref[...]
            spot = cells % block_cells + jnp.where(cells // block_cells == place_ref[0], 0, block_cells)
            size = cells.shape[1]
            row = lax.broadcasted_iota(jnp.int32, (size, size), 0)
            pick = jnp.where(row == spot, 1.0, 0.0).astype(jnp.bfloat16)
            high = terms.astype(jnp.bfloat16)
            middle, low = split(terms - high.astype(jnp.float32))
            dot = functools.partial(lax.dot_general, dimension_numbers=NT, preferred_element_type=jnp.float32)
            terms_ref[...] = dot(high, pick) + (dot(middle, pick) + dot(low, pick))


def chunk_step(place, block, sens, offsets, first, rows, models_t, gates, obs, cell_index, terms, square, block_cells, last):
    spectra, soundings, cells = block.shape
    pieces = len(sens) + 1
    members = terms.shape[0]
    own_groups = soundings // (pieces * GROUP)
    return pl.pallas_call(
        functools.partial(chunk_kernel, pieces, block_cells, last),
        grid_spec=pltpu.PrefetchScalarGridSpec(
            num_scalar_prefetch=1,
            grid=(rows // GROUP,),
            in_specs=[
                pl.BlockSpec((spectra, GROUP, cells), lambda i, place: (0, place[1] * own_groups + first + i, 0))
            ]
            + [
                pl.BlockSpec((spectra, GROUP, cells), lambda i, place, offset=offset: (0, offset + i, 0))
                for offset in offsets
            ]
            + [whole(a) for a in (*models_t, *gates)]
            + [pl.BlockSpec((1, 1, obs.shape[2]), lambda i, place: (first + i, 0, 0)), whole(cell_index)]
            + [whole(terms), whole(square)],
            out_specs=[whole(terms), whole(square)],
        ),
        out_shape=[
            jax.ShapeDtypeStruct(terms.shape, jnp.float32),
            jax.ShapeDtypeStruct(square.shape, jnp.float32),
        ],
        input_output_aliases={pieces + 7: 0, pieces + 8: 1},
        compiler_params=params(40),
        cost_estimate=cost(
            12 * pieces * spectra * rows * cells * members * 2, 4 * pieces * spectra * rows * cells
        ),
        name="chunk_step",
    )(place, block, *sens, *models_t, *gates, obs, cell_index, terms, square)


def exact_dot(a, b, dims):
    return lax.dot_general(a, b, dims, precision=HIGH, preferred_element_type=jnp.float32)


def gradient_kernel(tiles, owned, place_ref, borrowed_ref, got_ref, square_ref, out_ref):
    devices, slab, cells = got_ref.shape
    owners = devices // tiles
    block_cells = owned * owners
    members = square_ref.shape[0]
    sums = []
    for t in range(tiles):
        total = got_ref[t * owners]
        for f in range(1, owners):
            total = total + got_ref[t * owners + f]
        sums.append(total)
    gradient = []
    for b in range(tiles):
        block = sums[b][:, :block_cells]
        for t in range(tiles):
            block = block + jnp.where(borrowed_ref[place_ref[0] ^ t] == b, sums[t][:, block_cells:], 0.0)
        gradient.append(block)
    square = sum(jnp.sum(g * g, axis=1, keepdims=True) for g in gradient)
    scale = jnp.sqrt(square / (tiles * block_cells) + EPSILON)
    iota = lax.broadcasted_iota
    per_row = members // slab
    down = (iota(jnp.int32, (slab, members), 1) // per_row == iota(jnp.int32, (slab, members), 0))
    lane = iota(jnp.int32, (members, LANES), 1)
    spread = jnp.where(iota(jnp.int32, (members, LANES), 0) % per_row + owned == lane, square_ref[...], 0.0)
    rider = exact_dot(down.astype(jnp.float32), spread, NN)
    for b in range(tiles):
        step = gradient[b] / scale
        for f in range(owners):
            piece = step[:, f * owned : (f + 1) * owned]
            piece = jnp.concatenate([piece, jnp.zeros((slab, LANES - owned), jnp.float32)], axis=1)
            out_ref[b * owners + f] = piece + rider


def gradient_step(place, borrowed, got, square, tiles, owned):
    devices, slab, _ = got.shape
    return pl.pallas_call(
        functools.partial(gradient_kernel, tiles, owned),
        in_specs=[SCALARS] * 2 + [pl.BlockSpec(memory_space=pltpu.VMEM)] * 2,
        out_specs=pl.BlockSpec(memory_space=pltpu.VMEM),
        out_shape=jax.ShapeDtypeStruct((devices, slab, LANES), jnp.float32),
        compiler_params=params(16),
        cost_estimate=cost(1 << 22, 1 << 20),
        name="gradient_step",
    )(place, borrowed, got, square)


def update_kernel(divisor, models_ref, back_ref, updated_ref, misfit_ref):
    devices, slab, _ = back_ref.shape
    owned, members = models_ref.shape
    per_row = members // slab
    iota = lax.broadcasted_iota
    riders = back_ref[0]
    for d in range(1, devices):
        riders = riders + back_ref[d]
    down = (iota(jnp.int32, (slab, members), 1) // per_row == iota(jnp.int32, (slab, members), 0))
    tall = exact_dot(riders, down.astype(jnp.float32), (((0,), (0,)), ((), ())))
    mine = iota(jnp.int32, (LANES, members), 1) % per_row + owned == iota(jnp.int32, (LANES, members), 0)
    misfit = jnp.sum(jnp.where(mine, tall, 0.0), axis=0, keepdims=True) / divisor
    step = back_ref[...].reshape(members, LANES).T[:owned]
    updated_ref[...] = models_ref[...] - STEP_LENGTH * misfit * step
    misfit_ref[...] = misfit


def update(models, back, divisor):
    return pl.pallas_call(
        functools.partial(update_kernel, divisor),
        in_specs=[pl.BlockSpec(memory_space=pltpu.VMEM)] * 2,
        out_specs=[pl.BlockSpec(memory_space=pltpu.VMEM)] * 2,
        out_shape=[
            jax.ShapeDtypeStruct(models.shape, jnp.float32),
            jax.ShapeDtypeStruct((1, models.shape[1]), jnp.float32),
        ],
        compiler_params=params(16),
        cost_estimate=cost(1 << 20, 1 << 18),
        name="update",
    )(models, back)


def chunk_groups(groups):
    if groups < 16:
        return [1] * groups
    ends = [groups // 8, groups * 3 // 16, groups // 8, groups // 16]
    rest = groups - sum(ends)
    return [ends[0], rest - rest // 2, rest // 2] + ends[1:]


def body(sensitivity, models, observed, waveform, cell_index, gate_index):
    both = ("tile", "freq")
    tiles, owners, devices = lax.axis_size("tile"), lax.axis_size("freq"), lax.axis_size(both)
    _, own_freqs, parts, soundings, cells = sensitivity.shape
    freqs = own_freqs * owners
    spectra = own_freqs * parts
    owned, members = models.shape
    ncells = owned * devices
    gates = gate_index.shape[0]
    divisor = 2.0 * tiles * soundings * gates
    own = soundings // owners
    block_cells = owned * owners
    place = jnp.stack([lax.axis_index("tile"), lax.axis_index("freq")])

    block = sensitivity[0].reshape(spectra, soundings, cells)
    lanes = cells // members if owned % (GROUP * (cells // members)) == 0 else 1
    sizes = chunk_groups(own // GROUP)
    starts = [sum(sizes[:i]) for i in range(len(sizes))]
    distances = partner_order(owners)
    partners = [0] + distances
    received, offsets, done = [], [], []
    batches = list(range(max(1, len(sizes) - 1)))
    near_by = {}

    def send(i):
        after = [received[i - 1][distances[0]]] if i else []
        if i > 2:
            behind = min(i - 2, len(sizes) - 4)
            after = after + done[behind : behind + 1]
        batch = max(b for b in batches if b <= i)
        end = starts[min([b for b in batches if b > i] + [len(starts)])] if batch != batches[-1] else own // GROUP
        parts = []
        for k in distances:
            if k >= owners // 2:
                parts.append((k, starts[i] * GROUP, sizes[i] * GROUP))
            elif batch == i:
                parts.append((k, starts[i] * GROUP, (end - starts[i]) * GROUP))
        pieces = pack(place, block, models, after, parts, own, 0 if i else lanes)
        got = {k: swap(p, "freq", k) for p, (k, _, _) in zip(pieces, parts)}
        near_by.update({k: p for k, p in got.items() if k < owners // 2})
        received.append({k: got.get(k, near_by.get(k)) for k in distances})
        offsets.append([0 if k >= owners // 2 else starts[i] - starts[batch] for k in distances])

    send(0)
    send(1)
    near = near_models(
        place, cell_index, models, [received[0][k] for k in distances], received[0][distances[0]], sizes[0] * GROUP, lanes
    )
    blocks = [near] + [swap(near, "tile", k) for k in range(1, tiles)]
    borrowed = jnp.stack([b[block_cells, 0] for b in blocks]).astype(jnp.int32)
    models_t = tile_models(place, cell_index, blocks, owned, partners)

    order = place[1] ^ jnp.array(partners, jnp.int32)
    wide = wide_table(gate_table(order, own_freqs, freqs, waveform, gate_index).T)
    obs = observed[0].reshape(gates, own // GROUP, GROUP)
    obs = jnp.swapaxes(obs, 0, 1).reshape(own // GROUP, 1, gates * GROUP)

    terms = jnp.zeros((members, cells), jnp.float32)
    square = jnp.zeros((members, LANES), jnp.float32)
    for i, start in enumerate(starts):
        if i > 1:
            send(i)
        last = i == len(starts) - 1
        terms, square = chunk_step(
            place, block, [received[i][k] for k in distances], offsets[i], start, sizes[i] * GROUP,
            models_t, wide, obs, cell_index, terms, square, block_cells, last,
        )
        done.append(square)

    slab = members // devices
    sent = terms.reshape(devices, slab, cells)
    got = lax.all_to_all(sent, both, split_axis=0, concat_axis=0, tiled=True)
    if slab % GROUP == 0 and members // slab + owned <= LANES:
        step = gradient_step(place, borrowed, got, square, tiles, owned)
        back = lax.all_to_all(step, both, split_axis=0, concat_axis=0, tiled=True)
        updated, misfit = update(models, back, divisor)
        return (updated, misfit.reshape(members))

    got = jnp.sum(got.reshape(tiles, owners, slab, cells), axis=1)
    tile_ids = jnp.arange(tiles)
    lent = (jnp.take(borrowed, tile_ids ^ place[0])[None, :] == tile_ids[:, None]).astype(jnp.float32)
    gradient = got[:, :, :block_cells] + jnp.sum(
        lent[:, :, None, None] * got[None, :, :, block_cells:], axis=1
    )
    scale = jnp.sqrt(jnp.sum(gradient * gradient, axis=(0, 2)) / ncells + EPSILON)
    step = gradient / scale[None, :, None]
    step = step.reshape(tiles, slab, owners, owned).transpose(0, 2, 1, 3)
    step = step.reshape(devices, slab, owned)
    rider = jnp.broadcast_to(square[:, 0].reshape(1, slab, devices), (devices, slab, devices))
    back = lax.all_to_all(
        jnp.concatenate([step, rider], axis=2), both, split_axis=0, concat_axis=0, tiled=True
    )
    misfit = jnp.sum(back[:, :, owned:], axis=0).reshape(members) / divisor
    back = back[:, :, :owned].reshape(members, owned)
    return (models - (STEP_LENGTH * misfit)[None, :] * back.T, misfit)


def solution(mesh):
    in_specs = (
        P("tile", "freq", None, None, None),
        P(("tile", "freq"), None),
        P("tile", None, "freq"),
        P(),
        P("tile", None),
        P(),
    )
    out_specs = (P(("tile", "freq"), None), P())
    return jax.shard_map(body, mesh=mesh, in_specs=in_specs, out_specs=out_specs, check_vma=False)
```

```python
import functools
import math

import jax
import jax.numpy as jnp
from jax import lax
from jax.experimental import pallas as pl
from jax.experimental.pallas import tpu as pltpu
from jax.sharding import PartitionSpec as P

HIGH = lax.Precision.HIGHEST
PHASE_RATE = 0.37
STEP_LENGTH = 0.5
EPSILON = 1e-06
GROUP = 8
LANES = 128

NN = (((1,), (0,)), ((), ()))
NT = (((1,), (1,)), ((), ()))


def swap(x, axis, k):
    return lax.ppermute(x, axis, [(i, i ^ k) for i in range(lax.axis_size(axis))])


def partner_order(size):
    assert size & (size - 1) == 0
    half = size // 2
    pairs = zip(range(size - 1, half, -1), range(half - 1, 0, -1))
    return [half] + [k for pair in pairs for k in pair]


def gate_table(owner_order, own_freqs, freqs, waveform, gate_index):
    samples = waveform.shape[0]
    freq_ids = (owner_order[:, None] * own_freqs + jnp.arange(own_freqs)[None, :]).reshape(freqs)
    freq_col = freq_ids.astype(jnp.float32)[:, None] + 0.5
    time_row = jnp.arange(samples, dtype=jnp.float32)[None, :] + 0.5
    phases = PHASE_RATE * freq_col * time_row
    kernel = jnp.stack([jnp.cos(phases), jnp.sin(phases)], axis=1) / math.sqrt(freqs)
    steps = jnp.arange(samples)
    lag = gate_index[:, None] - steps[None, :]
    picked = jnp.sum(
        jnp.where(lag[:, :, None] == steps[None, None, :], waveform[None, None, :], 0.0), axis=-1
    )
    return jnp.einsum("gk,fpk->gfp", picked, kernel, precision=HIGH).reshape(gate_index.shape[0], freqs * 2)


def split(x):
    high = x.astype(jnp.bfloat16)
    return high, (x - high.astype(jnp.float32)).astype(jnp.bfloat16)


def three_pass(a, b, dims):
    dot = functools.partial(lax.dot_general, dimension_numbers=dims, preferred_element_type=jnp.float32)
    return dot(a[0], b[0]) + (dot(a[0], b[1]) + dot(a[1], b[0]))


def params(mebibytes):
    return pltpu.CompilerParams(vmem_limit_bytes=mebibytes * 1024 * 1024)


def cost(flops, bytes_accessed):
    return pl.CostEstimate(flops=flops, bytes_accessed=bytes_accessed, transcendentals=0)


def whole(a):
    return pl.BlockSpec(a.shape, lambda *_: (0,) * a.ndim)


HBM = pl.BlockSpec(memory_space=pltpu.HBM)
SCALARS = pl.BlockSpec(memory_space=pltpu.SMEM)


def pack_kernel(distances, own, first, rows, lanes, place_ref, block_ref, models_ref, *refs):
    outs, (held, in_sems, out_sems) = refs[-len(distances) - 3 : -3], refs[-3:]
    spectra = block_ref.shape[0]
    owned, members = models_ref.shape
    arrivals, departures = [], []
    for j, k in enumerate(distances):
        row = pl.multiple_of((place_ref[1] ^ k) * own + first, GROUP)
        source, target = block_ref.at[:, pl.ds(row, rows)], held.at[j, pl.ds(0, spectra)]
        arrivals.append(pltpu.make_async_copy(source, target, in_sems.at[j]))
        departures.append(pltpu.make_async_copy(held.at[j], outs[j], out_sems.at[j]))
        arrivals[j].start()
    for j in range(len(distances)):
        for lane in range(lanes):
            part = owned // lanes
            held[j, spectra, pl.ds(0, part), pl.ds(lane * members, members)] = models_ref[pl.ds(lane * part, part), :]
    for arrival, departure in zip(arrivals, departures):
        arrival.wait()
        departure.start()
    for departure in departures:
        departure.wait()


def pack(place, block, models, after, distances, own, first, rows, lanes):
    spectra, _, cells = block.shape
    count = len(distances)
    shape = (spectra + (lanes > 0), rows, cells)
    return pl.pallas_call(
        functools.partial(pack_kernel, distances, own, first, rows, lanes),
        in_specs=[SCALARS, HBM, pl.BlockSpec(memory_space=pltpu.VMEM)] + [HBM] * len(after),
        out_specs=[HBM] * count,
        out_shape=[jax.ShapeDtypeStruct(shape, jnp.float32)] * count,
        scratch_shapes=[
            pltpu.VMEM((count, *shape), jnp.float32),
            pltpu.SemaphoreType.DMA((count,)),
            pltpu.SemaphoreType.DMA((count,)),
        ],
        compiler_params=params(48),
        cost_estimate=cost(0, 8 * count * spectra * rows * cells),
        name="pack",
    )(place, block, models, *after)


def near_kernel(lanes, place_ref, cells_ref, models_ref, *refs):
    riders, out_ref = refs[:-1], refs[-1]
    owned, members = models_ref.shape
    part = owned // lanes
    out_ref[pl.ds(0, owned), :] = models_ref[...]
    for j, r in enumerate(riders):
        for lane in range(lanes):
            out_ref[pl.ds((j + 1) * owned + lane * part, part), :] = r[
                0, pl.ds(0, part), pl.ds(lane * members, members)
            ]
    block_cells = owned * (len(riders) + 1)
    home = cells_ref[...] // block_cells
    other = jnp.where(home == place_ref[0], -1, home).astype(jnp.float32)
    other = jnp.max(other, axis=1, keepdims=True)
    out_ref[pl.ds(block_cells, GROUP), :] = jnp.broadcast_to(other, (GROUP, members))


def near_models(place, cell_index, models, first, lanes):
    owned, members = models.shape
    slabs, rows, cells = first[0].shape
    rider = pl.BlockSpec((1, rows, cells), lambda i: (slabs - 1, 0, 0))
    return pl.pallas_call(
        functools.partial(near_kernel, lanes),
        grid=(1,),
        in_specs=[SCALARS, whole(cell_index), whole(models)] + [rider] * len(first),
        out_specs=pl.BlockSpec((owned * (len(first) + 1) + GROUP, members), lambda i: (0, 0)),
        out_shape=jax.ShapeDtypeStruct((owned * (len(first) + 1) + GROUP, members), jnp.float32),
        compiler_params=params(16),
        cost_estimate=cost(0, 1 << 20),
        name="near_models",
    )(place, cell_index, models, *first)


def tile_models_kernel(owned, partners, place_ref, cells_ref, *refs):
    tile_refs, (high_ref, low_ref) = refs[:-2], refs[-2:]
    block_cells = owned * len(partners)
    cells = cells_ref[...]
    distance = (cells // owned % len(partners)) ^ place_ref[1]
    slot = jnp.zeros_like(cells)
    for n, k in enumerate(partners):
        slot = jnp.where(distance == k, n, slot)
    spot = slot * owned + cells % owned
    away = (cells // block_cells) ^ place_ref[0]
    high, low = None, None
    for k, ref in enumerate(tile_refs):
        row = lax.broadcasted_iota(jnp.int32, (block_cells, cells.shape[1]), 0)
        pick = jnp.where((row == spot) & (away == k), 1.0, 0.0).astype(jnp.bfloat16)
        h, l = split(ref[pl.ds(0, block_cells), :].T)
        h = lax.dot_general(h, pick, NN, preferred_element_type=jnp.float32)
        l = lax.dot_general(l, pick, NN, preferred_element_type=jnp.float32)
        high, low = (h, l) if k == 0 else (high + h, low + l)
    high_ref[...] = high.astype(jnp.bfloat16)
    low_ref[...] = low.astype(jnp.bfloat16)


def tile_models(place, cell_index, tiles, owned, partners):
    shape = jax.ShapeDtypeStruct((tiles[0].shape[1], cell_index.shape[1]), jnp.bfloat16)
    return pl.pallas_call(
        functools.partial(tile_models_kernel, owned, partners),
        in_specs=[SCALARS] + [pl.BlockSpec(memory_space=pltpu.VMEM)] * (1 + len(tiles)),
        out_specs=[pl.BlockSpec(memory_space=pltpu.VMEM)] * 2,
        out_shape=[shape] * 2,
        compiler_params=params(16),
        cost_estimate=cost(1 << 30, 2 << 20),
        name="tile_models",
    )(place, cell_index, *tiles)


def wide_kernel(table_ref, high_ref, low_ref):
    fp, gates = table_ref.shape
    rows, columns = high_ref.shape
    iota = lax.broadcasted_iota
    down = (iota(jnp.int32, (rows, fp), 0) // GROUP == iota(jnp.int32, (rows, fp), 1)).astype(jnp.float32)
    across = iota(jnp.int32, (gates, columns), 1) // GROUP == iota(jnp.int32, (gates, columns), 0)
    across = across.astype(jnp.float32).astype(jnp.bfloat16)
    down = down.astype(jnp.bfloat16)
    same = iota(jnp.int32, (rows, columns), 0) % GROUP == iota(jnp.int32, (rows, columns), 1) % GROUP
    for part, ref in zip(split(table_ref[...]), (high_ref, low_ref)):
        tall = lax.dot_general(down, part, NN, preferred_element_type=jnp.float32).astype(jnp.bfloat16)
        full = lax.dot_general(tall, across, NN, preferred_element_type=jnp.float32)
        ref[...] = jnp.where(same, full, 0.0).astype(jnp.bfloat16)


def wide_table(table):
    shape = jax.ShapeDtypeStruct((table.shape[0] * GROUP, table.shape[1] * GROUP), jnp.bfloat16)
    return pl.pallas_call(
        wide_kernel,
        in_specs=[pl.BlockSpec(memory_space=pltpu.VMEM)],
        out_specs=[pl.BlockSpec(memory_space=pltpu.VMEM)] * 2,
        out_shape=[shape] * 2,
        compiler_params=params(16),
        cost_estimate=cost(1 << 28, 1 << 20),
        name="wide_table",
    )(table)


def chunk_kernel(pieces, block_cells, last, place_ref, *refs):
    sens_refs = refs[:pieces]
    model_h, model_l, gate_h, gate_l, obs_ref, cells_ref, terms_in, square_in, terms_ref, square_ref = refs[pieces:]

    @pl.when(pl.program_id(0) == 0)
    def _():
        terms_ref[...] = terms_in[...]
        square_ref[...] = square_in[...]

    sens = [split(r[...].reshape(r.shape[0] * r.shape[1], r.shape[2])) for r in sens_refs]
    sens = tuple(jnp.concatenate([s[i] for s in sens], axis=0) for i in range(2))
    gates = (gate_h[...], gate_l[...])
    predicted = three_pass((model_h[...], model_l[...]), sens, NT)
    misfit_rows = three_pass(split(predicted), gates, NN) - obs_ref[0]
    square_ref[...] += jnp.sum(misfit_rows * misfit_rows, axis=1, keepdims=True)
    back = three_pass(split(misfit_rows), gates, NT)
    terms = terms_ref[...] + three_pass(split(back), sens, NN)
    terms_ref[...] = terms

    if last:

        @pl.when(pl.program_id(0) == pl.num_programs(0) - 1)
        def _():
            cells = cells_ref[...]
            spot = cells % block_cells + jnp.where(cells // block_cells == place_ref[0], 0, block_cells)
            size = cells.shape[1]
            row = lax.broadcasted_iota(jnp.int32, (size, size), 0)
            pick = jnp.where(row == spot, 1.0, 0.0).astype(jnp.bfloat16)
            high = terms.astype(jnp.bfloat16)
            middle, low = split(terms - high.astype(jnp.float32))
            dot = functools.partial(lax.dot_general, dimension_numbers=NT, preferred_element_type=jnp.float32)
            terms_ref[...] = dot(high, pick) + (dot(middle, pick) + dot(low, pick))


def chunk_step(place, block, sens, first, models_t, gates, obs, cell_index, terms, square, block_cells, last):
    spectra, soundings, cells = block.shape
    rows = sens[0].shape[1]
    pieces = len(sens) + 1
    members = terms.shape[0]
    own_groups = soundings // (pieces * GROUP)
    return pl.pallas_call(
        functools.partial(chunk_kernel, pieces, block_cells, last),
        grid_spec=pltpu.PrefetchScalarGridSpec(
            num_scalar_prefetch=1,
            grid=(rows // GROUP,),
            in_specs=[
                pl.BlockSpec((spectra, GROUP, cells), lambda i, place: (0, place[1] * own_groups + first + i, 0))
            ]
            + [pl.BlockSpec((spectra, GROUP, cells), lambda i, place: (0, i, 0))] * len(sens)
            + [whole(a) for a in (*models_t, *gates)]
            + [pl.BlockSpec((1, 1, obs.shape[2]), lambda i, place: (first + i, 0, 0)), whole(cell_index)]
            + [whole(terms), whole(square)],
            out_specs=[whole(terms), whole(square)],
        ),
        out_shape=[
            jax.ShapeDtypeStruct(terms.shape, jnp.float32),
            jax.ShapeDtypeStruct(square.shape, jnp.float32),
        ],
        input_output_aliases={pieces + 7: 0, pieces + 8: 1},
        compiler_params=params(40),
        cost_estimate=cost(
            12 * pieces * spectra * rows * cells * members * 2, 4 * pieces * spectra * rows * cells
        ),
        name="chunk_step",
    )(place, block, *sens, *models_t, *gates, obs, cell_index, terms, square)


def exact_dot(a, b, dims):
    return lax.dot_general(a, b, dims, precision=HIGH, preferred_element_type=jnp.float32)


def gradient_kernel(tiles, owned, place_ref, borrowed_ref, got_ref, square_ref, out_ref):
    devices, slab, cells = got_ref.shape
    owners = devices // tiles
    block_cells = owned * owners
    members = square_ref.shape[0]
    sums = []
    for t in range(tiles):
        total = got_ref[t * owners]
        for f in range(1, owners):
            total = total + got_ref[t * owners + f]
        sums.append(total)
    gradient = []
    for b in range(tiles):
        block = sums[b][:, :block_cells]
        for t in range(tiles):
            block = block + jnp.where(borrowed_ref[place_ref[0] ^ t] == b, sums[t][:, block_cells:], 0.0)
        gradient.append(block)
    square = sum(jnp.sum(g * g, axis=1, keepdims=True) for g in gradient)
    scale = jnp.sqrt(square / (tiles * block_cells) + EPSILON)
    iota = lax.broadcasted_iota
    per_row = members // slab
    down = (iota(jnp.int32, (slab, members), 1) // per_row == iota(jnp.int32, (slab, members), 0))
    lane = iota(jnp.int32, (members, LANES), 1)
    spread = jnp.where(iota(jnp.int32, (members, LANES), 0) % per_row + owned == lane, square_ref[...], 0.0)
    rider = exact_dot(down.astype(jnp.float32), spread, NN)
    for b in range(tiles):
        step = gradient[b] / scale
        for f in range(owners):
            piece = step[:, f * owned : (f + 1) * owned]
            piece = jnp.concatenate([piece, jnp.zeros((slab, LANES - owned), jnp.float32)], axis=1)
            out_ref[b * owners + f] = piece + rider


def gradient_step(place, borrowed, got, square, tiles, owned):
    devices, slab, _ = got.shape
    return pl.pallas_call(
        functools.partial(gradient_kernel, tiles, owned),
        in_specs=[SCALARS] * 2 + [pl.BlockSpec(memory_space=pltpu.VMEM)] * 2,
        out_specs=pl.BlockSpec(memory_space=pltpu.VMEM),
        out_shape=jax.ShapeDtypeStruct((devices, slab, LANES), jnp.float32),
        compiler_params=params(16),
        cost_estimate=cost(1 << 22, 1 << 20),
        name="gradient_step",
    )(place, borrowed, got, square)


def update_kernel(divisor, models_ref, back_ref, updated_ref, misfit_ref):
    devices, slab, _ = back_ref.shape
    owned, members = models_ref.shape
    per_row = members // slab
    iota = lax.broadcasted_iota
    riders = back_ref[0]
    for d in range(1, devices):
        riders = riders + back_ref[d]
    down = (iota(jnp.int32, (slab, members), 1) // per_row == iota(jnp.int32, (slab, members), 0))
    tall = exact_dot(riders, down.astype(jnp.float32), (((0,), (0,)), ((), ())))
    mine = iota(jnp.int32, (LANES, members), 1) % per_row + owned == iota(jnp.int32, (LANES, members), 0)
    misfit = jnp.sum(jnp.where(mine, tall, 0.0), axis=0, keepdims=True) / divisor
    step = back_ref[...].reshape(members, LANES).T[:owned]
    updated_ref[...] = models_ref[...] - STEP_LENGTH * misfit * step
    misfit_ref[...] = misfit


def update(models, back, divisor):
    return pl.pallas_call(
        functools.partial(update_kernel, divisor),
        in_specs=[pl.BlockSpec(memory_space=pltpu.VMEM)] * 2,
        out_specs=[pl.BlockSpec(memory_space=pltpu.VMEM)] * 2,
        out_shape=[
            jax.ShapeDtypeStruct(models.shape, jnp.float32),
            jax.ShapeDtypeStruct((1, models.shape[1]), jnp.float32),
        ],
        compiler_params=params(16),
        cost_estimate=cost(1 << 20, 1 << 18),
        name="update",
    )(models, back)


def chunk_groups(groups):
    if groups < 16:
        return [1] * groups
    ends = [groups // 8, groups * 3 // 16, groups // 8, groups // 16]
    rest = groups - sum(ends)
    return [ends[0], rest - rest // 2, rest // 2] + ends[1:]


def body(sensitivity, models, observed, waveform, cell_index, gate_index):
    both = ("tile", "freq")
    tiles, owners, devices = lax.axis_size("tile"), lax.axis_size("freq"), lax.axis_size(both)
    _, own_freqs, parts, soundings, cells = sensitivity.shape
    freqs = own_freqs * owners
    spectra = own_freqs * parts
    owned, members = models.shape
    ncells = owned * devices
    gates = gate_index.shape[0]
    divisor = 2.0 * tiles * soundings * gates
    own = soundings // owners
    block_cells = owned * owners
    place = jnp.stack([lax.axis_index("tile"), lax.axis_index("freq")])

    block = sensitivity[0].reshape(spectra, soundings, cells)
    lanes = cells // members if owned % (GROUP * (cells // members)) == 0 else 1
    sizes = chunk_groups(own // GROUP)
    starts = [sum(sizes[:i]) for i in range(len(sizes))]
    distances = partner_order(owners)
    partners = [0] + distances
    received, done = [], []

    def send(i):
        after = received[i - 1][:1] if i else []
        if i > 2:
            after = after + done[i - 3 : i - 2]
        pieces = pack(
            place, block, models, after, distances, own, starts[i] * GROUP, sizes[i] * GROUP, 0 if i else lanes
        )
        received.append([swap(p, "freq", k) for p, k in zip(pieces, distances)])

    send(0)
    send(1)
    near = near_models(place, cell_index, models, received[0], lanes)
    blocks = [near] + [swap(near, "tile", k) for k in range(1, tiles)]
    borrowed = jnp.stack([b[block_cells, 0] for b in blocks]).astype(jnp.int32)
    models_t = tile_models(place, cell_index, blocks, owned, partners)

    order = place[1] ^ jnp.array(partners, jnp.int32)
    wide = wide_table(gate_table(order, own_freqs, freqs, waveform, gate_index).T)
    obs = observed[0].reshape(gates, own // GROUP, GROUP)
    obs = jnp.swapaxes(obs, 0, 1).reshape(own // GROUP, 1, gates * GROUP)

    terms = jnp.zeros((members, cells), jnp.float32)
    square = jnp.zeros((members, LANES), jnp.float32)
    for i, start in enumerate(starts):
        if i > 1:
            send(i)
        last = i == len(starts) - 1
        terms, square = chunk_step(
            place, block, received[i], start, models_t, wide, obs, cell_index, terms, square, block_cells, last
        )
        done.append(square)

    slab = members // devices
    sent = terms.reshape(devices, slab, cells)
    got = lax.all_to_all(sent, both, split_axis=0, concat_axis=0, tiled=True)
    if slab % GROUP == 0 and members // slab + owned <= LANES:
        step = gradient_step(place, borrowed, got, square, tiles, owned)
        back = lax.all_to_all(step, both, split_axis=0, concat_axis=0, tiled=True)
        updated, misfit = update(models, back, divisor)
        return (updated, misfit.reshape(members))

    got = jnp.sum(got.reshape(tiles, owners, slab, cells), axis=1)
    tile_ids = jnp.arange(tiles)
    lent = (jnp.take(borrowed, tile_ids ^ place[0])[None, :] == tile_ids[:, None]).astype(jnp.float32)
    gradient = got[:, :, :block_cells] + jnp.sum(
        lent[:, :, None, None] * got[None, :, :, block_cells:], axis=1
    )
    scale = jnp.sqrt(jnp.sum(gradient * gradient, axis=(0, 2)) / ncells + EPSILON)
    step = gradient / scale[None, :, None]
    step = step.reshape(tiles, slab, owners, owned).transpose(0, 2, 1, 3)
    step = step.reshape(devices, slab, owned)
    rider = jnp.broadcast_to(square[:, 0].reshape(1, slab, devices), (devices, slab, devices))
    back = lax.all_to_all(
        jnp.concatenate([step, rider], axis=2), both, split_axis=0, concat_axis=0, tiled=True
    )
    misfit = jnp.sum(back[:, :, owned:], axis=0).reshape(members) / divisor
    back = back[:, :, :owned].reshape(members, owned)
    return (models - (STEP_LENGTH * misfit)[None, :] * back.T, misfit)


def solution(mesh):
    in_specs = (
        P("tile", "freq", None, None, None),
        P(("tile", "freq"), None),
        P("tile", None, "freq"),
        P(),
        P("tile", None),
        P(),
    )
    out_specs = (P(("tile", "freq"), None), P())
    return jax.shard_map(body, mesh=mesh, in_specs=in_specs, out_specs=out_specs, check_vma=False)
```

```python
import functools
import math

import jax
import jax.numpy as jnp
from jax import lax
from jax.experimental import pallas as pl
from jax.experimental.pallas import tpu as pltpu
from jax.sharding import PartitionSpec as P

HIGH = lax.Precision.HIGHEST
PHASE_RATE = 0.37
STEP_LENGTH = 0.5
EPSILON = 1e-06
GROUP = 8
LANES = 128

NN = (((1,), (0,)), ((), ()))
NT = (((1,), (1,)), ((), ()))


def swap(x, axis, k):
    return lax.ppermute(x, axis, [(i, i ^ k) for i in range(lax.axis_size(axis))])


def partner_order(size):
    assert size & (size - 1) == 0
    half = size // 2
    pairs = zip(range(size - 1, half, -1), range(half - 1, 0, -1))
    return [half] + [k for pair in pairs for k in pair]


def gate_table(owner_order, own_freqs, freqs, waveform, gate_index):
    samples = waveform.shape[0]
    freq_ids = (owner_order[:, None] * own_freqs + jnp.arange(own_freqs)[None, :]).reshape(freqs)
    freq_col = freq_ids.astype(jnp.float32)[:, None] + 0.5
    time_row = jnp.arange(samples, dtype=jnp.float32)[None, :] + 0.5
    phases = PHASE_RATE * freq_col * time_row
    kernel = jnp.stack([jnp.cos(phases), jnp.sin(phases)], axis=1) / math.sqrt(freqs)
    steps = jnp.arange(samples)
    lag = gate_index[:, None] - steps[None, :]
    picked = jnp.sum(
        jnp.where(lag[:, :, None] == steps[None, None, :], waveform[None, None, :], 0.0), axis=-1
    )
    return jnp.einsum("gk,fpk->gfp", picked, kernel, precision=HIGH).reshape(gate_index.shape[0], freqs * 2)


def split(x):
    high = x.astype(jnp.bfloat16)
    return high, (x - high.astype(jnp.float32)).astype(jnp.bfloat16)


def three_pass(a, b, dims):
    dot = functools.partial(lax.dot_general, dimension_numbers=dims, preferred_element_type=jnp.float32)
    return dot(a[0], b[0]) + (dot(a[0], b[1]) + dot(a[1], b[0]))


def params(mebibytes):
    return pltpu.CompilerParams(vmem_limit_bytes=mebibytes * 1024 * 1024)


def cost(flops, bytes_accessed):
    return pl.CostEstimate(flops=flops, bytes_accessed=bytes_accessed, transcendentals=0)


def whole(a):
    return pl.BlockSpec(a.shape, lambda *_: (0,) * a.ndim)


HBM = pl.BlockSpec(memory_space=pltpu.HBM)
SCALARS = pl.BlockSpec(memory_space=pltpu.SMEM)


def pack_kernel(distances, own, first, rows, lanes, place_ref, block_ref, models_ref, *refs):
    outs, (held, in_sems, out_sems) = refs[-len(distances) - 3 : -3], refs[-3:]
    spectra = block_ref.shape[0]
    owned, members = models_ref.shape
    arrivals, departures = [], []
    for j, k in enumerate(distances):
        row = pl.multiple_of((place_ref[1] ^ k) * own + first, GROUP)
        source, target = block_ref.at[:, pl.ds(row, rows)], held.at[j, pl.ds(0, spectra)]
        arrivals.append(pltpu.make_async_copy(source, target, in_sems.at[j]))
        departures.append(pltpu.make_async_copy(held.at[j], outs[j], out_sems.at[j]))
        arrivals[j].start()
    for j in range(len(distances)):
        for lane in range(lanes):
            part = owned // lanes
            held[j, spectra, pl.ds(0, part), pl.ds(lane * members, members)] = models_ref[pl.ds(lane * part, part), :]
    for arrival, departure in zip(arrivals, departures):
        arrival.wait()
        departure.start()
    for departure in departures:
        departure.wait()


def pack(place, block, models, after, distances, own, first, rows, lanes):
    spectra, _, cells = block.shape
    count = len(distances)
    shape = (spectra + (lanes > 0), rows, cells)
    return pl.pallas_call(
        functools.partial(pack_kernel, distances, own, first, rows, lanes),
        in_specs=[SCALARS, HBM, pl.BlockSpec(memory_space=pltpu.VMEM)] + [HBM] * len(after),
        out_specs=[HBM] * count,
        out_shape=[jax.ShapeDtypeStruct(shape, jnp.float32)] * count,
        scratch_shapes=[
            pltpu.VMEM((count, *shape), jnp.float32),
            pltpu.SemaphoreType.DMA((count,)),
            pltpu.SemaphoreType.DMA((count,)),
        ],
        compiler_params=params(48),
        cost_estimate=cost(0, 8 * count * spectra * rows * cells),
        name="pack",
    )(place, block, models, *after)


def near_kernel(lanes, place_ref, cells_ref, models_ref, *refs):
    riders, out_ref = refs[:-1], refs[-1]
    owned, members = models_ref.shape
    part = owned // lanes
    out_ref[pl.ds(0, owned), :] = models_ref[...]
    for j, r in enumerate(riders):
        for lane in range(lanes):
            out_ref[pl.ds((j + 1) * owned + lane * part, part), :] = r[
                0, pl.ds(0, part), pl.ds(lane * members, members)
            ]
    block_cells = owned * (len(riders) + 1)
    home = cells_ref[...] // block_cells
    other = jnp.where(home == place_ref[0], -1, home).astype(jnp.float32)
    other = jnp.max(other, axis=1, keepdims=True)
    out_ref[pl.ds(block_cells, GROUP), :] = jnp.broadcast_to(other, (GROUP, members))


def near_models(place, cell_index, models, first, lanes):
    owned, members = models.shape
    slabs, rows, cells = first[0].shape
    rider = pl.BlockSpec((1, rows, cells), lambda i: (slabs - 1, 0, 0))
    return pl.pallas_call(
        functools.partial(near_kernel, lanes),
        grid=(1,),
        in_specs=[SCALARS, whole(cell_index), whole(models)] + [rider] * len(first),
        out_specs=pl.BlockSpec((owned * (len(first) + 1) + GROUP, members), lambda i: (0, 0)),
        out_shape=jax.ShapeDtypeStruct((owned * (len(first) + 1) + GROUP, members), jnp.float32),
        compiler_params=params(16),
        cost_estimate=cost(0, 1 << 20),
        name="near_models",
    )(place, cell_index, models, *first)


def tile_models_kernel(owned, partners, place_ref, cells_ref, *refs):
    tile_refs, (high_ref, low_ref) = refs[:-2], refs[-2:]
    block_cells = owned * len(partners)
    cells = cells_ref[...]
    distance = (cells // owned % len(partners)) ^ place_ref[1]
    slot = jnp.zeros_like(cells)
    for n, k in enumerate(partners):
        slot = jnp.where(distance == k, n, slot)
    spot = slot * owned + cells % owned
    away = (cells // block_cells) ^ place_ref[0]
    high, low = None, None
    for k, ref in enumerate(tile_refs):
        row = lax.broadcasted_iota(jnp.int32, (block_cells, cells.shape[1]), 0)
        pick = jnp.where((row == spot) & (away == k), 1.0, 0.0).astype(jnp.bfloat16)
        h, l = split(ref[pl.ds(0, block_cells), :].T)
        h = lax.dot_general(h, pick, NN, preferred_element_type=jnp.float32)
        l = lax.dot_general(l, pick, NN, preferred_element_type=jnp.float32)
        high, low = (h, l) if k == 0 else (high + h, low + l)
    high_ref[...] = high.astype(jnp.bfloat16)
    low_ref[...] = low.astype(jnp.bfloat16)


def tile_models(place, cell_index, tiles, owned, partners):
    shape = jax.ShapeDtypeStruct((tiles[0].shape[1], cell_index.shape[1]), jnp.bfloat16)
    return pl.pallas_call(
        functools.partial(tile_models_kernel, owned, partners),
        in_specs=[SCALARS] + [pl.BlockSpec(memory_space=pltpu.VMEM)] * (1 + len(tiles)),
        out_specs=[pl.BlockSpec(memory_space=pltpu.VMEM)] * 2,
        out_shape=[shape] * 2,
        compiler_params=params(16),
        cost_estimate=cost(1 << 30, 2 << 20),
        name="tile_models",
    )(place, cell_index, *tiles)


def wide_kernel(table_ref, high_ref, low_ref):
    fp, gates = table_ref.shape
    rows, columns = high_ref.shape
    iota = lax.broadcasted_iota
    down = (iota(jnp.int32, (rows, fp), 0) // GROUP == iota(jnp.int32, (rows, fp), 1)).astype(jnp.float32)
    across = iota(jnp.int32, (gates, columns), 1) // GROUP == iota(jnp.int32, (gates, columns), 0)
    across = across.astype(jnp.float32).astype(jnp.bfloat16)
    down = down.astype(jnp.bfloat16)
    same = iota(jnp.int32, (rows, columns), 0) % GROUP == iota(jnp.int32, (rows, columns), 1) % GROUP
    for part, ref in zip(split(table_ref[...]), (high_ref, low_ref)):
        tall = lax.dot_general(down, part, NN, preferred_element_type=jnp.float32).astype(jnp.bfloat16)
        full = lax.dot_general(tall, across, NN, preferred_element_type=jnp.float32)
        ref[...] = jnp.where(same, full, 0.0).astype(jnp.bfloat16)


def wide_table(table):
    shape = jax.ShapeDtypeStruct((table.shape[0] * GROUP, table.shape[1] * GROUP), jnp.bfloat16)
    return pl.pallas_call(
        wide_kernel,
        in_specs=[pl.BlockSpec(memory_space=pltpu.VMEM)],
        out_specs=[pl.BlockSpec(memory_space=pltpu.VMEM)] * 2,
        out_shape=[shape] * 2,
        compiler_params=params(16),
        cost_estimate=cost(1 << 28, 1 << 20),
        name="wide_table",
    )(table)


def chunk_kernel(pieces, block_cells, last, place_ref, *refs):
    sens_refs = refs[:pieces]
    model_h, model_l, gate_h, gate_l, obs_ref, cells_ref, terms_in, square_in, terms_ref, square_ref = refs[pieces:]

    @pl.when(pl.program_id(0) == 0)
    def _():
        terms_ref[...] = terms_in[...]
        square_ref[...] = square_in[...]

    sens = [split(r[...].reshape(r.shape[0] * r.shape[1], r.shape[2])) for r in sens_refs]
    sens = tuple(jnp.concatenate([s[i] for s in sens], axis=0) for i in range(2))
    gates = (gate_h[...], gate_l[...])
    predicted = three_pass((model_h[...], model_l[...]), sens, NT)
    misfit_rows = three_pass(split(predicted), gates, NN) - obs_ref[0]
    square_ref[...] += jnp.sum(misfit_rows * misfit_rows, axis=1, keepdims=True)
    back = three_pass(split(misfit_rows), gates, NT)
    terms = terms_ref[...] + three_pass(split(back), sens, NN)
    terms_ref[...] = terms

    if last:

        @pl.when(pl.program_id(0) == pl.num_programs(0) - 1)
        def _():
            cells = cells_ref[...]
            spot = cells % block_cells + jnp.where(cells // block_cells == place_ref[0], 0, block_cells)
            size = cells.shape[1]
            row = lax.broadcasted_iota(jnp.int32, (size, size), 0)
            pick = jnp.where(row == spot, 1.0, 0.0).astype(jnp.bfloat16)
            high = terms.astype(jnp.bfloat16)
            middle, low = split(terms - high.astype(jnp.float32))
            dot = functools.partial(lax.dot_general, dimension_numbers=NT, preferred_element_type=jnp.float32)
            terms_ref[...] = dot(high, pick) + (dot(middle, pick) + dot(low, pick))


def chunk_step(place, block, sens, first, models_t, gates, obs, cell_index, terms, square, block_cells, last):
    spectra, soundings, cells = block.shape
    rows = sens[0].shape[1]
    pieces = len(sens) + 1
    members = terms.shape[0]
    own_groups = soundings // (pieces * GROUP)
    return pl.pallas_call(
        functools.partial(chunk_kernel, pieces, block_cells, last),
        grid_spec=pltpu.PrefetchScalarGridSpec(
            num_scalar_prefetch=1,
            grid=(rows // GROUP,),
            in_specs=[
                pl.BlockSpec((spectra, GROUP, cells), lambda i, place: (0, place[1] * own_groups + first + i, 0))
            ]
            + [pl.BlockSpec((spectra, GROUP, cells), lambda i, place: (0, i, 0))] * len(sens)
            + [whole(a) for a in (*models_t, *gates)]
            + [pl.BlockSpec((1, 1, obs.shape[2]), lambda i, place: (first + i, 0, 0)), whole(cell_index)]
            + [whole(terms), whole(square)],
            out_specs=[whole(terms), whole(square)],
        ),
        out_shape=[
            jax.ShapeDtypeStruct(terms.shape, jnp.float32),
            jax.ShapeDtypeStruct(square.shape, jnp.float32),
        ],
        input_output_aliases={pieces + 7: 0, pieces + 8: 1},
        compiler_params=params(40),
        cost_estimate=cost(
            12 * pieces * spectra * rows * cells * members * 2, 4 * pieces * spectra * rows * cells
        ),
        name="chunk_step",
    )(place, block, *sens, *models_t, *gates, obs, cell_index, terms, square)


def exact_dot(a, b, dims):
    return lax.dot_general(a, b, dims, precision=HIGH, preferred_element_type=jnp.float32)


def gradient_kernel(tiles, owned, place_ref, borrowed_ref, got_ref, square_ref, out_ref):
    devices, slab, cells = got_ref.shape
    owners = devices // tiles
    block_cells = owned * owners
    members = square_ref.shape[0]
    sums = []
    for t in range(tiles):
        total = got_ref[t * owners]
        for f in range(1, owners):
            total = total + got_ref[t * owners + f]
        sums.append(total)
    gradient = []
    for b in range(tiles):
        block = sums[b][:, :block_cells]
        for t in range(tiles):
            block = block + jnp.where(borrowed_ref[place_ref[0] ^ t] == b, sums[t][:, block_cells:], 0.0)
        gradient.append(block)
    square = sum(jnp.sum(g * g, axis=1, keepdims=True) for g in gradient)
    scale = jnp.sqrt(square / (tiles * block_cells) + EPSILON)
    iota = lax.broadcasted_iota
    per_row = members // slab
    down = (iota(jnp.int32, (slab, members), 1) // per_row == iota(jnp.int32, (slab, members), 0))
    lane = iota(jnp.int32, (members, LANES), 1)
    spread = jnp.where(iota(jnp.int32, (members, LANES), 0) % per_row + owned == lane, square_ref[...], 0.0)
    rider = exact_dot(down.astype(jnp.float32), spread, NN)
    for b in range(tiles):
        step = gradient[b] / scale
        for f in range(owners):
            piece = step[:, f * owned : (f + 1) * owned]
            piece = jnp.concatenate([piece, jnp.zeros((slab, LANES - owned), jnp.float32)], axis=1)
            out_ref[b * owners + f] = piece + rider


def gradient_step(place, borrowed, got, square, tiles, owned):
    devices, slab, _ = got.shape
    return pl.pallas_call(
        functools.partial(gradient_kernel, tiles, owned),
        in_specs=[SCALARS] * 2 + [pl.BlockSpec(memory_space=pltpu.VMEM)] * 2,
        out_specs=pl.BlockSpec(memory_space=pltpu.VMEM),
        out_shape=jax.ShapeDtypeStruct((devices, slab, LANES), jnp.float32),
        compiler_params=params(16),
        cost_estimate=cost(1 << 22, 1 << 20),
        name="gradient_step",
    )(place, borrowed, got, square)


def update_kernel(divisor, models_ref, back_ref, updated_ref, misfit_ref):
    devices, slab, _ = back_ref.shape
    owned, members = models_ref.shape
    per_row = members // slab
    iota = lax.broadcasted_iota
    riders = back_ref[0]
    for d in range(1, devices):
        riders = riders + back_ref[d]
    down = (iota(jnp.int32, (slab, members), 1) // per_row == iota(jnp.int32, (slab, members), 0))
    tall = exact_dot(riders, down.astype(jnp.float32), (((0,), (0,)), ((), ())))
    mine = iota(jnp.int32, (LANES, members), 1) % per_row + owned == iota(jnp.int32, (LANES, members), 0)
    misfit = jnp.sum(jnp.where(mine, tall, 0.0), axis=0, keepdims=True) / divisor
    step = back_ref[...].reshape(members, LANES).T[:owned]
    updated_ref[...] = models_ref[...] - STEP_LENGTH * misfit * step
    misfit_ref[...] = misfit


def update(models, back, divisor):
    return pl.pallas_call(
        functools.partial(update_kernel, divisor),
        in_specs=[pl.BlockSpec(memory_space=pltpu.VMEM)] * 2,
        out_specs=[pl.BlockSpec(memory_space=pltpu.VMEM)] * 2,
        out_shape=[
            jax.ShapeDtypeStruct(models.shape, jnp.float32),
            jax.ShapeDtypeStruct((1, models.shape[1]), jnp.float32),
        ],
        compiler_params=params(16),
        cost_estimate=cost(1 << 20, 1 << 18),
        name="update",
    )(models, back)


def chunk_groups(groups):
    if groups < 16:
        return [1] * groups
    ends = [groups // 8, groups * 3 // 16, groups // 16]
    rest = groups - sum(ends)
    return [ends[0], rest - rest // 2, rest // 2] + ends[1:]


def body(sensitivity, models, observed, waveform, cell_index, gate_index):
    both = ("tile", "freq")
    tiles, owners, devices = lax.axis_size("tile"), lax.axis_size("freq"), lax.axis_size(both)
    _, own_freqs, parts, soundings, cells = sensitivity.shape
    freqs = own_freqs * owners
    spectra = own_freqs * parts
    owned, members = models.shape
    ncells = owned * devices
    gates = gate_index.shape[0]
    divisor = 2.0 * tiles * soundings * gates
    own = soundings // owners
    block_cells = owned * owners
    place = jnp.stack([lax.axis_index("tile"), lax.axis_index("freq")])

    block = sensitivity[0].reshape(spectra, soundings, cells)
    lanes = cells // members if owned % (GROUP * (cells // members)) == 0 else 1
    sizes = chunk_groups(own // GROUP)
    starts = [sum(sizes[:i]) for i in range(len(sizes))]
    distances = partner_order(owners)
    partners = [0] + distances
    received, done = [], []

    def send(i):
        after = received[i - 1][:1] if i else []
        if i > 2:
            after = after + done[i - 3 : i - 2]
        pieces = pack(
            place, block, models, after, distances, own, starts[i] * GROUP, sizes[i] * GROUP, 0 if i else lanes
        )
        received.append([swap(p, "freq", k) for p, k in zip(pieces, distances)])

    send(0)
    send(1)
    near = near_models(place, cell_index, models, received[0], lanes)
    blocks = [near] + [swap(near, "tile", k) for k in range(1, tiles)]
    borrowed = jnp.stack([b[block_cells, 0] for b in blocks]).astype(jnp.int32)
    models_t = tile_models(place, cell_index, blocks, owned, partners)

    order = place[1] ^ jnp.array(partners, jnp.int32)
    wide = wide_table(gate_table(order, own_freqs, freqs, waveform, gate_index).T)
    obs = observed[0].reshape(gates, own // GROUP, GROUP)
    obs = jnp.swapaxes(obs, 0, 1).reshape(own // GROUP, 1, gates * GROUP)

    terms = jnp.zeros((members, cells), jnp.float32)
    square = jnp.zeros((members, LANES), jnp.float32)
    for i, start in enumerate(starts):
        if i > 1:
            send(i)
        last = i == len(starts) - 1
        terms, square = chunk_step(
            place, block, received[i], start, models_t, wide, obs, cell_index, terms, square, block_cells, last
        )
        done.append(square)

    slab = members // devices
    sent = terms.reshape(devices, slab, cells)
    got = lax.all_to_all(sent, both, split_axis=0, concat_axis=0, tiled=True)
    if slab % GROUP == 0 and members // slab + owned <= LANES:
        step = gradient_step(place, borrowed, got, square, tiles, owned)
        back = lax.all_to_all(step, both, split_axis=0, concat_axis=0, tiled=True)
        updated, misfit = update(models, back, divisor)
        return (updated, misfit.reshape(members))

    got = jnp.sum(got.reshape(tiles, owners, slab, cells), axis=1)
    tile_ids = jnp.arange(tiles)
    lent = (jnp.take(borrowed, tile_ids ^ place[0])[None, :] == tile_ids[:, None]).astype(jnp.float32)
    gradient = got[:, :, :block_cells] + jnp.sum(
        lent[:, :, None, None] * got[None, :, :, block_cells:], axis=1
    )
    scale = jnp.sqrt(jnp.sum(gradient * gradient, axis=(0, 2)) / ncells + EPSILON)
    step = gradient / scale[None, :, None]
    step = step.reshape(tiles, slab, owners, owned).transpose(0, 2, 1, 3)
    step = step.reshape(devices, slab, owned)
    rider = jnp.broadcast_to(square[:, 0].reshape(1, slab, devices), (devices, slab, devices))
    back = lax.all_to_all(
        jnp.concatenate([step, rider], axis=2), both, split_axis=0, concat_axis=0, tiled=True
    )
    misfit = jnp.sum(back[:, :, owned:], axis=0).reshape(members) / divisor
    back = back[:, :, :owned].reshape(members, owned)
    return (models - (STEP_LENGTH * misfit)[None, :] * back.T, misfit)


def solution(mesh):
    in_specs = (
        P("tile", "freq", None, None, None),
        P(("tile", "freq"), None),
        P("tile", None, "freq"),
        P(),
        P("tile", None),
        P(),
    )
    out_specs = (P(("tile", "freq"), None), P())
    return jax.shard_map(body, mesh=mesh, in_specs=in_specs, out_specs=out_specs, check_vma=False)
```

```python
import functools
import math

import jax
import jax.numpy as jnp
from jax import lax
from jax.experimental import pallas as pl
from jax.experimental.pallas import tpu as pltpu
from jax.sharding import PartitionSpec as P

HIGH = lax.Precision.HIGHEST
PHASE_RATE = 0.37
STEP_LENGTH = 0.5
EPSILON = 1e-06
GROUP = 8
LANES = 128

NN = (((1,), (0,)), ((), ()))
NT = (((1,), (1,)), ((), ()))


def swap(x, axis, k):
    return lax.ppermute(x, axis, [(i, i ^ k) for i in range(lax.axis_size(axis))])


def partner_order(size):
    assert size & (size - 1) == 0
    half = size // 2
    pairs = zip(range(size - 1, half, -1), range(half - 1, 0, -1))
    return [half] + [k for pair in pairs for k in pair]


def gate_table(owner_order, own_freqs, freqs, waveform, gate_index):
    samples = waveform.shape[0]
    freq_ids = (owner_order[:, None] * own_freqs + jnp.arange(own_freqs)[None, :]).reshape(freqs)
    freq_col = freq_ids.astype(jnp.float32)[:, None] + 0.5
    time_row = jnp.arange(samples, dtype=jnp.float32)[None, :] + 0.5
    phases = PHASE_RATE * freq_col * time_row
    kernel = jnp.stack([jnp.cos(phases), jnp.sin(phases)], axis=1) / math.sqrt(freqs)
    steps = jnp.arange(samples)
    lag = gate_index[:, None] - steps[None, :]
    picked = jnp.sum(
        jnp.where(lag[:, :, None] == steps[None, None, :], waveform[None, None, :], 0.0), axis=-1
    )
    return jnp.einsum("gk,fpk->gfp", picked, kernel, precision=HIGH).reshape(gate_index.shape[0], freqs * 2)


def split(x):
    high = x.astype(jnp.bfloat16)
    return high, (x - high.astype(jnp.float32)).astype(jnp.bfloat16)


def three_pass(a, b, dims):
    dot = functools.partial(lax.dot_general, dimension_numbers=dims, preferred_element_type=jnp.float32)
    return dot(a[0], b[0]) + (dot(a[0], b[1]) + dot(a[1], b[0]))


def params(mebibytes):
    return pltpu.CompilerParams(vmem_limit_bytes=mebibytes * 1024 * 1024)


def cost(flops, bytes_accessed):
    return pl.CostEstimate(flops=flops, bytes_accessed=bytes_accessed, transcendentals=0)


def whole(a):
    return pl.BlockSpec(a.shape, lambda *_: (0,) * a.ndim)


HBM = pl.BlockSpec(memory_space=pltpu.HBM)
SCALARS = pl.BlockSpec(memory_space=pltpu.SMEM)


def pack_kernel(distances, own, first, rows, lanes, place_ref, block_ref, models_ref, *refs):
    outs, (held, in_sems, out_sems) = refs[-len(distances) - 3 : -3], refs[-3:]
    spectra = block_ref.shape[0]
    owned, members = models_ref.shape
    arrivals, departures = [], []
    for j, k in enumerate(distances):
        row = pl.multiple_of((place_ref[1] ^ k) * own + first, GROUP)
        source, target = block_ref.at[:, pl.ds(row, rows)], held.at[j, pl.ds(0, spectra)]
        arrivals.append(pltpu.make_async_copy(source, target, in_sems.at[j]))
        departures.append(pltpu.make_async_copy(held.at[j], outs[j], out_sems.at[j]))
        arrivals[j].start()
    for j in range(len(distances)):
        for lane in range(lanes):
            part = owned // lanes
            held[j, spectra, pl.ds(0, part), pl.ds(lane * members, members)] = models_ref[pl.ds(lane * part, part), :]
    for arrival, departure in zip(arrivals, departures):
        arrival.wait()
        departure.start()
    for departure in departures:
        departure.wait()


def pack(place, block, models, after, distances, own, first, rows, lanes):
    spectra, _, cells = block.shape
    count = len(distances)
    shape = (spectra + (lanes > 0), rows, cells)
    return pl.pallas_call(
        functools.partial(pack_kernel, distances, own, first, rows, lanes),
        in_specs=[SCALARS, HBM, pl.BlockSpec(memory_space=pltpu.VMEM)] + [HBM] * len(after),
        out_specs=[HBM] * count,
        out_shape=[jax.ShapeDtypeStruct(shape, jnp.float32)] * count,
        scratch_shapes=[
            pltpu.VMEM((count, *shape), jnp.float32),
            pltpu.SemaphoreType.DMA((count,)),
            pltpu.SemaphoreType.DMA((count,)),
        ],
        compiler_params=params(48),
        cost_estimate=cost(0, 8 * count * spectra * rows * cells),
        name="pack",
    )(place, block, models, *after)


def near_kernel(lanes, place_ref, cells_ref, models_ref, *refs):
    riders, out_ref = refs[:-1], refs[-1]
    owned, members = models_ref.shape
    part = owned // lanes
    out_ref[pl.ds(0, owned), :] = models_ref[...]
    for j, r in enumerate(riders):
        for lane in range(lanes):
            out_ref[pl.ds((j + 1) * owned + lane * part, part), :] = r[
                0, pl.ds(0, part), pl.ds(lane * members, members)
            ]
    block_cells = owned * (len(riders) + 1)
    home = cells_ref[...] // block_cells
    other = jnp.where(home == place_ref[0], -1, home).astype(jnp.float32)
    other = jnp.max(other, axis=1, keepdims=True)
    out_ref[pl.ds(block_cells, GROUP), :] = jnp.broadcast_to(other, (GROUP, members))


def near_models(place, cell_index, models, first, lanes):
    owned, members = models.shape
    slabs, rows, cells = first[0].shape
    rider = pl.BlockSpec((1, rows, cells), lambda i: (slabs - 1, 0, 0))
    return pl.pallas_call(
        functools.partial(near_kernel, lanes),
        grid=(1,),
        in_specs=[SCALARS, whole(cell_index), whole(models)] + [rider] * len(first),
        out_specs=pl.BlockSpec((owned * (len(first) + 1) + GROUP, members), lambda i: (0, 0)),
        out_shape=jax.ShapeDtypeStruct((owned * (len(first) + 1) + GROUP, members), jnp.float32),
        compiler_params=params(16),
        cost_estimate=cost(0, 1 << 20),
        name="near_models",
    )(place, cell_index, models, *first)


def tile_models_kernel(owned, partners, place_ref, cells_ref, *refs):
    tile_refs, (high_ref, low_ref) = refs[:-2], refs[-2:]
    block_cells = owned * len(partners)
    cells = cells_ref[...]
    distance = (cells // owned % len(partners)) ^ place_ref[1]
    slot = jnp.zeros_like(cells)
    for n, k in enumerate(partners):
        slot = jnp.where(distance == k, n, slot)
    spot = slot * owned + cells % owned
    away = (cells // block_cells) ^ place_ref[0]
    high, low = None, None
    for k, ref in enumerate(tile_refs):
        row = lax.broadcasted_iota(jnp.int32, (block_cells, cells.shape[1]), 0)
        pick = jnp.where((row == spot) & (away == k), 1.0, 0.0).astype(jnp.bfloat16)
        h, l = split(ref[pl.ds(0, block_cells), :].T)
        h = lax.dot_general(h, pick, NN, preferred_element_type=jnp.float32)
        l = lax.dot_general(l, pick, NN, preferred_element_type=jnp.float32)
        high, low = (h, l) if k == 0 else (high + h, low + l)
    high_ref[...] = high.astype(jnp.bfloat16)
    low_ref[...] = low.astype(jnp.bfloat16)


def tile_models(place, cell_index, tiles, owned, partners):
    shape = jax.ShapeDtypeStruct((tiles[0].shape[1], cell_index.shape[1]), jnp.bfloat16)
    return pl.pallas_call(
        functools.partial(tile_models_kernel, owned, partners),
        in_specs=[SCALARS] + [pl.BlockSpec(memory_space=pltpu.VMEM)] * (1 + len(tiles)),
        out_specs=[pl.BlockSpec(memory_space=pltpu.VMEM)] * 2,
        out_shape=[shape] * 2,
        compiler_params=params(16),
        cost_estimate=cost(1 << 30, 2 << 20),
        name="tile_models",
    )(place, cell_index, *tiles)


def wide_kernel(table_ref, high_ref, low_ref):
    fp, gates = table_ref.shape
    rows, columns = high_ref.shape
    iota = lax.broadcasted_iota
    down = (iota(jnp.int32, (rows, fp), 0) // GROUP == iota(jnp.int32, (rows, fp), 1)).astype(jnp.float32)
    across = iota(jnp.int32, (gates, columns), 1) // GROUP == iota(jnp.int32, (gates, columns), 0)
    across = across.astype(jnp.float32).astype(jnp.bfloat16)
    down = down.astype(jnp.bfloat16)
    same = iota(jnp.int32, (rows, columns), 0) % GROUP == iota(jnp.int32, (rows, columns), 1) % GROUP
    for part, ref in zip(split(table_ref[...]), (high_ref, low_ref)):
        tall = lax.dot_general(down, part, NN, preferred_element_type=jnp.float32).astype(jnp.bfloat16)
        full = lax.dot_general(tall, across, NN, preferred_element_type=jnp.float32)
        ref[...] = jnp.where(same, full, 0.0).astype(jnp.bfloat16)


def wide_table(table):
    shape = jax.ShapeDtypeStruct((table.shape[0] * GROUP, table.shape[1] * GROUP), jnp.bfloat16)
    return pl.pallas_call(
        wide_kernel,
        in_specs=[pl.BlockSpec(memory_space=pltpu.VMEM)],
        out_specs=[pl.BlockSpec(memory_space=pltpu.VMEM)] * 2,
        out_shape=[shape] * 2,
        compiler_params=params(16),
        cost_estimate=cost(1 << 28, 1 << 20),
        name="wide_table",
    )(table)


def chunk_kernel(pieces, block_cells, last, place_ref, *refs):
    sens_refs = refs[:pieces]
    model_h, model_l, gate_h, gate_l, obs_ref, cells_ref, terms_in, square_in, terms_ref, square_ref = refs[pieces:]

    @pl.when(pl.program_id(0) == 0)
    def _():
        terms_ref[...] = terms_in[...]
        square_ref[...] = square_in[...]

    sens = [split(r[...].reshape(r.shape[0] * r.shape[1], r.shape[2])) for r in sens_refs]
    sens = tuple(jnp.concatenate([s[i] for s in sens], axis=0) for i in range(2))
    gates = (gate_h[...], gate_l[...])
    predicted = three_pass((model_h[...], model_l[...]), sens, NT)
    misfit_rows = three_pass(split(predicted), gates, NN) - obs_ref[0]
    square_ref[...] += jnp.sum(misfit_rows * misfit_rows, axis=1, keepdims=True)
    back = three_pass(split(misfit_rows), gates, NT)
    terms = terms_ref[...] + three_pass(split(back), sens, NN)
    terms_ref[...] = terms

    if last:

        @pl.when(pl.program_id(0) == pl.num_programs(0) - 1)
        def _():
            cells = cells_ref[...]
            spot = cells % block_cells + jnp.where(cells // block_cells == place_ref[0], 0, block_cells)
            size = cells.shape[1]
            row = lax.broadcasted_iota(jnp.int32, (size, size), 0)
            pick = jnp.where(row == spot, 1.0, 0.0).astype(jnp.bfloat16)
            high = terms.astype(jnp.bfloat16)
            middle, low = split(terms - high.astype(jnp.float32))
            dot = functools.partial(lax.dot_general, dimension_numbers=NT, preferred_element_type=jnp.float32)
            terms_ref[...] = dot(high, pick) + (dot(middle, pick) + dot(low, pick))


def chunk_step(place, block, sens, first, skip, count, models_t, gates, obs, cell_index, terms, square, block_cells, last):
    spectra, soundings, cells = block.shape
    rows = count * GROUP
    pieces = len(sens) + 1
    members = terms.shape[0]
    own_groups = soundings // (pieces * GROUP)
    return pl.pallas_call(
        functools.partial(chunk_kernel, pieces, block_cells, last),
        grid_spec=pltpu.PrefetchScalarGridSpec(
            num_scalar_prefetch=1,
            grid=(count,),
            in_specs=[
                pl.BlockSpec((spectra, GROUP, cells), lambda i, place: (0, place[1] * own_groups + first + skip + i, 0))
            ]
            + [pl.BlockSpec((spectra, GROUP, cells), lambda i, place: (0, skip + i, 0))] * len(sens)
            + [whole(a) for a in (*models_t, *gates)]
            + [pl.BlockSpec((1, 1, obs.shape[2]), lambda i, place: (first + skip + i, 0, 0)), whole(cell_index)]
            + [whole(terms), whole(square)],
            out_specs=[whole(terms), whole(square)],
        ),
        out_shape=[
            jax.ShapeDtypeStruct(terms.shape, jnp.float32),
            jax.ShapeDtypeStruct(square.shape, jnp.float32),
        ],
        input_output_aliases={pieces + 7: 0, pieces + 8: 1},
        compiler_params=params(40),
        cost_estimate=cost(
            12 * pieces * spectra * rows * cells * members * 2, 4 * pieces * spectra * rows * cells
        ),
        name="chunk_step",
    )(place, block, *sens, *models_t, *gates, obs, cell_index, terms, square)


def exact_dot(a, b, dims):
    return lax.dot_general(a, b, dims, precision=HIGH, preferred_element_type=jnp.float32)


def gradient_kernel(tiles, owned, place_ref, borrowed_ref, got_ref, square_ref, out_ref):
    devices, slab, cells = got_ref.shape
    owners = devices // tiles
    block_cells = owned * owners
    members = square_ref.shape[0]
    sums = []
    for t in range(tiles):
        total = got_ref[t * owners]
        for f in range(1, owners):
            total = total + got_ref[t * owners + f]
        sums.append(total)
    gradient = []
    for b in range(tiles):
        block = sums[b][:, :block_cells]
        for t in range(tiles):
            block = block + jnp.where(borrowed_ref[place_ref[0] ^ t] == b, sums[t][:, block_cells:], 0.0)
        gradient.append(block)
    square = sum(jnp.sum(g * g, axis=1, keepdims=True) for g in gradient)
    scale = jnp.sqrt(square / (tiles * block_cells) + EPSILON)
    iota = lax.broadcasted_iota
    per_row = members // slab
    down = (iota(jnp.int32, (slab, members), 1) // per_row == iota(jnp.int32, (slab, members), 0))
    lane = iota(jnp.int32, (members, LANES), 1)
    spread = jnp.where(iota(jnp.int32, (members, LANES), 0) % per_row + owned == lane, square_ref[...], 0.0)
    rider = exact_dot(down.astype(jnp.float32), spread, NN)
    for b in range(tiles):
        step = gradient[b] / scale
        for f in range(owners):
            piece = step[:, f * owned : (f + 1) * owned]
            piece = jnp.concatenate([piece, jnp.zeros((slab, LANES - owned), jnp.float32)], axis=1)
            out_ref[b * owners + f] = piece + rider


def gradient_step(place, borrowed, got, square, tiles, owned):
    devices, slab, _ = got.shape
    return pl.pallas_call(
        functools.partial(gradient_kernel, tiles, owned),
        in_specs=[SCALARS] * 2 + [pl.BlockSpec(memory_space=pltpu.VMEM)] * 2,
        out_specs=pl.BlockSpec(memory_space=pltpu.VMEM),
        out_shape=jax.ShapeDtypeStruct((devices, slab, LANES), jnp.float32),
        compiler_params=params(16),
        cost_estimate=cost(1 << 22, 1 << 20),
        name="gradient_step",
    )(place, borrowed, got, square)


def update_kernel(divisor, models_ref, back_ref, updated_ref, misfit_ref):
    devices, slab, _ = back_ref.shape
    owned, members = models_ref.shape
    per_row = members // slab
    iota = lax.broadcasted_iota
    riders = back_ref[0]
    for d in range(1, devices):
        riders = riders + back_ref[d]
    down = (iota(jnp.int32, (slab, members), 1) // per_row == iota(jnp.int32, (slab, members), 0))
    tall = exact_dot(riders, down.astype(jnp.float32), (((0,), (0,)), ((), ())))
    mine = iota(jnp.int32, (LANES, members), 1) % per_row + owned == iota(jnp.int32, (LANES, members), 0)
    misfit = jnp.sum(jnp.where(mine, tall, 0.0), axis=0, keepdims=True) / divisor
    step = back_ref[...].reshape(members, LANES).T[:owned]
    updated_ref[...] = models_ref[...] - STEP_LENGTH * misfit * step
    misfit_ref[...] = misfit


def update(models, back, divisor):
    return pl.pallas_call(
        functools.partial(update_kernel, divisor),
        in_specs=[pl.BlockSpec(memory_space=pltpu.VMEM)] * 2,
        out_specs=[pl.BlockSpec(memory_space=pltpu.VMEM)] * 2,
        out_shape=[
            jax.ShapeDtypeStruct(models.shape, jnp.float32),
            jax.ShapeDtypeStruct((1, models.shape[1]), jnp.float32),
        ],
        compiler_params=params(16),
        cost_estimate=cost(1 << 20, 1 << 18),
        name="update",
    )(models, back)


def chunk_groups(groups):
    if groups < 16:
        return [1] * groups
    ends = [groups // 8, groups * 3 // 16, groups // 8, groups // 16]
    rest = groups - sum(ends)
    return [ends[0], rest - rest // 2, rest // 2] + ends[1:]


def body(sensitivity, models, observed, waveform, cell_index, gate_index):
    both = ("tile", "freq")
    tiles, owners, devices = lax.axis_size("tile"), lax.axis_size("freq"), lax.axis_size(both)
    _, own_freqs, parts, soundings, cells = sensitivity.shape
    freqs = own_freqs * owners
    spectra = own_freqs * parts
    owned, members = models.shape
    ncells = owned * devices
    gates = gate_index.shape[0]
    divisor = 2.0 * tiles * soundings * gates
    own = soundings // owners
    block_cells = owned * owners
    place = jnp.stack([lax.axis_index("tile"), lax.axis_index("freq")])

    block = sensitivity[0].reshape(spectra, soundings, cells)
    lanes = cells // members if owned % (GROUP * (cells // members)) == 0 else 1
    sizes = chunk_groups(own // GROUP)
    starts = [sum(sizes[:i]) for i in range(len(sizes))]
    distances = partner_order(owners)
    partners = [0] + distances
    received, done = [], []

    def send(i):
        after = received[i - 1][:1] if i else []
        if i > 2:
            after = after + done[i - 3 : i - 2]
        pieces = pack(
            place, block, models, after, distances, own, starts[i] * GROUP, sizes[i] * GROUP, 0 if i else lanes
        )
        received.append([swap(p, "freq", k) for p, k in zip(pieces, distances)])

    send(0)
    send(1)
    near = near_models(place, cell_index, models, received[0], lanes)
    blocks = [near] + [swap(near, "tile", k) for k in range(1, tiles)]
    borrowed = jnp.stack([b[block_cells, 0] for b in blocks]).astype(jnp.int32)
    models_t = tile_models(place, cell_index, blocks, owned, partners)

    order = place[1] ^ jnp.array(partners, jnp.int32)
    wide = wide_table(gate_table(order, own_freqs, freqs, waveform, gate_index).T)
    obs = observed[0].reshape(gates, own // GROUP, GROUP)
    obs = jnp.swapaxes(obs, 0, 1).reshape(own // GROUP, 1, gates * GROUP)

    terms = jnp.zeros((members, cells), jnp.float32)
    square = jnp.zeros((members, LANES), jnp.float32)
    for i, start in enumerate(starts):
        if i > 1:
            send(i)
        last = i == len(starts) - 1
        cuts = [0, sizes[i]] if sizes[i] < 3 else [0, sizes[i] // 2, sizes[i]]
        for skip, end in zip(cuts, cuts[1:]):
            terms, square = chunk_step(
                place, block, received[i], start, skip, end - skip, models_t, wide, obs, cell_index, terms, square,
                block_cells, last and end == sizes[i],
            )
        done.append(square)

    slab = members // devices
    sent = terms.reshape(devices, slab, cells)
    got = lax.all_to_all(sent, both, split_axis=0, concat_axis=0, tiled=True)
    if slab % GROUP == 0 and members // slab + owned <= LANES:
        step = gradient_step(place, borrowed, got, square, tiles, owned)
        back = lax.all_to_all(step, both, split_axis=0, concat_axis=0, tiled=True)
        updated, misfit = update(models, back, divisor)
        return (updated, misfit.reshape(members))

    got = jnp.sum(got.reshape(tiles, owners, slab, cells), axis=1)
    tile_ids = jnp.arange(tiles)
    lent = (jnp.take(borrowed, tile_ids ^ place[0])[None, :] == tile_ids[:, None]).astype(jnp.float32)
    gradient = got[:, :, :block_cells] + jnp.sum(
        lent[:, :, None, None] * got[None, :, :, block_cells:], axis=1
    )
    scale = jnp.sqrt(jnp.sum(gradient * gradient, axis=(0, 2)) / ncells + EPSILON)
    step = gradient / scale[None, :, None]
    step = step.reshape(tiles, slab, owners, owned).transpose(0, 2, 1, 3)
    step = step.reshape(devices, slab, owned)
    rider = jnp.broadcast_to(square[:, 0].reshape(1, slab, devices), (devices, slab, devices))
    back = lax.all_to_all(
        jnp.concatenate([step, rider], axis=2), both, split_axis=0, concat_axis=0, tiled=True
    )
    misfit = jnp.sum(back[:, :, owned:], axis=0).reshape(members) / divisor
    back = back[:, :, :owned].reshape(members, owned)
    return (models - (STEP_LENGTH * misfit)[None, :] * back.T, misfit)


def solution(mesh):
    in_specs = (
        P("tile", "freq", None, None, None),
        P(("tile", "freq"), None),
        P("tile", None, "freq"),
        P(),
        P("tile", None),
        P(),
    )
    out_specs = (P(("tile", "freq"), None), P())
    return jax.shard_map(body, mesh=mesh, in_specs=in_specs, out_specs=out_specs, check_vma=False)
```
